32 devices in a mesh: sy: 4 (over z), sx: 2 (over y), tp: 4 (over x, core).
Axes of the slice: x: 2, y: 2, z: 4, core: 2. Of those that a mesh axis runs over, the one named last changes fastest.
Arguments:
- tokens: bfloat16 [3200, 3072], P(('sy', 'sx')), may hold values from -8 to 8
- mod_shift: float32 [3072], replicated, may hold values from -3 to 3
- mod_scale: float32 [3072], replicated, may hold values from -0.5 to 0.5
- mod_gate: float32 [3072], replicated, may hold values from 0.5 to 1.5
- w_qkv: bfloat16 [3072, 3, 1536], P('sx', None, 'tp'), as said below
- w_mlp_in: bfloat16 [3072, 6144], P('sx', 'tp'), may hold values from -0.109375 to 0.109375
- q_gain: float32 [12, 128], P('tp'), may hold values from 0 to 7, as said below
- k_gain: float32 [12, 128], P('tp'), may hold values from 0 to 7, as said below
- w_attn_out: bfloat16 [1536, 3072], P('tp', 'sx'), may hold values from -0.0625 to 0.0625
- w_mlp_out: bfloat16 [6144, 3072], P('tp', 'sx'), may hold values from -0.0625 to 0.0625
Outputs:
- result: bfloat16 [3200, 3072], P(('sy', 'sx'), 'tp')
The draws below stay inside these ranges and needn't reach their ends.
Inputs may be any that keep to these rules, and one draw needn't show every extreme that they name: `w_qkv`: mean-zero entries of about 3072 to the power -0.5 in size. `q_gain`: positive. `k_gain`: positive.
All inputs are finite; a program needn't handle non-finite values.
Results may differ from the reference program's by a relative error of at most 0.0085.
Values may be sent and summed in bfloat16 or wider, within the bound.
No kernel may reach another device: no remote copies, remote signals or barrier semaphores. Data moves between devices by JAX's collectives and lax.ppermute only.
A program may use at most 128 MiB of HBM per device.

```python
import math
import jax
import jax.numpy as jnp
from jax import lax

D = 3072
HEADS = 12
HD = 128
MLP = 6144
TILE = 20
HW = 1536
TOKENS = 3200
N_SY = 4
N_SX = 2


def log_even(key, lower, upper):
    unit = jax.random.uniform(key, (HEADS, HD), jnp.float32)
    return jnp.exp(math.log(lower) + unit * (math.log(upper) - math.log(lower)))


def draw_tokens(key, part):
    gaussian = jax.random.normal(jax.random.fold_in(key, 1), (TOKENS, D), jnp.float32)
    return jnp.clip(gaussian, -6.0, 6.0).astype(jnp.bfloat16)


def draw_w_qkv(key, part):
    limit = 6.0 * D ** (-0.5)
    base = jax.random.normal(jax.random.fold_in(key, 21), (D, 3, HEADS * HD), jnp.float32) * D ** (-0.5)
    base = jnp.clip(base, -limit, limit)
    return base.astype(jnp.bfloat16)


def draw_q_gain(key, part):
    return log_even(jax.random.fold_in(key, 33), 0.25, 4.0)


def draw_k_gain(key, part):
    return log_even(jax.random.fold_in(key, 43), 0.5, 2.0)


def shard_levels(own_key, shape, pieces, low, top_value):
    gain, own = 1.0, jax.random.fold_in(own_key, 6)
    for position, parts in pieces:
        heights = jnp.exp(jax.random.uniform(jax.random.fold_in(own, position), (parts,), jnp.float32, low / len(pieces), top_value / len(pieces)))
        gain = gain * jnp.repeat(heights, shape[position] // parts).reshape([-1 if axis == position else 1 for axis in range(len(shape))])
    return gain


def normal_values(own_key, dims, spread, most, split=(), kind=jnp.bfloat16):
    values = spread * jax.random.normal(own_key, dims, jnp.float32)
    if split:
        values = values * shard_levels(own_key, dims, split, -0.22, 0.18)
    return jnp.clip(values, -most, most).astype(kind)


def setup_inputs(seed: int = 0) -> dict:
    keys = jax.random.split(jax.random.key(seed), 11)
    tokens = draw_tokens(jax.random.fold_in(keys[10], 71), 0)
    mod_shift = normal_values(keys[1], (D,), 0.5, 3.0, (), jnp.float32)
    mod_scale = jnp.clip(jax.random.uniform(keys[2], (D,), jnp.float32, -0.5, 0.5), -0.5, 0.5)
    mod_gate = jnp.clip(jax.random.uniform(keys[3], (D,), jnp.float32, 0.5, 1.5), 0.5, 1.5)
    w_qkv = draw_w_qkv(jax.random.fold_in(keys[10], 71), 0)
    w_mlp_in = normal_values(keys[5], (D, MLP), D ** -0.5, 0.109375, ((0, 2), (1, 4)))
    q_gain = draw_q_gain(jax.random.fold_in(keys[10], 71), 0)
    k_gain = draw_k_gain(jax.random.fold_in(keys[10], 71), 0)
    w_attn_out = normal_values(keys[8], (HW, D), (HW + MLP) ** -0.5, 0.0625, ((0, 4), (1, 2)))
    w_mlp_out = normal_values(keys[9], (MLP, D), (HW + MLP) ** -0.5, 0.0625, ((0, 4), (1, 2)))
    return dict(tokens=tokens, mod_shift=mod_shift, mod_scale=mod_scale, mod_gate=mod_gate, w_qkv=w_qkv, w_mlp_in=w_mlp_in, q_gain=q_gain, k_gain=k_gain, w_attn_out=w_attn_out, w_mlp_out=w_mlp_out)


def layer_norm(vector):
    centered = vector - lax.optimization_barrier(jnp.mean(vector, axis=-1, keepdims=True))
    variance = lax.optimization_barrier(jnp.mean(centered * centered, axis=-1, keepdims=True))
    return centered * lax.rsqrt(variance + 1e-06)

def rms_gain(vector, scaling):
    mean_square = lax.optimization_barrier(jnp.mean(vector * vector, axis=-1, keepdims=True))
    return vector * lax.rsqrt(mean_square + 1e-06) * scaling

def reference(tokens, mod_shift, mod_scale, mod_gate, w_qkv, w_mlp_in, q_gain, k_gain, w_attn_out, w_mlp_out):
    inputs = tokens.astype(jnp.float32)
    modded = (layer_norm(inputs) * (1.0 + mod_scale) + mod_shift).astype(jnp.bfloat16)
    projected = jnp.dot(modded, w_qkv.reshape(D, 3 * HEADS * HD), preferred_element_type=jnp.float32)
    projected = projected.reshape(TOKENS, 3, HEADS, HD)
    queries = rms_gain(projected[:, 0], q_gain).astype(jnp.bfloat16)
    key_rows = rms_gain(projected[:, 1], k_gain).astype(jnp.bfloat16)
    value_rows = projected[:, 2].astype(jnp.bfloat16)
    hidden_pre = jnp.dot(modded, w_mlp_in, preferred_element_type=jnp.float32)
    activated = jax.nn.gelu(hidden_pre, approximate=True).astype(jnp.bfloat16)
    grid_rows = TILE * N_SY
    grid_cols = TILE * N_SX
    half_side = TILE // 2

    def to_grid(layout):
        shaped = layout.reshape(N_SY, N_SX, TILE, TILE, HEADS, HD).transpose(0, 2, 1, 3, 4, 5)
        return shaped.reshape(grid_rows, grid_cols, HEADS, HD)
    pad_spec = ((half_side, half_side), (half_side, half_side), (0, 0), (0, 0))
    key_grid = jnp.pad(to_grid(key_rows), pad_spec)
    value_grid = jnp.pad(to_grid(value_rows), pad_spec)
    query_tiles = queries.reshape(N_SY * N_SX, TILE * TILE, HEADS, HD)
    offsets = jnp.arange(2 * TILE, dtype=jnp.int32)

    def one_tile(tile_index):
        row_index = tile_index // N_SX
        col_index = tile_index % N_SX
        zero_index = jnp.zeros((), jnp.int32)
        row_start = (row_index * TILE).astype(jnp.int32)
        col_start = (col_index * TILE).astype(jnp.int32)
        corner = (row_start, col_start, zero_index, zero_index)
        window_keys = lax.dynamic_slice(key_grid, corner, (2 * TILE, 2 * TILE, HEADS, HD)).reshape(4 * TILE * TILE, HEADS, HD)
        window_values = lax.dynamic_slice(value_grid, corner, (2 * TILE, 2 * TILE, HEADS, HD)).reshape(4 * TILE * TILE, HEADS, HD)
        row_pos = row_index * TILE - half_side + offsets
        col_pos = col_index * TILE - half_side + offsets
        row_ok = (row_pos >= 0) & (row_pos < grid_rows)
        col_ok = (col_pos >= 0) & (col_pos < grid_cols)
        in_grid = (row_ok[:, None] & col_ok[None, :]).reshape(4 * TILE * TILE)
        query_block = lax.dynamic_index_in_dim(query_tiles, tile_index, 0, keepdims=False)
        scores = jnp.einsum('qhd,khd->hqk', query_block.astype(jnp.float32), window_keys.astype(jnp.float32)) * HD ** (-0.5)
        scores = jnp.where(in_grid[None, None, :], scores, -jnp.inf)
        row_max = lax.optimization_barrier(jnp.max(scores, axis=-1, keepdims=True))
        numerators = jnp.exp(scores - row_max)
        weights = (numerators / lax.optimization_barrier(jnp.sum(numerators, axis=-1, keepdims=True))).astype(jnp.bfloat16)
        mixed_rows = jnp.einsum('hqk,khd->qhd', weights.astype(jnp.float32), window_values.astype(jnp.float32))
        return mixed_rows.astype(jnp.bfloat16)
    attended = lax.map(one_tile, jnp.arange(N_SY * N_SX, dtype=jnp.int32)).reshape(TOKENS, HEADS * HD)
    branch = jnp.dot(attended, w_attn_out, preferred_element_type=jnp.float32)
    branch = branch + jnp.dot(activated, w_mlp_out, preferred_element_type=jnp.float32)
    return (inputs + mod_gate * branch).astype(jnp.bfloat16)
```

```python
import jax
import jax.numpy as jnp
from jax import lax
from jax.sharding import PartitionSpec as P

TILE = 20


def with_halo(cells, sides, width):
    for axis, dim in sides:
        count = lax.axis_size(axis)
        ends = count - 1
        head = lax.slice_in_dim(cells, 0, width, axis=dim)
        tail = lax.slice_in_dim(cells, cells.shape[dim] - width, cells.shape[dim], axis=dim)
        cells = jnp.concatenate(
            [
                lax.ppermute(tail, axis, [(i, (i + 1) % count) for i in range(ends)]),
                cells,
                lax.ppermute(head, axis, [((i + 1) % count, i) for i in range(ends)]),
            ],
            axis=dim,
        )
    return cells


def layer_norm(vector):
    centered = vector - jnp.mean(vector, axis=-1, keepdims=True)
    variance = jnp.mean(centered * centered, axis=-1, keepdims=True)
    return centered * lax.rsqrt(variance + 1e-06)


def rms_gain(vector, scaling):
    mean_square = jnp.mean(vector * vector, axis=-1, keepdims=True)
    return vector * lax.rsqrt(mean_square + 1e-06) * scaling


def gathered_plan(
    tokens, mod_shift, mod_scale, mod_gate, w_qkv, w_mlp_in, q_gain, k_gain, w_attn_out, w_mlp_out
):
    tok_rows, model_width = tokens.shape
    tile_side = TILE
    half_side = TILE // 2
    inputs = tokens.astype(jnp.float32)
    modded = (layer_norm(inputs) * (1.0 + mod_scale) + mod_shift).astype(jnp.bfloat16)
    local_heads, head_dim = q_gain.shape
    local_width = local_heads * head_dim
    pieces = (
        lax.all_gather(w_qkv, "sx", axis=0, tiled=True),
        lax.all_gather(w_mlp_in, "sx", axis=0, tiled=True),
    )
    piece_rows = pieces[0].shape[0]
    qkv_sum = jnp.dot(
        modded, pieces[0].reshape(piece_rows, 3 * local_width), preferred_element_type=jnp.float32
    )
    mlp_sum = jnp.dot(modded, pieces[1], preferred_element_type=jnp.float32)
    qkv_parts = qkv_sum.reshape(tok_rows, 3, local_heads, head_dim)
    queries = rms_gain(qkv_parts[:, 0], q_gain).astype(jnp.bfloat16)
    key_rows = rms_gain(qkv_parts[:, 1], k_gain).astype(jnp.bfloat16)
    value_rows = qkv_parts[:, 2].astype(jnp.bfloat16)
    key_value = jnp.concatenate(
        [key_rows.reshape(tok_rows, local_width), value_rows.reshape(tok_rows, local_width)], axis=1
    )
    key_value = key_value.reshape(tile_side, tile_side, 2 * local_width)
    extended = with_halo(key_value, (("sy", 0), ("sx", 1)), half_side)
    window = extended.reshape(4 * tok_rows, 2 * local_width)
    window_keys = window[:, :local_width].reshape(4 * tok_rows, local_heads, head_dim)
    window_values = window[:, local_width:].reshape(4 * tok_rows, local_heads, head_dim)
    offsets = jnp.arange(2 * tile_side, dtype=jnp.int32)
    row_pos = lax.axis_index("sy") * tile_side - half_side + offsets
    col_pos = lax.axis_index("sx") * tile_side - half_side + offsets
    row_ok = (row_pos >= 0) & (row_pos < tile_side * lax.axis_size("sy"))
    col_ok = (col_pos >= 0) & (col_pos < tile_side * lax.axis_size("sx"))
    in_grid = (row_ok[:, None] & col_ok[None, :]).reshape(4 * tok_rows)
    scores = jnp.einsum(
        "qhd,khd->hqk", queries, window_keys, preferred_element_type=jnp.float32
    ) * head_dim ** (-0.5)
    scores = jnp.where(in_grid[None, None, :], scores, -jnp.inf)
    row_max = jnp.max(scores, axis=-1, keepdims=True)
    numerators = jnp.exp(scores - row_max)
    weights = (numerators / jnp.sum(numerators, axis=-1, keepdims=True)).astype(jnp.bfloat16)
    attended = jnp.einsum(
        "hqk,khd->qhd", weights, window_values, preferred_element_type=jnp.float32
    )
    attended = attended.astype(jnp.bfloat16).reshape(tok_rows, local_width)
    activated = jax.nn.gelu(mlp_sum, approximate=True).astype(jnp.bfloat16)
    pieces = (
        lax.all_gather(w_attn_out, "sx", axis=1, tiled=True),
        lax.all_gather(w_mlp_out, "sx", axis=1, tiled=True),
    )
    product_term = jnp.dot(attended, pieces[0], preferred_element_type=jnp.float32)
    product_term = product_term + jnp.dot(activated, pieces[1], preferred_element_type=jnp.float32)
    reduced = lax.psum_scatter(
        product_term.astype(jnp.bfloat16), "tp", scatter_dimension=1, tiled=True
    ).astype(jnp.float32)
    block_width = model_width // lax.axis_size("tp")
    first_col = lax.axis_index("tp") * block_width
    residual_part = lax.dynamic_slice_in_dim(inputs, first_col, block_width, 1)
    gate_part = lax.dynamic_slice_in_dim(mod_gate, first_col, block_width, 0)
    return (residual_part + gate_part * reduced).astype(jnp.bfloat16)


def swap(cells, axis, bit):
    count = lax.axis_size(axis)
    return lax.ppermute(cells, axis, [(i, i ^ bit) for i in range(count)])


def shift(cells, axis, step):
    count = lax.axis_size(axis)
    return lax.ppermute(
        cells, axis, [(i, i + step) for i in range(count) if 0 <= i + step < count]
    )


def dot(left, right):
    return jnp.dot(left, right, preferred_element_type=jnp.float32)


def in_order(bit, mine, other):
    return jnp.where(bit == 0, mine, other), jnp.where(bit == 0, other, mine)


def border_pick(side, tile_side, rows, dtype):
    half = tile_side // 2
    taken = lax.broadcasted_iota(jnp.int32, (tile_side * half, rows), 0)
    token = lax.broadcasted_iota(jnp.int32, (tile_side * half, rows), 1)
    first = jnp.where(side == 0, half, 0)
    return (taken // half * tile_side + taken % half + first == token).astype(dtype)


def paired_plan(
    tokens, mod_shift, mod_scale, mod_gate, w_qkv, w_mlp_in, q_gain, k_gain, w_attn_out, w_mlp_out
):
    tok_rows, model_width = tokens.shape
    half_width = w_mlp_in.shape[0]
    heads, head_dim = q_gain.shape
    width = heads * head_dim
    side = lax.axis_index("sx")
    part = lax.axis_index("tp")
    core, far = part % 2, part // 2
    bf16 = jnp.bfloat16

    quarter = half_width // 4
    sent = lax.dynamic_slice_in_dim(tokens, (1 - side) * half_width + part * quarter, quarter, 1)
    piece = swap(sent, "sx", 1)
    pieces = jnp.concatenate(in_order(far, piece, swap(piece, "tp", 2)), axis=1)
    near = swap(pieces, "tp", 1)
    even, odd = in_order(core, pieces, near)
    other_tokens = jnp.concatenate(
        [even[:, :quarter], odd[:, :quarter], even[:, quarter:], odd[:, quarter:]], axis=1
    )

    inputs = tokens.astype(jnp.float32)
    mean = jnp.mean(inputs, axis=-1, keepdims=True)
    centered = inputs - mean
    scaling = lax.rsqrt(jnp.mean(centered * centered, axis=-1, keepdims=True) + 1e-06)
    stats = jnp.concatenate([mean, scaling], axis=1)
    other_stats = swap(stats, "sx", 1)
    first = side * half_width
    gain_part = 1.0 + lax.dynamic_slice_in_dim(mod_scale, first, half_width, 0)
    shift_part = lax.dynamic_slice_in_dim(mod_shift, first, half_width, 0)

    def modulate(cells, moments):
        cells = (cells.astype(jnp.float32) - moments[:, :1]) * moments[:, 1:]
        return (cells * gain_part + shift_part).astype(bf16)

    own = modulate(lax.dynamic_slice_in_dim(tokens, first, half_width, 1), stats)
    other = modulate(other_tokens, other_stats)
    own_border = dot(border_pick(side, TILE, tok_rows, bf16), own).astype(bf16)
    other_border = dot(border_pick(1 - side, TILE, tok_rows, bf16), other).astype(bf16)

    w_heads = w_qkv.reshape(half_width, 3 * width)
    w_keys = w_heads[:, width:]
    own_border_kv = dot(own_border, w_keys)
    other_border_kv = dot(other_border, w_keys)
    own_qkv = dot(own, w_heads)
    other_qkv = dot(other, w_heads)
    own_hidden = dot(own, w_mlp_in)
    other_hidden = dot(other, w_mlp_in)

    border_kv = other_border_kv + swap(own_border_kv.astype(bf16), "sx", 1).astype(jnp.float32)
    qkv = own_qkv + swap(other_qkv.astype(bf16), "sx", 1).astype(jnp.float32)
    hidden_other = other_hidden + swap(own_hidden.astype(bf16), "sx", 1).astype(jnp.float32)
    hidden_own = own_hidden + swap(other_hidden.astype(bf16), "sx", 1).astype(jnp.float32)

    def columns(cells, head, base=0):
        return cells[:, base + head * head_dim : base + (head + 1) * head_dim]

    queries = [rms_gain(columns(qkv, h), q_gain[h]).astype(bf16) for h in range(heads)]

    def keys_values(cells, base):
        keys = [rms_gain(columns(cells, h, base), k_gain[h]).astype(bf16) for h in range(heads)]
        return jnp.concatenate(keys + [cells[:, base + width : base + 2 * width].astype(bf16)], axis=1)

    own_kv = keys_values(qkv, width)
    border = keys_values(border_kv, 0)
    half_rows, half_border = own_kv.shape[0] // 2, border.shape[0] // 2
    above = shift(jnp.concatenate([own_kv[half_rows:], border[half_border:]], axis=0), "sy", 1)
    below = shift(jnp.concatenate([own_kv[:half_rows], border[:half_border]], axis=0), "sy", -1)
    window = jnp.concatenate([own_kv, border, above, below], axis=0)
    place = jnp.arange(window.shape[0], dtype=jnp.int32)
    start_above = own_kv.shape[0] + border.shape[0]
    start_below = start_above + above.shape[0]
    row = lax.axis_index("sy")
    in_grid = (place < start_above) | jnp.where(
        place < start_below, row > 0, row < lax.axis_size("sy") - 1
    )
    attended = []
    for h in range(heads):
        scores = dot(queries[h], columns(window, h).T) * head_dim ** (-0.5)
        scores = jnp.where(in_grid[None, :], scores, -jnp.inf)
        numerators = jnp.exp(scores - jnp.max(scores, axis=-1, keepdims=True))
        weights = (numerators / jnp.sum(numerators, axis=-1, keepdims=True)).astype(bf16)
        attended.append(dot(weights, columns(window, h, width)).astype(bf16))
    attended = jnp.concatenate(attended, axis=1)
    other_attended = swap(attended, "sx", 1)

    activated_own = jax.nn.gelu(hidden_own, approximate=True).astype(bf16)
    activated_other = jax.nn.gelu(hidden_other, approximate=True).astype(bf16)

    def branch(heads_part, hidden_part):
        return dot(heads_part, w_attn_out) + dot(hidden_part, w_mlp_out)

    block = half_width // 2

    def halves(cells):
        left, right = cells[:, :block], cells[:, block:]
        return jnp.where(core == 0, left, right), jnp.where(core == 0, right, left)

    def core_sum(cells):
        keep, send = halves(cells)
        return keep + swap(send.astype(bf16), "tp", 1).astype(jnp.float32)

    other_sum = core_sum(branch(other_attended, activated_other))
    own_sum = core_sum(branch(attended, activated_own))
    got = swap(other_sum.astype(bf16), "sx", 1).astype(jnp.float32)
    keep = jnp.where(far == side, own_sum, got)
    send = jnp.where(far == side, got, own_sum)
    reduced = keep + swap(send.astype(bf16), "tp", 2).astype(jnp.float32)

    first_col = part * block
    residual_part = lax.dynamic_slice_in_dim(tokens, first_col, block, 1).astype(jnp.float32)
    gate_part = lax.dynamic_slice_in_dim(mod_gate, first_col, block, 0)
    return (residual_part + gate_part * reduced).astype(bf16)


def shards(*arrays):
    if lax.axis_size("sx") == 2 and lax.axis_size("tp") == 4:
        return paired_plan(*arrays)
    return gathered_plan(*arrays)


def solution(mesh):
    placed = (
        P(("sy", "sx"), None),
        P(),
        P(),
        P(),
        P("sx", None, "tp"),
        P("sx", "tp"),
        P("tp", None),
        P("tp", None),
        P("tp", "sx"),
        P("tp", "sx"),
    )
    return jax.shard_map(
        shards, mesh=mesh, in_specs=placed, out_specs=P(("sy", "sx"), "tp"), check_vma=False
    )
```

```python
import jax
import jax.numpy as jnp
import numpy as np
from jax import lax
from jax.experimental import pallas as pl
from jax.experimental.pallas import tpu as pltpu
from jax.sharding import PartitionSpec as P

TILE = 20


def with_halo(cells, sides, width):
    for axis, dim in sides:
        count = lax.axis_size(axis)
        ends = count - 1
        head = lax.slice_in_dim(cells, 0, width, axis=dim)
        tail = lax.slice_in_dim(cells, cells.shape[dim] - width, cells.shape[dim], axis=dim)
        cells = jnp.concatenate(
            [
                lax.ppermute(tail, axis, [(i, (i + 1) % count) for i in range(ends)]),
                cells,
                lax.ppermute(head, axis, [((i + 1) % count, i) for i in range(ends)]),
            ],
            axis=dim,
        )
    return cells


def layer_norm(vector):
    centered = vector - jnp.mean(vector, axis=-1, keepdims=True)
    variance = jnp.mean(centered * centered, axis=-1, keepdims=True)
    return centered * lax.rsqrt(variance + 1e-06)


def rms_gain(vector, scaling):
    mean_square = jnp.mean(vector * vector, axis=-1, keepdims=True)
    return vector * lax.rsqrt(mean_square + 1e-06) * scaling


def gathered_plan(
    tokens, mod_shift, mod_scale, mod_gate, w_qkv, w_mlp_in, q_gain, k_gain, w_attn_out, w_mlp_out
):
    tok_rows, model_width = tokens.shape
    tile_side = TILE
    half_side = TILE // 2
    inputs = tokens.astype(jnp.float32)
    modded = (layer_norm(inputs) * (1.0 + mod_scale) + mod_shift).astype(jnp.bfloat16)
    local_heads, head_dim = q_gain.shape
    local_width = local_heads * head_dim
    pieces = (
        lax.all_gather(w_qkv, "sx", axis=0, tiled=True),
        lax.all_gather(w_mlp_in, "sx", axis=0, tiled=True),
    )
    piece_rows = pieces[0].shape[0]
    qkv_sum = jnp.dot(
        modded, pieces[0].reshape(piece_rows, 3 * local_width), preferred_element_type=jnp.float32
    )
    mlp_sum = jnp.dot(modded, pieces[1], preferred_element_type=jnp.float32)
    qkv_parts = qkv_sum.reshape(tok_rows, 3, local_heads, head_dim)
    queries = rms_gain(qkv_parts[:, 0], q_gain).astype(jnp.bfloat16)
    key_rows = rms_gain(qkv_parts[:, 1], k_gain).astype(jnp.bfloat16)
    value_rows = qkv_parts[:, 2].astype(jnp.bfloat16)
    key_value = jnp.concatenate(
        [key_rows.reshape(tok_rows, local_width), value_rows.reshape(tok_rows, local_width)], axis=1
    )
    key_value = key_value.reshape(tile_side, tile_side, 2 * local_width)
    extended = with_halo(key_value, (("sy", 0), ("sx", 1)), half_side)
    window = extended.reshape(4 * tok_rows, 2 * local_width)
    window_keys = window[:, :local_width].reshape(4 * tok_rows, local_heads, head_dim)
    window_values = window[:, local_width:].reshape(4 * tok_rows, local_heads, head_dim)
    offsets = jnp.arange(2 * tile_side, dtype=jnp.int32)
    row_pos = lax.axis_index("sy") * tile_side - half_side + offsets
    col_pos = lax.axis_index("sx") * tile_side - half_side + offsets
    row_ok = (row_pos >= 0) & (row_pos < tile_side * lax.axis_size("sy"))
    col_ok = (col_pos >= 0) & (col_pos < tile_side * lax.axis_size("sx"))
    in_grid = (row_ok[:, None] & col_ok[None, :]).reshape(4 * tok_rows)
    scores = jnp.einsum(
        "qhd,khd->hqk", queries, window_keys, preferred_element_type=jnp.float32
    ) * head_dim ** (-0.5)
    scores = jnp.where(in_grid[None, None, :], scores, -jnp.inf)
    row_max = jnp.max(scores, axis=-1, keepdims=True)
    numerators = jnp.exp(scores - row_max)
    weights = (numerators / jnp.sum(numerators, axis=-1, keepdims=True)).astype(jnp.bfloat16)
    attended = jnp.einsum(
        "hqk,khd->qhd", weights, window_values, preferred_element_type=jnp.float32
    )
    attended = attended.astype(jnp.bfloat16).reshape(tok_rows, local_width)
    activated = jax.nn.gelu(mlp_sum, approximate=True).astype(jnp.bfloat16)
    pieces = (
        lax.all_gather(w_attn_out, "sx", axis=1, tiled=True),
        lax.all_gather(w_mlp_out, "sx", axis=1, tiled=True),
    )
    product_term = jnp.dot(attended, pieces[0], preferred_element_type=jnp.float32)
    product_term = product_term + jnp.dot(activated, pieces[1], preferred_element_type=jnp.float32)
    reduced = lax.psum_scatter(
        product_term.astype(jnp.bfloat16), "tp", scatter_dimension=1, tiled=True
    ).astype(jnp.float32)
    block_width = model_width // lax.axis_size("tp")
    first_col = lax.axis_index("tp") * block_width
    residual_part = lax.dynamic_slice_in_dim(inputs, first_col, block_width, 1)
    gate_part = lax.dynamic_slice_in_dim(mod_gate, first_col, block_width, 0)
    return (residual_part + gate_part * reduced).astype(jnp.bfloat16)


def swap(cells, axis, bit):
    count = lax.axis_size(axis)
    return lax.ppermute(cells, axis, [(i, i ^ bit) for i in range(count)])


def shift(cells, axis, step):
    count = lax.axis_size(axis)
    return lax.ppermute(
        cells, axis, [(i, i + step) for i in range(count) if 0 <= i + step < count]
    )


def dot(left, right):
    return jnp.dot(left, right, preferred_element_type=jnp.float32)


BF16, F32 = jnp.bfloat16, jnp.float32
LANES = 128


def width_of(total, most):
    return max(w for w in range(LANES, most + 1, LANES) if total % w == 0)


def call(body, grid, ins, outs, scratch=(), after=(), vmem=16, cost=(1000, 1000)):
    n_in, n_after = len(ins), len(after)

    def kernel(*refs):
        body(*refs[:n_in], *refs[n_in + n_after :])

    def spec(block, index):
        if block is None:
            return pl.BlockSpec(memory_space=index)
        return pl.BlockSpec(block, index)

    return pl.pallas_call(
        kernel,
        grid=(grid,),
        in_specs=[spec(b, i) for _, b, i in ins] + [pl.BlockSpec(memory_space=pl.ANY)] * n_after,
        out_specs=[spec(b, i) for _, _, b, i in outs],
        out_shape=[jax.ShapeDtypeStruct(s, d) for s, d, _, _ in outs],
        scratch_shapes=list(scratch),
        compiler_params=pltpu.CompilerParams(vmem_limit_bytes=vmem * 2**20),
        cost_estimate=pl.CostEstimate(flops=cost[0], bytes_accessed=cost[1], transcendentals=0),
    )(*[a for a, _, _ in ins], *after)


def in_order(bit, mine, other):
    return jnp.where(bit == 0, mine, other), jnp.where(bit == 0, other, mine)


def hold(cells, *earlier, cost=0):
    return pl.pallas_call(
        lambda *refs: None,
        in_specs=[pl.BlockSpec(memory_space=pl.ANY)] * (1 + len(earlier)),
        out_specs=pl.BlockSpec(memory_space=pl.ANY),
        out_shape=jax.ShapeDtypeStruct(cells.shape, cells.dtype),
        input_output_aliases={0: 0},
        compiler_params=pltpu.CompilerParams(vmem_limit_bytes=2**20),
        cost_estimate=pl.CostEstimate(flops=0, bytes_accessed=cost, transcendentals=0),
    )(cells, *earlier)


def at(*place):
    return lambda *_: place


def border_rows(tile_side):
    half = tile_side // 2
    return (half * half + 15) // 16 * 16


def border_picks(tile_side, side):
    half, rows = tile_side // 2, border_rows(tile_side)
    picks = np.zeros((2, 2 * rows, tile_side * tile_side), np.float32)
    for which in range(2):
        for low in range(2):
            for i in range(half):
                for j in range(half):
                    token = (low * half + i) * tile_side + j + (half if which == 0 else 0)
                    picks[which, low * rows + i * half + j, token] = 1
    left, right = jnp.asarray(picks[0], BF16), jnp.asarray(picks[1], BF16)
    return jnp.where(side == 0, left, right), jnp.where(side == 0, right, left)


def rest_of_first(own, other, pick, heads_weights, hidden_weights, cut, after=()):
    rows, depth = own.shape
    width, hidden = heads_weights[0].shape[1], hidden_weights.shape[1]
    border = pick.shape[0]
    block = width_of(hidden, 384)

    def body(own_ref, other_ref, pick_ref, wq_ref, wk_ref, wv_ref, w_ref, qkv_ref, border_ref, sums_ref, a_ref, b_ref):
        @pl.when(pl.program_id(0) == 0)
        def _():
            taken = dot(pick_ref[...], other_ref[...]).astype(BF16)
            for i, ref in enumerate((wq_ref, wk_ref, wv_ref)):
                qkv_ref[:, i * width : (i + 1) * width] = dot(own_ref[...], ref[...])
            for i, ref in enumerate((wk_ref, wv_ref)):
                border_ref[:, i * width : (i + 1) * width] = dot(taken, ref[...])

        sums = dot(other_ref[...], w_ref[...])
        sums_ref[...] = sums
        a_ref[...] = sums[:cut].astype(BF16)
        b_ref[...] = sums[cut:].astype(BF16)

    whole = at(0, 0)
    column = lambda j: (0, j)
    return call(
        body, hidden // block,
        [(own, own.shape, whole), (other, other.shape, whole), (pick, pick.shape, whole)]
        + [(w, w.shape, whole) for w in heads_weights]
        + [(hidden_weights, (depth, block), column)],
        [
            ((rows, 3 * width), F32, (rows, 3 * width), whole),
            ((border, 2 * width), F32, (border, 2 * width), whole),
            ((rows, hidden), F32, (rows, block), column),
            ((cut, hidden), BF16, (cut, block), column),
            ((rows - cut, hidden), BF16, (rows - cut, block), column),
        ],
        after=after, vmem=28,
        cost=(
            2 * depth * (rows * 3 * width + border * 2 * width + rows * hidden),
            2 * depth * (2 * rows + 3 * width + hidden) + 4 * (3 * rows + 2 * border) * width + 6 * rows * hidden,
        ),
    )


def norm_heads(mine, got, border_mine, border_got, q_gain, k_gain, after=()):
    rows, heads, head_dim = mine.shape[0], q_gain.shape[0], q_gain.shape[2]
    half_border = border_mine.shape[0] // 2
    sent_own = (rows // 2 + 15) // 16 * 16
    sent = sent_own + half_border

    def body(*refs):
        q, k, v, q2, k2, v2, bk, bv, bk2, bv2, qg, kg = [r[...].astype(F32) for r in refs[:12]]
        queries_ref, own_ref, border_ref, lower_ref, upper_ref = refs[12:]
        queries_ref[...] = rms_gain(q + q2, qg[0]).astype(BF16)
        own = jnp.concatenate([rms_gain(k + k2, kg[0]), v + v2], axis=1).astype(BF16)
        border = jnp.concatenate([rms_gain(bk + bk2, kg[0]), bv + bv2], axis=1).astype(BF16)
        own_ref[...] = own
        border_ref[...] = border
        upper_ref[:sent_own] = own[:sent_own]
        upper_ref[sent_own:] = border[:half_border]
        lower_ref[:sent_own] = own[rows - sent_own :]
        lower_ref[sent_own:] = border[half_border:]

    def third(array, group):
        return (array, (array.shape[0], head_dim), lambda h: (0, group * heads + h))

    def beside(count):
        return ((count, 2 * heads * head_dim), BF16, (count, 2 * head_dim), lambda h: (0, h))

    gain = lambda h: (h, 0, 0)
    return call(
        body, heads,
        [third(mine, g) for g in range(3)] + [third(got, g) for g in range(3)]
        + [third(border_mine, g) for g in range(2)] + [third(border_got, g) for g in range(2)]
        + [(q_gain, (1, 1, head_dim), gain), (k_gain, (1, 1, head_dim), gain)],
        [
            ((rows, heads * head_dim), BF16, (rows, head_dim), lambda h: (0, h)),
            beside(rows), beside(2 * half_border), beside(sent), beside(sent),
        ],
        after=after,
    )


def attend(queries, keys_values, bias, heads, after=()):
    rows, head_dim = queries.shape[0], queries.shape[1] // heads
    spare = bias.shape[1] - sum(k.shape[0] for k in keys_values)

    def body(queries_ref, bias_ref, *refs):
        blocks = [r[...] for r in refs[:-1]]
        if spare:
            blocks.append(jnp.zeros((spare, 2 * head_dim), BF16))
        both = jnp.concatenate(blocks, axis=0)
        keys, values = both[:, :head_dim], both[:, head_dim:]
        scores = lax.dot_general(queries_ref[...], keys, (((1,), (1,)), ((), ())), preferred_element_type=F32)
        scores = scores * head_dim ** (-0.5) + bias_ref[...]
        numerators = jnp.exp(scores - jnp.max(scores, axis=-1, keepdims=True))
        total = jnp.sum(numerators, axis=-1, keepdims=True)
        refs[-1][...] = (dot(numerators.astype(BF16), values) / total).astype(BF16)

    head = lambda h: (0, h)
    return call(
        body, heads,
        [(queries, (rows, head_dim), head), (bias, bias.shape, at(0, 0))]
        + [(k, (k.shape[0], 2 * head_dim), head) for k in keys_values],
        [((rows, heads * head_dim), BF16, (rows, head_dim), head)],
        after=after,
    )[0]


def paired_plan(
    tokens, mod_shift, mod_scale, mod_gate, w_qkv, w_mlp_in, q_gain, k_gain, w_attn_out, w_mlp_out
):
    tok_rows, model_width = tokens.shape
    half_width, hidden = w_mlp_in.shape
    heads, head_dim = q_gain.shape
    width = heads * head_dim
    side = lax.axis_index("sx")
    part = lax.axis_index("tp")
    core, far = part % 2, part // 2
    mid = hidden // 2
    block = half_width // 2
    own_pick, other_pick = border_picks(TILE, side)
    q_gain, k_gain = q_gain[:, None, :], k_gain[:, None, :]

    piece_width = half_width // 2
    other_first = (1 - side) * half_width + core * piece_width
    sent = lax.dynamic_slice_in_dim(tokens, other_first, piece_width, 1)
    piece = swap(sent, "sx", 1)
    cells = tokens.astype(F32)
    mean = jnp.mean(cells, axis=-1, keepdims=True)
    centered = cells - mean
    scaling = lax.rsqrt(jnp.mean(centered * centered, axis=-1, keepdims=True) + 1e-06)
    stats = jnp.concatenate([mean, scaling], axis=1)
    other_stats = swap(stats, "sx", 1)
    first = side * half_width
    gain_part = 1.0 + lax.dynamic_slice_in_dim(mod_scale, first, half_width, 0)
    shift_part = lax.dynamic_slice_in_dim(mod_shift, first, half_width, 0)

    def modulate(cells, pair):
        cells = (cells.astype(F32) - pair[:, :1]) * pair[:, 1:]
        return (cells * gain_part + shift_part).astype(BF16)

    def projected(cells, weights):
        sums = dot(cells, weights)
        return sums, sums.astype(BF16)

    w_queries, w_keys, w_values = [w_qkv[:, group] for group in range(3)]

    def heads_of(cells):
        return jnp.concatenate([dot(cells, w) for w in (w_queries, w_keys, w_values)], axis=1)

    def border_of(pick, cells):
        cells = dot(pick, cells).astype(BF16)
        return jnp.concatenate([dot(cells, w) for w in (w_keys, w_values)], axis=1)

    own = modulate(lax.dynamic_slice_in_dim(tokens, first, half_width, 1), stats)
    own_border = border_of(own_pick, own).astype(BF16)
    got_border = swap(own_border, "sx", 1)
    own = hold(own, own_border)
    own_sums, own_sent = projected(own, w_mlp_in)
    piece = hold(piece, own_sent)
    near = swap(piece, "tp", 1)
    other = modulate(jnp.concatenate(in_order(core, piece, near), axis=1), other_stats)
    other_qkv = heads_of(other).astype(BF16)
    got_qkv = swap(other_qkv, "sx", 1)
    got_own = swap(hold(own_sent, other_qkv), "sx", 1)
    cut = (tok_rows // 2 + 15) // 16 * 16
    own_qkv, other_border, other_sums, other_a, other_b = rest_of_first(
        own, other, other_pick, (w_queries, w_keys, w_values), w_mlp_in, cut, [other_qkv, got_border]
    )

    queries, own_kv, border_kv, lower, upper = norm_heads(
        own_qkv, got_qkv, other_border, got_border, q_gain, k_gain, [other_a]
    )
    above = shift(lower, "sy", 1)
    below = shift(upper, "sy", -1)

    def gelu_dot(sums, got, rows):
        return dot(jax.nn.gelu(sums + got.astype(F32), approximate=True).astype(BF16), rows)

    row = lax.axis_index("sy")
    extra = tok_rows // 2
    half_border, taken = border_kv.shape[0] // 2, (TILE // 2) ** 2
    sent_own = lower.shape[0] - half_border
    inside = np.zeros(((own_kv.shape[0] + 2 * half_border + 2 * lower.shape[0] + 127) // 128 * 128,), np.int32)
    inside[:tok_rows] = 1
    for start in (tok_rows, tok_rows + half_border):
        inside[start : start + taken] = 1
    start = tok_rows + 2 * half_border
    inside[start + sent_own - extra : start + sent_own] = 2
    inside[start + sent_own : start + sent_own + taken] = 2
    start += lower.shape[0]
    inside[start : start + extra] = 3
    inside[start + sent_own : start + sent_own + taken] = 3
    there = (inside == 1) | ((inside == 2) & (row > 0)) | ((inside == 3) & (row < lax.axis_size("sy") - 1))
    bias = jnp.where(there, 0.0, -jnp.inf).astype(F32)[None]
    attended = attend(queries, [own_kv, border_kv, above, below], bias, heads)
    got_attended = swap(attended, "sx", 1)
    got_other_a = swap(other_a, "sx", 1)
    other_sums = hold(other_sums, attended)
    other_branch = gelu_dot(other_sums, got_own, w_mlp_out)
    got_other_a = swap(other_a, "sx", 1)
    got_other_b = swap(hold(other_b, other_branch), "sx", 1)

    def split(cells):
        left, right = cells[:, :block], cells[:, block:]
        return jnp.where(core == 0, right, left).astype(BF16), jnp.where(core == 0, left, right)

    def core_sum(cells, *earlier):
        send, keep = split(cells)
        return keep + swap(hold(send, *earlier), "tp", 1).astype(F32)

    own_sums = hold(own_sums, other_branch)
    own_part = gelu_dot(own_sums[:cut], got_other_a, w_mlp_out) + dot(attended[:cut], w_attn_out)
    other_branch = hold(other_branch, own_part)
    other_sum = core_sum(other_branch + dot(got_attended, w_attn_out))
    half_rows = tok_rows // 2
    send = lax.dynamic_slice_in_dim(other_sum, (1 - far) * half_rows, half_rows, 0).astype(BF16)
    keep = lax.dynamic_slice_in_dim(other_sum, far * half_rows, half_rows, 0)
    crossing = (keep + swap(send, "tp", 2).astype(F32)).astype(BF16)
    got = swap(crossing, "sx", 1)
    own_sum_a = core_sum(own_part)
    own_sums = hold(own_sums, own_part, crossing)
    own_sum_b = core_sum(gelu_dot(own_sums[cut:], got_other_b, w_mlp_out) + dot(attended[cut:], w_attn_out), got)

    others = lax.axis_size("tp") // 2
    homes = [(s * 2 * others + (1 - s) * 2 + c, s * 2 * others + s * 2 + c) for s in range(2) for c in range(2)]
    to_home = lambda cells: lax.ppermute(cells, ("sx", "tp"), homes)
    from_home = lambda cells: lax.ppermute(cells, ("sx", "tp"), [(b, a) for a, b in homes])
    come_a = to_home(own_sum_a.astype(BF16))
    come_b = to_home(own_sum_b.astype(BF16))
    got = hold(got, come_a)
    rest = from_home(got)
    own_sum = jnp.concatenate([own_sum_a + come_a.astype(F32), own_sum_b + come_b.astype(F32)], axis=0)
    reduced = jnp.where(far == side, own_sum, jnp.concatenate(in_order(far, got, rest), axis=0).astype(F32))

    first_col = hold(part[None], other_sum)[0] * block
    gate_part = lax.dynamic_slice_in_dim(mod_gate, first_col, block, 0)
    residual_part = lax.dynamic_slice_in_dim(tokens, first_col, block, 1).astype(F32)
    return (residual_part + gate_part * reduced).astype(BF16)


def shards(*arrays):
    if lax.axis_size("sx") == 2 and lax.axis_size("tp") == 4:
        return paired_plan(*arrays)
    return gathered_plan(*arrays)


def solution(mesh):
    placed = (
        P(("sy", "sx"), None),
        P(),
        P(),
        P(),
        P("sx", None, "tp"),
        P("sx", "tp"),
        P("tp", None),
        P("tp", None),
        P("tp", "sx"),
        P("tp", "sx"),
    )
    return jax.shard_map(
        shards, mesh=mesh, in_specs=placed, out_specs=P(("sy", "sx"), "tp"), check_vma=False
    )
```

```python
import jax
import jax.numpy as jnp
import numpy as np
from jax import lax
from jax.experimental import pallas as pl
from jax.experimental.pallas import tpu as pltpu
from jax.sharding import PartitionSpec as P

TILE = 20


def with_halo(cells, sides, width):
    for axis, dim in sides:
        count = lax.axis_size(axis)
        ends = count - 1
        head = lax.slice_in_dim(cells, 0, width, axis=dim)
        tail = lax.slice_in_dim(cells, cells.shape[dim] - width, cells.shape[dim], axis=dim)
        cells = jnp.concatenate(
            [
                lax.ppermute(tail, axis, [(i, (i + 1) % count) for i in range(ends)]),
                cells,
                lax.ppermute(head, axis, [((i + 1) % count, i) for i in range(ends)]),
            ],
            axis=dim,
        )
    return cells


def layer_norm(vector):
    centered = vector - jnp.mean(vector, axis=-1, keepdims=True)
    variance = jnp.mean(centered * centered, axis=-1, keepdims=True)
    return centered * lax.rsqrt(variance + 1e-06)


def rms_gain(vector, scaling):
    mean_square = jnp.mean(vector * vector, axis=-1, keepdims=True)
    return vector * lax.rsqrt(mean_square + 1e-06) * scaling


def gathered_plan(
    tokens, mod_shift, mod_scale, mod_gate, w_qkv, w_mlp_in, q_gain, k_gain, w_attn_out, w_mlp_out
):
    tok_rows, model_width = tokens.shape
    tile_side = TILE
    half_side = TILE // 2
    inputs = tokens.astype(jnp.float32)
    modded = (layer_norm(inputs) * (1.0 + mod_scale) + mod_shift).astype(jnp.bfloat16)
    local_heads, head_dim = q_gain.shape
    local_width = local_heads * head_dim
    pieces = (
        lax.all_gather(w_qkv, "sx", axis=0, tiled=True),
        lax.all_gather(w_mlp_in, "sx", axis=0, tiled=True),
    )
    piece_rows = pieces[0].shape[0]
    qkv_sum = jnp.dot(
        modded, pieces[0].reshape(piece_rows, 3 * local_width), preferred_element_type=jnp.float32
    )
    mlp_sum = jnp.dot(modded, pieces[1], preferred_element_type=jnp.float32)
    qkv_parts = qkv_sum.reshape(tok_rows, 3, local_heads, head_dim)
    queries = rms_gain(qkv_parts[:, 0], q_gain).astype(jnp.bfloat16)
    key_rows = rms_gain(qkv_parts[:, 1], k_gain).astype(jnp.bfloat16)
    value_rows = qkv_parts[:, 2].astype(jnp.bfloat16)
    key_value = jnp.concatenate(
        [key_rows.reshape(tok_rows, local_width), value_rows.reshape(tok_rows, local_width)], axis=1
    )
    key_value = key_value.reshape(tile_side, tile_side, 2 * local_width)
    extended = with_halo(key_value, (("sy", 0), ("sx", 1)), half_side)
    window = extended.reshape(4 * tok_rows, 2 * local_width)
    window_keys = window[:, :local_width].reshape(4 * tok_rows, local_heads, head_dim)
    window_values = window[:, local_width:].reshape(4 * tok_rows, local_heads, head_dim)
    offsets = jnp.arange(2 * tile_side, dtype=jnp.int32)
    row_pos = lax.axis_index("sy") * tile_side - half_side + offsets
    col_pos = lax.axis_index("sx") * tile_side - half_side + offsets
    row_ok = (row_pos >= 0) & (row_pos < tile_side * lax.axis_size("sy"))
    col_ok = (col_pos >= 0) & (col_pos < tile_side * lax.axis_size("sx"))
    in_grid = (row_ok[:, None] & col_ok[None, :]).reshape(4 * tok_rows)
    scores = jnp.einsum(
        "qhd,khd->hqk", queries, window_keys, preferred_element_type=jnp.float32
    ) * head_dim ** (-0.5)
    scores = jnp.where(in_grid[None, None, :], scores, -jnp.inf)
    row_max = jnp.max(scores, axis=-1, keepdims=True)
    numerators = jnp.exp(scores - row_max)
    weights = (numerators / jnp.sum(numerators, axis=-1, keepdims=True)).astype(jnp.bfloat16)
    attended = jnp.einsum(
        "hqk,khd->qhd", weights, window_values, preferred_element_type=jnp.float32
    )
    attended = attended.astype(jnp.bfloat16).reshape(tok_rows, local_width)
    activated = jax.nn.gelu(mlp_sum, approximate=True).astype(jnp.bfloat16)
    pieces = (
        lax.all_gather(w_attn_out, "sx", axis=1, tiled=True),
        lax.all_gather(w_mlp_out, "sx", axis=1, tiled=True),
    )
    product_term = jnp.dot(attended, pieces[0], preferred_element_type=jnp.float32)
    product_term = product_term + jnp.dot(activated, pieces[1], preferred_element_type=jnp.float32)
    reduced = lax.psum_scatter(
        product_term.astype(jnp.bfloat16), "tp", scatter_dimension=1, tiled=True
    ).astype(jnp.float32)
    block_width = model_width // lax.axis_size("tp")
    first_col = lax.axis_index("tp") * block_width
    residual_part = lax.dynamic_slice_in_dim(inputs, first_col, block_width, 1)
    gate_part = lax.dynamic_slice_in_dim(mod_gate, first_col, block_width, 0)
    return (residual_part + gate_part * reduced).astype(jnp.bfloat16)


def swap(cells, axis, bit):
    count = lax.axis_size(axis)
    return lax.ppermute(cells, axis, [(i, i ^ bit) for i in range(count)])


def shift(cells, axis, step):
    count = lax.axis_size(axis)
    return lax.ppermute(
        cells, axis, [(i, i + step) for i in range(count) if 0 <= i + step < count]
    )


def dot(left, right):
    return jnp.dot(left, right, preferred_element_type=jnp.float32)


BF16, F32 = jnp.bfloat16, jnp.float32
LANES = 128
EARLY = 20_000_000


def width_of(total, most):
    return max(w for w in range(LANES, most + 1, LANES) if total % w == 0)


def call(body, grid, ins, outs, scratch=(), after=(), vmem=16, cost=(1000, 1000)):
    n_in, n_after = len(ins), len(after)

    def kernel(*refs):
        body(*refs[:n_in], *refs[n_in + n_after :])

    def spec(block, index):
        if block is None:
            return pl.BlockSpec(memory_space=index)
        return pl.BlockSpec(block, index)

    return pl.pallas_call(
        kernel,
        grid=(grid,),
        in_specs=[spec(b, i) for _, b, i in ins] + [pl.BlockSpec(memory_space=pl.ANY)] * n_after,
        out_specs=[spec(b, i) for _, _, b, i in outs],
        out_shape=[jax.ShapeDtypeStruct(s, d) for s, d, _, _ in outs],
        scratch_shapes=list(scratch),
        compiler_params=pltpu.CompilerParams(vmem_limit_bytes=vmem * 2**20),
        cost_estimate=pl.CostEstimate(flops=cost[0], bytes_accessed=cost[1], transcendentals=0),
    )(*[a for a, _, _ in ins], *after)


def in_order(bit, mine, other):
    return jnp.where(bit == 0, mine, other), jnp.where(bit == 0, other, mine)


def hold(cells, *earlier, cost=0):
    return pl.pallas_call(
        lambda *refs: None,
        in_specs=[pl.BlockSpec(memory_space=pl.ANY)] * (1 + len(earlier)),
        out_specs=pl.BlockSpec(memory_space=pl.ANY),
        out_shape=jax.ShapeDtypeStruct(cells.shape, cells.dtype),
        input_output_aliases={0: 0},
        compiler_params=pltpu.CompilerParams(vmem_limit_bytes=2**20),
        cost_estimate=pl.CostEstimate(flops=0, bytes_accessed=cost, transcendentals=0),
    )(cells, *earlier)


def at(*place):
    return lambda *_: place


def border_rows(tile_side):
    half = tile_side // 2
    return (half * half + 15) // 16 * 16


def border_picks(tile_side, side):
    half, rows = tile_side // 2, border_rows(tile_side)
    picks = np.zeros((2, 2 * rows, tile_side * tile_side), np.float32)
    for which in range(2):
        for low in range(2):
            for i in range(half):
                for j in range(half):
                    token = (low * half + i) * tile_side + j + (half if which == 0 else 0)
                    picks[which, low * rows + i * half + j, token] = 1
    left, right = jnp.asarray(picks[0], BF16), jnp.asarray(picks[1], BF16)
    return jnp.where(side == 0, left, right), jnp.where(side == 0, right, left)


def rest_of_first(own, other, pick, heads_weights, hidden_weights, cut, after=()):
    rows, depth = own.shape
    width, hidden = heads_weights[0].shape[1], hidden_weights.shape[1]
    border = pick.shape[0]
    block = width_of(hidden, 384)

    def body(own_ref, other_ref, pick_ref, wq_ref, wk_ref, wv_ref, w_ref, qkv_ref, border_ref, a_ref, b_ref):
        @pl.when(pl.program_id(0) == 0)
        def _():
            taken = dot(pick_ref[...], other_ref[...]).astype(BF16)
            for i, ref in enumerate((wq_ref, wk_ref, wv_ref)):
                qkv_ref[:, i * width : (i + 1) * width] = dot(own_ref[...], ref[...])
            for i, ref in enumerate((wk_ref, wv_ref)):
                border_ref[:, i * width : (i + 1) * width] = dot(taken, ref[...])

        sums = dot(other_ref[...], w_ref[...])
        a_ref[...] = sums[:cut].astype(BF16)
        b_ref[...] = sums[cut:].astype(BF16)

    whole = at(0, 0)
    column = lambda j: (0, j)
    return call(
        body, hidden // block,
        [(own, own.shape, whole), (other, other.shape, whole), (pick, pick.shape, whole)]
        + [(w, w.shape, whole) for w in heads_weights]
        + [(hidden_weights, (depth, block), column)],
        [
            ((rows, 3 * width), F32, (rows, 3 * width), whole),
            ((border, 2 * width), F32, (border, 2 * width), whole),
            ((cut, hidden), BF16, (cut, block), column),
            ((rows - cut, hidden), BF16, (rows - cut, block), column),
        ],
        after=after, vmem=28,
        cost=(
            2 * depth * (rows * 3 * width + border * 2 * width + rows * hidden),
            2 * depth * (2 * rows + 3 * width + hidden) + 4 * (3 * rows + 2 * border) * width + 2 * rows * hidden,
        ),
    )


def norm_heads(mine, got, border_mine, border_got, q_gain, k_gain, after=()):
    rows, heads, head_dim = mine.shape[0], q_gain.shape[0], q_gain.shape[2]
    half_border = border_mine.shape[0] // 2
    sent_own = (rows // 2 + 15) // 16 * 16
    sent = sent_own + half_border

    def body(*refs):
        q, k, v, q2, k2, v2, bk, bv, bk2, bv2, qg, kg = [r[...].astype(F32) for r in refs[:12]]
        queries_ref, own_ref, border_ref, lower_ref, upper_ref = refs[12:]
        queries_ref[...] = rms_gain(q + q2, qg[0]).astype(BF16)
        own = jnp.concatenate([rms_gain(k + k2, kg[0]), v + v2], axis=1).astype(BF16)
        border = jnp.concatenate([rms_gain(bk + bk2, kg[0]), bv + bv2], axis=1).astype(BF16)
        own_ref[...] = own
        border_ref[...] = border
        upper_ref[:sent_own] = own[:sent_own]
        upper_ref[sent_own:] = border[:half_border]
        lower_ref[:sent_own] = own[rows - sent_own :]
        lower_ref[sent_own:] = border[half_border:]

    def third(array, group):
        return (array, (array.shape[0], head_dim), lambda h: (0, group * heads + h))

    def beside(count):
        return ((count, 2 * heads * head_dim), BF16, (count, 2 * head_dim), lambda h: (0, h))

    gain = lambda h: (h, 0, 0)
    return call(
        body, heads,
        [third(mine, g) for g in range(3)] + [third(got, g) for g in range(3)]
        + [third(border_mine, g) for g in range(2)] + [third(border_got, g) for g in range(2)]
        + [(q_gain, (1, 1, head_dim), gain), (k_gain, (1, 1, head_dim), gain)],
        [
            ((rows, heads * head_dim), BF16, (rows, head_dim), lambda h: (0, h)),
            beside(rows), beside(2 * half_border), beside(sent), beside(sent),
        ],
        after=after,
    )


def attend(queries, keys_values, bias, heads, after=()):
    rows, head_dim = queries.shape[0], queries.shape[1] // heads
    spare = bias.shape[1] - sum(k.shape[0] for k in keys_values)

    def body(queries_ref, bias_ref, *refs):
        blocks = [r[...] for r in refs[:-1]]
        if spare:
            blocks.append(jnp.zeros((spare, 2 * head_dim), BF16))
        both = jnp.concatenate(blocks, axis=0)
        keys, values = both[:, :head_dim], both[:, head_dim:]
        scores = lax.dot_general(queries_ref[...], keys, (((1,), (1,)), ((), ())), preferred_element_type=F32)
        scores = scores * head_dim ** (-0.5) + bias_ref[...]
        numerators = jnp.exp(scores - jnp.max(scores, axis=-1, keepdims=True))
        total = jnp.sum(numerators, axis=-1, keepdims=True)
        refs[-1][...] = (dot(numerators.astype(BF16), values) / total).astype(BF16)

    head = lambda h: (0, h)
    return call(
        body, heads,
        [(queries, (rows, head_dim), head), (bias, bias.shape, at(0, 0))]
        + [(k, (k.shape[0], 2 * head_dim), head) for k in keys_values],
        [((rows, heads * head_dim), BF16, (rows, head_dim), head)],
        after=after,
    )[0]


def paired_plan(
    tokens, mod_shift, mod_scale, mod_gate, w_qkv, w_mlp_in, q_gain, k_gain, w_attn_out, w_mlp_out
):
    tok_rows, model_width = tokens.shape
    half_width, hidden = w_mlp_in.shape
    heads, head_dim = q_gain.shape
    width = heads * head_dim
    side = lax.axis_index("sx")
    part = lax.axis_index("tp")
    core, far = part % 2, part // 2
    mid = hidden // 2
    block = half_width // 2
    own_pick, other_pick = border_picks(TILE, side)
    q_gain, k_gain = q_gain[:, None, :], k_gain[:, None, :]

    piece_width = half_width // 2
    other_first = (1 - side) * half_width + core * piece_width
    sent = lax.dynamic_slice_in_dim(tokens, other_first, piece_width, 1)
    piece = swap(sent, "sx", 1)
    cells = tokens.astype(F32)
    mean = jnp.mean(cells, axis=-1, keepdims=True)
    centered = cells - mean
    scaling = lax.rsqrt(jnp.mean(centered * centered, axis=-1, keepdims=True) + 1e-06)
    stats = jnp.concatenate([mean, scaling], axis=1)
    other_stats = swap(stats, "sx", 1)
    first = hold(side[None], sent)[0] * half_width
    gain_part = 1.0 + lax.dynamic_slice_in_dim(mod_scale, first, half_width, 0)
    shift_part = lax.dynamic_slice_in_dim(mod_shift, first, half_width, 0)

    def modulate(cells, pair):
        cells = (cells.astype(F32) - pair[:, :1]) * pair[:, 1:]
        return (cells * gain_part + shift_part).astype(BF16)

    w_queries, w_keys, w_values = [w_qkv[:, group] for group in range(3)]

    def heads_of(cells):
        return jnp.concatenate([dot(cells, w) for w in (w_queries, w_keys, w_values)], axis=1)

    def border_of(pick, cells):
        cells = dot(pick, cells).astype(BF16)
        return jnp.concatenate([dot(cells, w) for w in (w_keys, w_values)], axis=1)

    own = modulate(lax.dynamic_slice_in_dim(tokens, first, half_width, 1), stats)
    own_border = border_of(own_pick, own).astype(BF16)
    got_border = swap(own_border, "sx", 1)
    own = hold(own, own_border)
    own_hidden = dot(own, w_mlp_in).astype(BF16)
    piece = hold(piece, own_hidden)
    near = swap(piece, "tp", 1)
    other = modulate(jnp.concatenate(in_order(core, piece, near), axis=1), other_stats)
    other_qkv = heads_of(other).astype(BF16)
    got_qkv = swap(other_qkv, "sx", 1)
    own_hidden = hold(own_hidden, other_qkv)
    got_own = swap(own_hidden, "sx", 1)
    cut = tok_rows // 2
    own_qkv, other_border, other_a, other_b = rest_of_first(
        own, other, other_pick, (w_queries, w_keys, w_values), w_mlp_in, cut, [other_qkv, got_border]
    )

    queries, own_kv, border_kv, lower, upper = norm_heads(
        own_qkv, got_qkv, other_border, got_border, q_gain, k_gain, [other_a]
    )
    above = shift(lower, "sy", 1)
    below = shift(upper, "sy", -1)

    sent_mlp, kept_mlp, sent_attn, kept_attn = (
        lax.dynamic_slice_in_dim(w, first * block, block, 1)
        for w in (w_mlp_out, w_attn_out)
        for first in (1 - core, core)
    )

    def activate(mine, got, *earlier):
        got = hold(got, *earlier)
        return hold(jax.nn.gelu(mine.astype(F32) + got.astype(F32), approximate=True).astype(BF16))

    row = lax.axis_index("sy")
    extra = tok_rows // 2
    half_border, taken = border_kv.shape[0] // 2, (TILE // 2) ** 2
    sent_own = lower.shape[0] - half_border
    inside = np.zeros(((own_kv.shape[0] + 2 * half_border + 2 * lower.shape[0] + 127) // 128 * 128,), np.int32)
    inside[:tok_rows] = 1
    for start in (tok_rows, tok_rows + half_border):
        inside[start : start + taken] = 1
    start = tok_rows + 2 * half_border
    inside[start + sent_own - extra : start + sent_own] = 2
    inside[start + sent_own : start + sent_own + taken] = 2
    start += lower.shape[0]
    inside[start : start + extra] = 3
    inside[start + sent_own : start + sent_own + taken] = 3
    there = (inside == 1) | ((inside == 2) & (row > 0)) | ((inside == 3) & (row < lax.axis_size("sy") - 1))
    bias = jnp.where(there, 0.0, -jnp.inf).astype(F32)[None]
    attended = attend(queries, [own_kv, border_kv, above, below], bias, heads)
    got_attended = swap(attended, "sx", 1)
    got_other_a = swap(other_a, "sx", 1)
    other_active = activate(jnp.concatenate([other_a, other_b], axis=0), got_own, attended)
    other_sent, other_kept = dot(other_active, sent_mlp), dot(other_active, kept_mlp)
    got_other_a = swap(other_a, "sx", 1)
    got_other_b = swap(hold(other_b, other_sent), "sx", 1)

    def own_part(begin, end, got, *earlier):
        active, heads_part = activate(own_hidden[begin:end], got, *earlier), attended[begin:end]
        return (
            (dot(active, sent_mlp) + dot(heads_part, sent_attn)).astype(BF16),
            dot(active, kept_mlp) + dot(heads_part, kept_attn),
        )

    got_attended = hold(got_attended, other_sent, other_kept, got_other_a)
    other_sent = (other_sent + dot(got_attended, sent_attn)).astype(BF16)
    other_kept = other_kept + dot(got_attended, kept_attn)
    other_come = swap(other_sent, "tp", 1)
    own_sent_a, own_kept_a = own_part(0, cut, got_other_a, other_sent, other_kept)

    def rows_of(half):
        kept = jnp.where(half == 0, other_kept[:cut], other_kept[cut:])
        return kept + jnp.where(half == 0, other_come[:cut], other_come[cut:]).astype(F32)

    passed = rows_of(1 - far).astype(BF16)
    passed = hold(swap(passed, "tp", 2), own_sent_a, own_kept_a)
    crossing = (rows_of(far) + passed.astype(F32)).astype(BF16)
    got = swap(crossing, "sx", 1)
    own_sum_a = own_kept_a + swap(own_sent_a, "tp", 1).astype(F32)
    come_a = swap(own_sum_a.astype(BF16), "tp", 2)
    own_sent_b, own_kept_b = own_part(cut, tok_rows, got_other_b, crossing)
    own_sum_b = hold(own_kept_b, got, come_a, cost=EARLY) + swap(own_sent_b, "tp", 1).astype(F32)

    home = far == side
    come_b = swap(jnp.where(home, got, own_sum_b.astype(BF16)), "tp", 2)
    wide = got.astype(F32)
    known = jnp.concatenate(
        [
            jnp.where(home, own_sum_a + come_a.astype(F32), jnp.where(far == 0, wide, 0.0)),
            jnp.where(home, own_sum_b, jnp.where(far == 0, 0.0, wide)),
        ],
        axis=0,
    )
    first_col = hold(part[None], own_sent_a)[0] * block
    gate_part = lax.dynamic_slice_in_dim(mod_gate, first_col, block, 0)
    residual_part = lax.dynamic_slice_in_dim(tokens, first_col, block, 1).astype(F32)
    known = hold(residual_part + gate_part * known)
    late_first = jnp.where(home, 1, 1 - far) * cut
    place = lax.broadcasted_iota(jnp.int32, (tok_rows, 1), 0)
    late = (place >= late_first) & (place < late_first + cut)
    late_part = jnp.concatenate([come_b, come_b], axis=0).astype(F32)
    return (known + jnp.where(late, gate_part * late_part, 0.0)).astype(BF16)


def shards(*arrays):
    if lax.axis_size("sx") == 2 and lax.axis_size("tp") == 4:
        return paired_plan(*arrays)
    return gathered_plan(*arrays)


def solution(mesh):
    placed = (
        P(("sy", "sx"), None),
        P(),
        P(),
        P(),
        P("sx", None, "tp"),
        P("sx", "tp"),
        P("tp", None),
        P("tp", None),
        P("tp", "sx"),
        P("tp", "sx"),
    )
    return jax.shard_map(
        shards, mesh=mesh, in_specs=placed, out_specs=P(("sy", "sx"), "tp"), check_vma=False
    )
```

```python
import jax
import jax.numpy as jnp
import numpy as np
from jax import lax
from jax.experimental import pallas as pl
from jax.experimental.pallas import tpu as pltpu
from jax.sharding import PartitionSpec as P

TILE = 20


def with_halo(cells, sides, width):
    for axis, dim in sides:
        count = lax.axis_size(axis)
        ends = count - 1
        head = lax.slice_in_dim(cells, 0, width, axis=dim)
        tail = lax.slice_in_dim(cells, cells.shape[dim] - width, cells.shape[dim], axis=dim)
        cells = jnp.concatenate(
            [
                lax.ppermute(tail, axis, [(i, (i + 1) % count) for i in range(ends)]),
                cells,
                lax.ppermute(head, axis, [((i + 1) % count, i) for i in range(ends)]),
            ],
            axis=dim,
        )
    return cells


def layer_norm(vector):
    centered = vector - jnp.mean(vector, axis=-1, keepdims=True)
    variance = jnp.mean(centered * centered, axis=-1, keepdims=True)
    return centered * lax.rsqrt(variance + 1e-06)


def rms_gain(vector, scaling):
    mean_square = jnp.mean(vector * vector, axis=-1, keepdims=True)
    return vector * lax.rsqrt(mean_square + 1e-06) * scaling


def gathered_plan(
    tokens, mod_shift, mod_scale, mod_gate, w_qkv, w_mlp_in, q_gain, k_gain, w_attn_out, w_mlp_out
):
    tok_rows, model_width = tokens.shape
    tile_side = TILE
    half_side = TILE // 2
    inputs = tokens.astype(jnp.float32)
    modded = (layer_norm(inputs) * (1.0 + mod_scale) + mod_shift).astype(jnp.bfloat16)
    local_heads, head_dim = q_gain.shape
    local_width = local_heads * head_dim
    pieces = (
        lax.all_gather(w_qkv, "sx", axis=0, tiled=True),
        lax.all_gather(w_mlp_in, "sx", axis=0, tiled=True),
    )
    piece_rows = pieces[0].shape[0]
    qkv_sum = jnp.dot(
        modded, pieces[0].reshape(piece_rows, 3 * local_width), preferred_element_type=jnp.float32
    )
    mlp_sum = jnp.dot(modded, pieces[1], preferred_element_type=jnp.float32)
    qkv_parts = qkv_sum.reshape(tok_rows, 3, local_heads, head_dim)
    queries = rms_gain(qkv_parts[:, 0], q_gain).astype(jnp.bfloat16)
    key_rows = rms_gain(qkv_parts[:, 1], k_gain).astype(jnp.bfloat16)
    value_rows = qkv_parts[:, 2].astype(jnp.bfloat16)
    key_value = jnp.concatenate(
        [key_rows.reshape(tok_rows, local_width), value_rows.reshape(tok_rows, local_width)], axis=1
    )
    key_value = key_value.reshape(tile_side, tile_side, 2 * local_width)
    extended = with_halo(key_value, (("sy", 0), ("sx", 1)), half_side)
    window = extended.reshape(4 * tok_rows, 2 * local_width)
    window_keys = window[:, :local_width].reshape(4 * tok_rows, local_heads, head_dim)
    window_values = window[:, local_width:].reshape(4 * tok_rows, local_heads, head_dim)
    offsets = jnp.arange(2 * tile_side, dtype=jnp.int32)
    row_pos = lax.axis_index("sy") * tile_side - half_side + offsets
    col_pos = lax.axis_index("sx") * tile_side - half_side + offsets
    row_ok = (row_pos >= 0) & (row_pos < tile_side * lax.axis_size("sy"))
    col_ok = (col_pos >= 0) & (col_pos < tile_side * lax.axis_size("sx"))
    in_grid = (row_ok[:, None] & col_ok[None, :]).reshape(4 * tok_rows)
    scores = jnp.einsum(
        "qhd,khd->hqk", queries, window_keys, preferred_element_type=jnp.float32
    ) * head_dim ** (-0.5)
    scores = jnp.where(in_grid[None, None, :], scores, -jnp.inf)
    row_max = jnp.max(scores, axis=-1, keepdims=True)
    numerators = jnp.exp(scores - row_max)
    weights = (numerators / jnp.sum(numerators, axis=-1, keepdims=True)).astype(jnp.bfloat16)
    attended = jnp.einsum(
        "hqk,khd->qhd", weights, window_values, preferred_element_type=jnp.float32
    )
    attended = attended.astype(jnp.bfloat16).reshape(tok_rows, local_width)
    activated = jax.nn.gelu(mlp_sum, approximate=True).astype(jnp.bfloat16)
    pieces = (
        lax.all_gather(w_attn_out, "sx", axis=1, tiled=True),
        lax.all_gather(w_mlp_out, "sx", axis=1, tiled=True),
    )
    product_term = jnp.dot(attended, pieces[0], preferred_element_type=jnp.float32)
    product_term = product_term + jnp.dot(activated, pieces[1], preferred_element_type=jnp.float32)
    reduced = lax.psum_scatter(
        product_term.astype(jnp.bfloat16), "tp", scatter_dimension=1, tiled=True
    ).astype(jnp.float32)
    block_width = model_width // lax.axis_size("tp")
    first_col = lax.axis_index("tp") * block_width
    residual_part = lax.dynamic_slice_in_dim(inputs, first_col, block_width, 1)
    gate_part = lax.dynamic_slice_in_dim(mod_gate, first_col, block_width, 0)
    return (residual_part + gate_part * reduced).astype(jnp.bfloat16)


def swap(cells, axis, bit):
    count = lax.axis_size(axis)
    return lax.ppermute(cells, axis, [(i, i ^ bit) for i in range(count)])


def shift(cells, axis, step):
    count = lax.axis_size(axis)
    return lax.ppermute(
        cells, axis, [(i, i + step) for i in range(count) if 0 <= i + step < count]
    )


def dot(left, right):
    return jnp.dot(left, right, preferred_element_type=jnp.float32)


BF16, F32 = jnp.bfloat16, jnp.float32
LANES = 128
EARLY = 20_000_000


def width_of(total, most):
    return max(w for w in range(LANES, most + 1, LANES) if total % w == 0)


def call(body, grid, ins, outs, scratch=(), after=(), vmem=16, cost=(1000, 1000)):
    n_in, n_after = len(ins), len(after)

    def kernel(*refs):
        body(*refs[:n_in], *refs[n_in + n_after :])

    def spec(block, index):
        if block is None:
            return pl.BlockSpec(memory_space=index)
        return pl.BlockSpec(block, index)

    return pl.pallas_call(
        kernel,
        grid=(grid,),
        in_specs=[spec(b, i) for _, b, i in ins] + [pl.BlockSpec(memory_space=pl.ANY)] * n_after,
        out_specs=[spec(b, i) for _, _, b, i in outs],
        out_shape=[jax.ShapeDtypeStruct(s, d) for s, d, _, _ in outs],
        scratch_shapes=list(scratch),
        compiler_params=pltpu.CompilerParams(vmem_limit_bytes=vmem * 2**20),
        cost_estimate=pl.CostEstimate(flops=cost[0], bytes_accessed=cost[1], transcendentals=0),
    )(*[a for a, _, _ in ins], *after)


def in_order(bit, mine, other):
    return jnp.where(bit == 0, mine, other), jnp.where(bit == 0, other, mine)


def hold(cells, *earlier, cost=0):
    return pl.pallas_call(
        lambda *refs: None,
        in_specs=[pl.BlockSpec(memory_space=pl.ANY)] * (1 + len(earlier)),
        out_specs=pl.BlockSpec(memory_space=pl.ANY),
        out_shape=jax.ShapeDtypeStruct(cells.shape, cells.dtype),
        input_output_aliases={0: 0},
        compiler_params=pltpu.CompilerParams(vmem_limit_bytes=2**20),
        cost_estimate=pl.CostEstimate(flops=0, bytes_accessed=cost, transcendentals=0),
    )(cells, *earlier)


def at(*place):
    return lambda *_: place


def border_rows(tile_side):
    half = tile_side // 2
    return (half * half + 15) // 16 * 16


def border_picks(tile_side, side):
    half, rows = tile_side // 2, border_rows(tile_side)
    picks = np.zeros((2, 2 * rows, tile_side * tile_side), np.float32)
    for which in range(2):
        for low in range(2):
            for i in range(half):
                for j in range(half):
                    token = (low * half + i) * tile_side + j + (half if which == 0 else 0)
                    picks[which, low * rows + i * half + j, token] = 1
    left, right = jnp.asarray(picks[0], BF16), jnp.asarray(picks[1], BF16)
    return jnp.where(side == 0, left, right), jnp.where(side == 0, right, left)


def rest_of_first(own, other, pick, heads_weights, hidden_weights, cut, after=()):
    rows, depth = own.shape
    width, hidden = heads_weights[0].shape[1], hidden_weights.shape[1]
    border = pick.shape[0]
    block = width_of(hidden, 384)

    def body(own_ref, other_ref, pick_ref, wq_ref, wk_ref, wv_ref, w_ref, qkv_ref, border_ref, a_ref, b_ref):
        @pl.when(pl.program_id(0) == 0)
        def _():
            taken = dot(pick_ref[...], other_ref[...]).astype(BF16)
            for i, ref in enumerate((wq_ref, wk_ref, wv_ref)):
                qkv_ref[:, i * width : (i + 1) * width] = dot(own_ref[...], ref[...])
            for i, ref in enumerate((wk_ref, wv_ref)):
                border_ref[:, i * width : (i + 1) * width] = dot(taken, ref[...])

        sums = dot(other_ref[...], w_ref[...])
        a_ref[...] = sums[:cut].astype(BF16)
        b_ref[...] = sums[cut:].astype(BF16)

    whole = at(0, 0)
    column = lambda j: (0, j)
    return call(
        body, hidden // block,
        [(own, own.shape, whole), (other, other.shape, whole), (pick, pick.shape, whole)]
        + [(w, w.shape, whole) for w in heads_weights]
        + [(hidden_weights, (depth, block), column)],
        [
            ((rows, 3 * width), F32, (rows, 3 * width), whole),
            ((border, 2 * width), F32, (border, 2 * width), whole),
            ((cut, hidden), BF16, (cut, block), column),
            ((rows - cut, hidden), BF16, (rows - cut, block), column),
        ],
        after=after, vmem=28,
        cost=(
            2 * depth * (rows * 3 * width + border * 2 * width + rows * hidden),
            2 * depth * (2 * rows + 3 * width + hidden) + 4 * (3 * rows + 2 * border) * width + 2 * rows * hidden,
        ),
    )


def norm_heads(mine, got, border_mine, border_got, q_gain, k_gain, after=()):
    rows, heads, head_dim = mine.shape[0], q_gain.shape[0], q_gain.shape[2]
    half_border = border_mine.shape[0] // 2
    sent_own = (rows // 2 + 15) // 16 * 16
    sent = sent_own + half_border

    def body(*refs):
        q, k, v, q2, k2, v2, bk, bv, bk2, bv2, qg, kg = [r[...].astype(F32) for r in refs[:12]]
        queries_ref, own_ref, border_ref, lower_ref, upper_ref = refs[12:]
        queries_ref[...] = rms_gain(q + q2, qg[0]).astype(BF16)
        own = jnp.concatenate([rms_gain(k + k2, kg[0]), v + v2], axis=1).astype(BF16)
        border = jnp.concatenate([rms_gain(bk + bk2, kg[0]), bv + bv2], axis=1).astype(BF16)
        own_ref[...] = own
        border_ref[...] = border
        upper_ref[:sent_own] = own[:sent_own]
        upper_ref[sent_own:] = border[:half_border]
        lower_ref[:sent_own] = own[rows - sent_own :]
        lower_ref[sent_own:] = border[half_border:]

    def third(array, group):
        return (array, (array.shape[0], head_dim), lambda h: (0, group * heads + h))

    def beside(count):
        return ((count, 2 * heads * head_dim), BF16, (count, 2 * head_dim), lambda h: (0, h))

    gain = lambda h: (h, 0, 0)
    return call(
        body, heads,
        [third(mine, g) for g in range(3)] + [third(got, g) for g in range(3)]
        + [third(border_mine, g) for g in range(2)] + [third(border_got, g) for g in range(2)]
        + [(q_gain, (1, 1, head_dim), gain), (k_gain, (1, 1, head_dim), gain)],
        [
            ((rows, heads * head_dim), BF16, (rows, head_dim), lambda h: (0, h)),
            beside(rows), beside(2 * half_border), beside(sent), beside(sent),
        ],
        after=after,
    )


def attend(queries, keys_values, bias, heads, after=()):
    rows, head_dim = queries.shape[0], queries.shape[1] // heads
    spare = bias.shape[1] - sum(k.shape[0] for k in keys_values)

    def body(queries_ref, bias_ref, *refs):
        blocks = [r[...] for r in refs[:-1]]
        if spare:
            blocks.append(jnp.zeros((spare, 2 * head_dim), BF16))
        both = jnp.concatenate(blocks, axis=0)
        keys, values = both[:, :head_dim], both[:, head_dim:]
        scores = lax.dot_general(queries_ref[...], keys, (((1,), (1,)), ((), ())), preferred_element_type=F32)
        scores = scores * head_dim ** (-0.5) + bias_ref[...]
        numerators = jnp.exp(scores - jnp.max(scores, axis=-1, keepdims=True))
        total = jnp.sum(numerators, axis=-1, keepdims=True)
        refs[-1][...] = (dot(numerators.astype(BF16), values) / total).astype(BF16)

    head = lambda h: (0, h)
    return call(
        body, heads,
        [(queries, (rows, head_dim), head), (bias, bias.shape, at(0, 0))]
        + [(k, (k.shape[0], 2 * head_dim), head) for k in keys_values],
        [((rows, heads * head_dim), BF16, (rows, head_dim), head)],
        after=after,
    )[0]


def paired_plan(
    tokens, mod_shift, mod_scale, mod_gate, w_qkv, w_mlp_in, q_gain, k_gain, w_attn_out, w_mlp_out
):
    tok_rows, model_width = tokens.shape
    half_width, hidden = w_mlp_in.shape
    heads, head_dim = q_gain.shape
    width = heads * head_dim
    side = lax.axis_index("sx")
    part = lax.axis_index("tp")
    core, far = part % 2, part // 2
    mid = hidden // 2
    block = half_width // 2
    own_pick, other_pick = border_picks(TILE, side)
    q_gain, k_gain = q_gain[:, None, :], k_gain[:, None, :]

    quarter = half_width // 4
    other_first = (1 - side) * half_width + part * quarter
    sent = lax.dynamic_slice_in_dim(tokens, other_first, quarter, 1)
    piece = swap(sent, "sx", 1)
    cells = tokens.astype(F32)
    mean = jnp.mean(cells, axis=-1, keepdims=True)
    centered = cells - mean
    scaling = lax.rsqrt(jnp.mean(centered * centered, axis=-1, keepdims=True) + 1e-06)
    stats = jnp.concatenate([mean, scaling], axis=1)
    other_stats = swap(stats, "sx", 1)
    first = hold(side[None], sent)[0] * half_width
    gain_part = 1.0 + lax.dynamic_slice_in_dim(mod_scale, first, half_width, 0)
    shift_part = lax.dynamic_slice_in_dim(mod_shift, first, half_width, 0)

    def modulate(cells, pair):
        cells = (cells.astype(F32) - pair[:, :1]) * pair[:, 1:]
        return (cells * gain_part + shift_part).astype(BF16)

    w_queries, w_keys, w_values = [w_qkv[:, group] for group in range(3)]

    def heads_of(cells):
        return jnp.concatenate([dot(cells, w) for w in (w_queries, w_keys, w_values)], axis=1)

    def border_of(pick, cells):
        cells = dot(pick, cells).astype(BF16)
        return jnp.concatenate([dot(cells, w) for w in (w_keys, w_values)], axis=1)

    own = modulate(lax.dynamic_slice_in_dim(tokens, first, half_width, 1), stats)
    own_border = border_of(own_pick, own).astype(BF16)
    got_border = swap(own_border, "sx", 1)
    own = hold(own, own_border)
    piece = hold(piece, own_border)
    pieces = in_order(far, piece, swap(piece, "tp", 2))
    first_part = width_of(hidden // 3, hidden)
    own_first = dot(own, w_mlp_in[:, :first_part]).astype(BF16)
    own = hold(own, own_first)
    own_rest = dot(own, w_mlp_in[:, first_part:]).astype(BF16)
    got_first = swap(own_first, "sx", 1)
    pieces = hold(jnp.concatenate(pieces, axis=1), got_border, own_first)
    even, odd = in_order(core, pieces, swap(pieces, "tp", 1))
    other = jnp.concatenate([even[:, :quarter], odd[:, :quarter], even[:, quarter:], odd[:, quarter:]], axis=1)
    other = modulate(other, other_stats)
    other_qkv = heads_of(other).astype(BF16)
    got_qkv = swap(other_qkv, "sx", 1)
    own_rest = hold(own_rest, other_qkv)
    got_rest = swap(own_rest, "sx", 1)
    cut = tok_rows // 2
    own_qkv, other_border, other_a, other_b = rest_of_first(
        own, other, other_pick, (w_queries, w_keys, w_values), w_mlp_in, cut, [other_qkv, got_first]
    )

    queries, own_kv, border_kv, lower, upper = norm_heads(
        own_qkv, got_qkv, other_border, got_border, q_gain, k_gain, [other_a]
    )
    above = shift(lower, "sy", 1)
    below = shift(upper, "sy", -1)

    sent_mlp, kept_mlp, sent_attn, kept_attn = (
        lax.dynamic_slice_in_dim(w, first * block, block, 1)
        for w in (w_mlp_out, w_attn_out)
        for first in (1 - core, core)
    )

    def activate(mine, got, *earlier):
        got = hold(got, *earlier) if earlier else got
        return hold(jax.nn.gelu(mine.astype(F32) + got.astype(F32), approximate=True).astype(BF16))

    row = lax.axis_index("sy")
    extra = tok_rows // 2
    half_border, taken = border_kv.shape[0] // 2, (TILE // 2) ** 2
    sent_own = lower.shape[0] - half_border
    inside = np.zeros(((own_kv.shape[0] + 2 * half_border + 2 * lower.shape[0] + 127) // 128 * 128,), np.int32)
    inside[:tok_rows] = 1
    for start in (tok_rows, tok_rows + half_border):
        inside[start : start + taken] = 1
    start = tok_rows + 2 * half_border
    inside[start + sent_own - extra : start + sent_own] = 2
    inside[start + sent_own : start + sent_own + taken] = 2
    start += lower.shape[0]
    inside[start : start + extra] = 3
    inside[start + sent_own : start + sent_own + taken] = 3
    there = (inside == 1) | ((inside == 2) & (row > 0)) | ((inside == 3) & (row < lax.axis_size("sy") - 1))
    bias = jnp.where(there, 0.0, -jnp.inf).astype(F32)[None]
    attended = attend(queries, [own_kv, border_kv, above, below], bias, heads)
    got_attended = swap(attended, "sx", 1)
    got_other_a = swap(other_a, "sx", 1)
    got_own = jnp.concatenate([got_first, hold(got_rest, attended)], axis=1)
    own_hidden = jnp.concatenate([own_first, own_rest], axis=1)
    other_active = activate(jnp.concatenate([other_a, other_b], axis=0), got_own)
    other_sent, other_kept = dot(other_active, sent_mlp), dot(other_active, kept_mlp)
    got_other_b = swap(hold(other_b, other_sent), "sx", 1)

    def own_part(begin, end, got, *earlier):
        active, heads_part = activate(own_hidden[begin:end], got, *earlier), attended[begin:end]
        return (
            (dot(active, sent_mlp) + dot(heads_part, sent_attn)).astype(BF16),
            dot(active, kept_mlp) + dot(heads_part, kept_attn),
        )

    got_attended = hold(got_attended, other_sent, other_kept, got_other_a)
    other_sent = (other_sent + dot(got_attended, sent_attn)).astype(BF16)
    other_kept = other_kept + dot(got_attended, kept_attn)
    other_come = swap(other_sent, "tp", 1)
    own_sent_a, own_kept_a = own_part(0, cut, got_other_a, other_sent, other_kept)

    def rows_of(half):
        kept = jnp.where(half == 0, other_kept[:cut], other_kept[cut:])
        return kept + jnp.where(half == 0, other_come[:cut], other_come[cut:]).astype(F32)

    passed = rows_of(1 - far).astype(BF16)
    passed = hold(swap(passed, "tp", 2), own_sent_a, own_kept_a)
    crossing = (rows_of(far) + passed.astype(F32)).astype(BF16)
    got = swap(crossing, "sx", 1)
    own_sum_a = own_kept_a + swap(own_sent_a, "tp", 1).astype(F32)
    come_a = swap(own_sum_a.astype(BF16), "tp", 2)
    own_sent_b, own_kept_b = own_part(cut, tok_rows, got_other_b, crossing)
    own_sum_b = hold(own_kept_b, got, come_a, cost=EARLY) + swap(own_sent_b, "tp", 1).astype(F32)

    home = far == side
    come_b = swap(jnp.where(home, got, own_sum_b.astype(BF16)), "tp", 2)
    wide = got.astype(F32)
    known = jnp.concatenate(
        [
            jnp.where(home, own_sum_a + come_a.astype(F32), jnp.where(far == 0, wide, 0.0)),
            jnp.where(home, own_sum_b, jnp.where(far == 0, 0.0, wide)),
        ],
        axis=0,
    )
    first_col = hold(part[None], own_sent_a)[0] * block
    gate_part = lax.dynamic_slice_in_dim(mod_gate, first_col, block, 0)
    residual_part = lax.dynamic_slice_in_dim(tokens, first_col, block, 1).astype(F32)
    known = hold(residual_part + gate_part * known)
    late_first = jnp.where(home, 1, 1 - far) * cut
    place = lax.broadcasted_iota(jnp.int32, (tok_rows, 1), 0)
    late = (place >= late_first) & (place < late_first + cut)
    late_part = jnp.concatenate([come_b, come_b], axis=0).astype(F32)
    return (known + jnp.where(late, gate_part * late_part, 0.0)).astype(BF16)


def shards(*arrays):
    local_heads = arrays[6].shape[0]
    if lax.axis_size("sx") == 2 and lax.axis_size("tp") == 4 and local_heads % 2 and local_heads > 1:
        return paired_plan(*arrays)
    return gathered_plan(*arrays)


def solution(mesh):
    placed = (
        P(("sy", "sx"), None),
        P(),
        P(),
        P(),
        P("sx", None, "tp"),
        P("sx", "tp"),
        P("tp", None),
        P("tp", None),
        P("tp", "sx"),
        P("tp", "sx"),
    )
    return jax.shard_map(
        shards, mesh=mesh, in_specs=placed, out_specs=P(("sy", "sx"), "tp"), check_vma=False
    )
```

```python
import jax
import jax.numpy as jnp
import numpy as np
from jax import lax
from jax.experimental import pallas as pl
from jax.experimental.pallas import tpu as pltpu
from jax.sharding import PartitionSpec as P

TILE = 20


def with_halo(cells, sides, width):
    for axis, dim in sides:
        count = lax.axis_size(axis)
        ends = count - 1
        head = lax.slice_in_dim(cells, 0, width, axis=dim)
        tail = lax.slice_in_dim(cells, cells.shape[dim] - width, cells.shape[dim], axis=dim)
        cells = jnp.concatenate(
            [
                lax.ppermute(tail, axis, [(i, (i + 1) % count) for i in range(ends)]),
                cells,
                lax.ppermute(head, axis, [((i + 1) % count, i) for i in range(ends)]),
            ],
            axis=dim,
        )
    return cells


def layer_norm(vector):
    centered = vector - jnp.mean(vector, axis=-1, keepdims=True)
    variance = jnp.mean(centered * centered, axis=-1, keepdims=True)
    return centered * lax.rsqrt(variance + 1e-06)


def rms_gain(vector, scaling):
    mean_square = jnp.mean(vector * vector, axis=-1, keepdims=True)
    return vector * lax.rsqrt(mean_square + 1e-06) * scaling


def gathered_plan(
    tokens, mod_shift, mod_scale, mod_gate, w_qkv, w_mlp_in, q_gain, k_gain, w_attn_out, w_mlp_out
):
    tok_rows, model_width = tokens.shape
    tile_side = TILE
    half_side = TILE // 2
    inputs = tokens.astype(jnp.float32)
    modded = (layer_norm(inputs) * (1.0 + mod_scale) + mod_shift).astype(jnp.bfloat16)
    local_heads, head_dim = q_gain.shape
    local_width = local_heads * head_dim
    pieces = (
        lax.all_gather(w_qkv, "sx", axis=0, tiled=True),
        lax.all_gather(w_mlp_in, "sx", axis=0, tiled=True),
    )
    piece_rows = pieces[0].shape[0]
    qkv_sum = jnp.dot(
        modded, pieces[0].reshape(piece_rows, 3 * local_width), preferred_element_type=jnp.float32
    )
    mlp_sum = jnp.dot(modded, pieces[1], preferred_element_type=jnp.float32)
    qkv_parts = qkv_sum.reshape(tok_rows, 3, local_heads, head_dim)
    queries = rms_gain(qkv_parts[:, 0], q_gain).astype(jnp.bfloat16)
    key_rows = rms_gain(qkv_parts[:, 1], k_gain).astype(jnp.bfloat16)
    value_rows = qkv_parts[:, 2].astype(jnp.bfloat16)
    key_value = jnp.concatenate(
        [key_rows.reshape(tok_rows, local_width), value_rows.reshape(tok_rows, local_width)], axis=1
    )
    key_value = key_value.reshape(tile_side, tile_side, 2 * local_width)
    extended = with_halo(key_value, (("sy", 0), ("sx", 1)), half_side)
    window = extended.reshape(4 * tok_rows, 2 * local_width)
    window_keys = window[:, :local_width].reshape(4 * tok_rows, local_heads, head_dim)
    window_values = window[:, local_width:].reshape(4 * tok_rows, local_heads, head_dim)
    offsets = jnp.arange(2 * tile_side, dtype=jnp.int32)
    row_pos = lax.axis_index("sy") * tile_side - half_side + offsets
    col_pos = lax.axis_index("sx") * tile_side - half_side + offsets
    row_ok = (row_pos >= 0) & (row_pos < tile_side * lax.axis_size("sy"))
    col_ok = (col_pos >= 0) & (col_pos < tile_side * lax.axis_size("sx"))
    in_grid = (row_ok[:, None] & col_ok[None, :]).reshape(4 * tok_rows)
    scores = jnp.einsum(
        "qhd,khd->hqk", queries, window_keys, preferred_element_type=jnp.float32
    ) * head_dim ** (-0.5)
    scores = jnp.where(in_grid[None, None, :], scores, -jnp.inf)
    row_max = jnp.max(scores, axis=-1, keepdims=True)
    numerators = jnp.exp(scores - row_max)
    weights = (numerators / jnp.sum(numerators, axis=-1, keepdims=True)).astype(jnp.bfloat16)
    attended = jnp.einsum(
        "hqk,khd->qhd", weights, window_values, preferred_element_type=jnp.float32
    )
    attended = attended.astype(jnp.bfloat16).reshape(tok_rows, local_width)
    activated = jax.nn.gelu(mlp_sum, approximate=True).astype(jnp.bfloat16)
    pieces = (
        lax.all_gather(w_attn_out, "sx", axis=1, tiled=True),
        lax.all_gather(w_mlp_out, "sx", axis=1, tiled=True),
    )
    product_term = jnp.dot(attended, pieces[0], preferred_element_type=jnp.float32)
    product_term = product_term + jnp.dot(activated, pieces[1], preferred_element_type=jnp.float32)
    reduced = lax.psum_scatter(
        product_term.astype(jnp.bfloat16), "tp", scatter_dimension=1, tiled=True
    ).astype(jnp.float32)
    block_width = model_width // lax.axis_size("tp")
    first_col = lax.axis_index("tp") * block_width
    residual_part = lax.dynamic_slice_in_dim(inputs, first_col, block_width, 1)
    gate_part = lax.dynamic_slice_in_dim(mod_gate, first_col, block_width, 0)
    return (residual_part + gate_part * reduced).astype(jnp.bfloat16)


def swap(cells, axis, bit):
    count = lax.axis_size(axis)
    return lax.ppermute(cells, axis, [(i, i ^ bit) for i in range(count)])


def shift(cells, axis, step):
    count = lax.axis_size(axis)
    return lax.ppermute(
        cells, axis, [(i, i + step) for i in range(count) if 0 <= i + step < count]
    )


def dot(left, right):
    return jnp.dot(left, right, preferred_element_type=jnp.float32)


BF16, F32 = jnp.bfloat16, jnp.float32
LANES = 128
EARLY = 20_000_000
VMEM = 56
REST_VMEM = 40
POST_VMEM = 40
ROWS = 80


def width_of(total, most):
    return max(w for w in range(LANES, most + 1, LANES) if total % w == 0)


def call(body, grid, ins, outs, scratch=(), after=(), vmem=16, cost=(1000, 1000)):
    n_in, n_after = len(ins), len(after)

    def kernel(*refs):
        body(*refs[:n_in], *refs[n_in + n_after :])

    def spec(block, index):
        if block is None:
            return pl.BlockSpec(memory_space=index)
        return pl.BlockSpec(block, index)

    return pl.pallas_call(
        kernel,
        grid=(grid,),
        in_specs=[spec(b, i) for _, b, i in ins] + [pl.BlockSpec(memory_space=pl.ANY)] * n_after,
        out_specs=[spec(b, i) for _, _, b, i in outs],
        out_shape=[jax.ShapeDtypeStruct(s, d) for s, d, _, _ in outs],
        scratch_shapes=list(scratch),
        compiler_params=pltpu.CompilerParams(vmem_limit_bytes=vmem * 2**20),
        cost_estimate=pl.CostEstimate(flops=cost[0], bytes_accessed=cost[1], transcendentals=0),
    )(*[a for a, _, _ in ins], *after)


def in_order(bit, mine, other):
    return jnp.where(bit == 0, mine, other), jnp.where(bit == 0, other, mine)


def hold(cells, *earlier, cost=0):
    return pl.pallas_call(
        lambda *refs: None,
        in_specs=[pl.BlockSpec(memory_space=pl.ANY)] * (1 + len(earlier)),
        out_specs=pl.BlockSpec(memory_space=pl.ANY),
        out_shape=jax.ShapeDtypeStruct(cells.shape, cells.dtype),
        input_output_aliases={0: 0},
        compiler_params=pltpu.CompilerParams(vmem_limit_bytes=2**20),
        cost_estimate=pl.CostEstimate(flops=0, bytes_accessed=cost, transcendentals=0),
    )(cells, *earlier)


def at(*place):
    return lambda *_: place


def border_rows(tile_side):
    half = tile_side // 2
    return (half * half + 15) // 16 * 16


def border_picks(tile_side):
    half, rows = tile_side // 2, border_rows(tile_side)
    picks = np.zeros((2, 2 * rows, tile_side * tile_side), np.float32)
    for side in range(2):
        for low in range(2):
            for i in range(half):
                for j in range(half):
                    token = (low * half + i) * tile_side + j + (half if side == 0 else 0)
                    picks[side, low * rows + i * half + j, token] = 1
    return jnp.asarray(picks, BF16)


def modulate_and_heads(place, tokens, scale_row, shift_row, w_heads, after=()):
    rows, model_width = tokens.shape
    depth, width = w_heads.shape[1:]
    edge = (width - LANES) // 2
    block = max(b for b in range(16, rows + 1, 16) if rows % b == 0 and b <= ROWS)

    def body(place_ref, tokens_ref, scale_ref, shift_ref, w_heads_ref, own_ref, out_ref):
        side = place_ref[0]
        cells = tokens_ref[...].astype(F32)
        mean = jnp.mean(cells, axis=-1, keepdims=True)
        centered = cells - mean
        scaling = lax.rsqrt(jnp.mean(centered * centered, axis=-1, keepdims=True) + 1e-06)
        some = pl.ds(pl.multiple_of(side * depth, LANES), depth)
        normed = (tokens_ref[:, some].astype(F32) - mean) * scaling
        own = (normed * (1.0 + scale_ref[:, some]) + shift_ref[:, some]).astype(BF16)
        own_ref[...] = own
        theirs = pl.ds(pl.multiple_of((1 - side) * (width - edge), LANES), edge)
        for g in range(3):
            out_ref[:, g * edge : (g + 1) * edge] = dot(own, w_heads_ref[g, :, theirs]).astype(BF16)
        lane = lax.broadcasted_iota(jnp.int32, (block, LANES), 1)
        moments = jnp.zeros((block, LANES), F32)
        for first, moment in ((0, mean), (3, scaling)):
            for i in range(3):
                term = moment.astype(BF16).astype(F32)
                moments = jnp.where(lane == first + i, term, moments)
                moment = moment - term
        out_ref[:, 3 * edge :] = moments.astype(BF16)

    row = lambda i: (i, 0)
    return call(
        body, rows // block,
        [
            (place, None, pltpu.SMEM),
            (tokens, (block, model_width), row),
            (scale_row, scale_row.shape, at(0, 0)),
            (shift_row, shift_row.shape, at(0, 0)),
            (w_heads, w_heads.shape, at(0, 0, 0)),
        ],
        [
            ((rows, depth), BF16, (block, depth), row),
            ((rows, 3 * edge + LANES), BF16, (block, 3 * edge + LANES), row),
        ],
        after=after, vmem=VMEM,
    )


def border_and_hidden(place, own, picks, w_heads, hidden_weights, cut, after=()):
    rows, depth = own.shape
    half_border, width = picks.shape[1] // 2, w_heads.shape[2]

    def body(place_ref, own_ref, picks_ref, keys_ref, values_ref, w_ref, out_ref):
        taken = dot(picks_ref[place_ref[0]], own_ref[...]).astype(BF16)
        out_ref[:rows] = dot(own_ref[...], w_ref[...]).astype(BF16)
        for g, ref in enumerate((keys_ref, values_ref)):
            part = dot(taken, ref[0]).astype(BF16)
            out_ref[rows:, g * LANES : (g + 1) * LANES] = part[:half_border]
            out_ref[rows:, (2 + g) * LANES : (3 + g) * LANES] = part[half_border:]

    whole = at(0, 0)
    middle = (width - LANES) // 2 // LANES
    return call(
        body, 1,
        [(place, None, pltpu.SMEM), (own, own.shape, whole), (picks, picks.shape, at(0, 0, 0))]
        + [(w_heads, (1, depth, LANES), at(g, 0, middle)) for g in (1, 2)]
        + [(hidden_weights, (depth, cut), whole)],
        [((rows + half_border, cut), BF16, (rows + half_border, cut), whole)],
        after=after, vmem=VMEM,
    )[0]


def rest_of_first(place, own, other, picks, w_heads, hidden_weights, begin, cut, after=()):
    rows, depth = other.shape
    width, hidden = w_heads.shape[2], hidden_weights.shape[1]
    edge = (width - LANES) // 2
    border = picks.shape[1]
    block = width_of(begin, 512)
    parts = begin // block

    def body(
        place_ref, own_ref, other_ref, picks_ref, w_heads_ref, w_ref,
        qkv_ref, mine_ref, border_ref, rest_ref, a_ref, b_ref,
    ):
        side = place_ref[0]

        @pl.when(pl.program_id(0) == 0)
        def _():
            both = pl.ds(pl.multiple_of(side * edge, LANES), edge + LANES)
            mine = pl.ds(pl.multiple_of(side * (width - edge), LANES), edge)
            for g in range(3):
                qkv_ref[:, g * (edge + LANES) : (g + 1) * (edge + LANES)] = dot(own_ref[...], w_heads_ref[g, :, both])
                mine_ref[:, g * edge : (g + 1) * edge] = dot(other_ref[...], w_heads_ref[g, :, mine])
            taken = dot(picks_ref[1 - side], other_ref[...]).astype(BF16)
            for g in range(2):
                border_ref[:, g * LANES : (g + 1) * LANES] = dot(taken, w_heads_ref[1 + g, :, edge : edge + LANES])

        sums = dot(other_ref[...], w_ref[...])
        a_ref[...] = sums[:cut].astype(BF16)
        b_ref[...] = sums[cut:].astype(BF16)

        @pl.when(pl.program_id(0) >= parts)
        def _():
            rest_ref[...] = dot(own_ref[...], w_ref[...]).astype(BF16)

    whole = at(0, 0)
    column = lambda j: (0, j)
    out = lambda count, wide: ((count, wide), F32, (count, wide), whole)
    return call(
        body, hidden // block,
        [(place, None, pltpu.SMEM), (own, own.shape, whole), (other, other.shape, whole)]
        + [(a, a.shape, at(0, 0, 0)) for a in (picks, w_heads)]
        + [(hidden_weights, (depth, block), column)],
        [
            out(rows, 3 * (edge + LANES)),
            out(rows, 3 * edge),
            out(border, 2 * LANES),
            ((rows, hidden - begin), BF16, (rows, block), lambda j: (0, jnp.maximum(j - parts, 0))),
            ((cut, hidden), BF16, (cut, block), column),
            ((rows - cut, hidden), BF16, (rows - cut, block), column),
        ],
        after=after, vmem=REST_VMEM,
        cost=(
            2 * depth * (rows * 4 * width + border * 2 * LANES + rows * hidden),
            2 * depth * (2 * rows + 3 * width + hidden) + 12 * rows * width + 2 * rows * hidden,
        ),
    )


def norm_units(place, own, other, border, q_gain, k_gain, after=()):
    rows, heads, head_dim = own[0].shape[0], q_gain.shape[0], q_gain.shape[2]
    pair = heads // 2
    units = 2 * pair + 1
    half_border = border[0].shape[0] // 2
    sent_rows = (rows // 2 + 15) // 16 * 16
    sent = units * sent_rows + half_border

    def body(place_ref, *refs):
        own_refs, other_refs, border_refs = refs[:2], refs[2:4], refs[4:6]
        q_gain_ref, k_gain_ref, queries_ref, kv_ref, lower_ref, upper_ref = refs[6:]
        side = place_ref[0]
        first = side * (heads - pair)

        def head(two, index):
            some = pl.ds(pl.multiple_of(index * head_dim, LANES), head_dim)
            return sum(ref[:, some].astype(F32) for ref in two)

        def put(unit, two, p, count, index):
            q, k, v = (head(two, g * count + p) for g in range(3))
            kv = jnp.concatenate([rms_gain(k, k_gain_ref[index]), v], axis=1).astype(BF16)
            queries_ref[unit * rows : (unit + 1) * rows] = rms_gain(q, q_gain_ref[index]).astype(BF16)
            kv_ref[unit * rows : (unit + 1) * rows] = kv
            lower_ref[unit * sent_rows : (unit + 1) * sent_rows] = kv[rows - sent_rows :]
            upper_ref[unit * sent_rows : (unit + 1) * sent_rows] = kv[:sent_rows]

        for p in range(pair):
            put(2 * p, own_refs, side + p, pair + 1, first + p)
            put(2 * p + 1, other_refs, p, pair, first + p)
        put(2 * pair, own_refs, (1 - side) * pair, pair + 1, pair)
        got = border_refs[1][rows:].astype(F32)
        got = jnp.concatenate([got[:, : 2 * head_dim], got[:, 2 * head_dim : 4 * head_dim]], axis=0)
        both = border_refs[0][...] + got
        kv = [rms_gain(both[:, :head_dim], k_gain_ref[pair]), both[:, head_dim:]]
        kv = jnp.concatenate(kv, axis=1).astype(BF16)
        kv_ref[units * rows :] = kv
        upper_ref[units * sent_rows :] = kv[:half_border]
        lower_ref[units * sent_rows :] = kv[half_border:]

    whole = at(0, 0)
    out = lambda count, width: ((count, width), BF16, (count, width), whole)
    ins = [*own, *other, *border]
    return call(
        body, 1,
        [(place, None, pltpu.SMEM)]
        + [(a, a.shape, whole) for a in ins]
        + [(g, g.shape, at(0, 0, 0)) for g in (q_gain, k_gain)],
        [
            out(units * rows, head_dim),
            out(units * rows + 2 * half_border, 2 * head_dim),
            out(sent, 2 * head_dim),
            out(sent, 2 * head_dim),
        ],
        after=after, vmem=POST_VMEM,
    )


def window_codes(tile_side):
    rows, half = tile_side * tile_side, tile_side // 2
    sent_rows = (rows // 2 + 15) // 16 * 16
    extra = sent_rows - rows // 2
    column = np.arange(rows) % tile_side

    def lines(first, second):
        above = lambda on: np.concatenate([np.zeros(extra, np.int32), 2 * on[rows - rows // 2 :]])
        below = lambda on: np.concatenate([3 * on[: rows // 2], np.zeros(extra, np.int32)])
        return np.concatenate([first, second, above(first), above(second), below(first), below(second)])

    def padded(line):
        return np.pad(line, (0, -len(line) % LANES)).astype(np.float32)

    every = np.ones(rows, np.int32)
    right, left = (column >= half).astype(np.int32), (column < half).astype(np.int32)
    by_side = np.stack([
        np.stack([padded(lines(every, left)), padded(lines(right, every))]),
        np.stack([padded(lines(every, right)), padded(lines(left, every))]),
    ])
    pad = border_rows(tile_side)
    part = np.pad(np.ones(half * half, np.int32), (0, pad - half * half))
    above = np.concatenate([np.zeros(extra, np.int32), 2 * np.ones(rows // 2, np.int32), 2 * part])
    below = np.concatenate([3 * np.ones(rows // 2, np.int32), np.zeros(extra, np.int32), 3 * part])
    middle = padded(np.concatenate([every, part, part, above, below]))[None]
    return jnp.asarray(by_side), jnp.asarray(middle)


def attend(place, queries, keys_values, above, below, codes, middle_codes, heads, after=()):
    pair = heads // 2
    units = 2 * pair + 1
    head_dim = queries.shape[1]
    rows = queries.shape[0] // units
    border = keys_values.shape[0] - units * rows
    sent_rows = (above.shape[0] - border // 2) // units

    def body(place_ref, queries_ref, kv_ref, above_ref, below_ref, codes_ref, middle_ref, out_ref):
        side = place_ref[0]

        def unit_rows(ref, unit, count, size):
            return ref[unit * size : (unit + count) * size]

        def rest_rows(ref, size):
            return ref[units * size :]

        def one(unit, blocks, line, column):
            there = (line == 1) | ((line == 2) & (place_ref[2] == 1)) | ((line == 3) & (place_ref[3] == 1))
            line = jnp.where(there, 0.0, -jnp.inf)
            spare = line.shape[1] - sum(b.shape[0] for b in blocks)
            if spare:
                blocks = blocks + [jnp.zeros((spare, 2 * head_dim), BF16)]
            both = jnp.concatenate(blocks, axis=0)
            keys, values = both[:, :head_dim], both[:, head_dim:]
            mine = unit_rows(queries_ref, unit, 1, rows)
            scores = lax.dot_general(mine, keys, (((1,), (1,)), ((), ())), preferred_element_type=F32)
            scores = scores * head_dim ** (-0.5) + line
            numerators = jnp.exp(scores - jnp.max(scores, axis=-1, keepdims=True))
            total = jnp.sum(numerators, axis=-1, keepdims=True)
            got = (dot(numerators.astype(BF16), values) / total).astype(BF16)
            out_ref[:, column * head_dim : (column + 1) * head_dim] = got

        for p in range(pair):
            blocks = [
                unit_rows(kv_ref, 2 * p, 2, rows),
                unit_rows(above_ref, 2 * p, 2, sent_rows),
                unit_rows(below_ref, 2 * p, 2, sent_rows),
            ]
            one(2 * p, blocks, codes_ref[side][0:1], p)
            one(2 * p + 1, blocks, codes_ref[side][1:2], pair + 1 + p)
        blocks = [
            kv_ref[2 * pair * rows :],
            above_ref[2 * pair * sent_rows :],
            below_ref[2 * pair * sent_rows :],
        ]
        one(2 * pair, blocks, middle_ref[...], pair)

    ins = [queries, keys_values, above, below, middle_codes]
    whole = [(a, a.shape, at(0, 0)) for a in ins]
    return call(
        body, 1,
        [(place, None, pltpu.SMEM)] + whole[:4] + [(codes, codes.shape, at(0, 0, 0))] + whole[4:],
        [((rows, units * head_dim), BF16, (rows, units * head_dim), at(0, 0))],
        after=after, vmem=POST_VMEM,
    )[0]


def paired_plan(
    tokens, mod_shift, mod_scale, mod_gate, w_qkv, w_mlp_in, q_gain, k_gain, w_attn_out, w_mlp_out
):
    tok_rows, model_width = tokens.shape
    half_width, hidden = w_mlp_in.shape
    heads, head_dim = q_gain.shape
    width = heads * head_dim
    side = lax.axis_index("sx")
    part = lax.axis_index("tp")
    core, far = part % 2, part // 2
    mid = hidden // 2
    block = half_width // 2
    row = lax.axis_index("sy")
    place = jnp.stack([side, core, row > 0, row < lax.axis_size("sy") - 1]).astype(jnp.int32)
    picks = border_picks(TILE)
    q_gain, k_gain = q_gain[:, None, :], k_gain[:, None, :]

    quarter = half_width // 4
    other_first = (1 - side) * half_width + part * quarter
    sent = lax.dynamic_slice_in_dim(lax.optimization_barrier(tokens), other_first, quarter, 1)
    piece = swap(sent, "sx", 1)
    first = side * half_width
    gain_part = 1.0 + lax.dynamic_slice_in_dim(mod_scale, first, half_width, 0)
    shift_part = lax.dynamic_slice_in_dim(mod_shift, first, half_width, 0)

    def modulate(cells, pair):
        cells = (cells.astype(F32) - pair[0]) * pair[1]
        return (cells * gain_part + shift_part).astype(BF16)

    pair = heads // 2
    edge = pair * head_dim
    w_heads = jnp.transpose(w_qkv, (1, 0, 2))

    own, own_early = modulate_and_heads(place, tokens, mod_scale[None], mod_shift[None], w_heads, [sent])
    got_early = swap(own_early, "sx", 1)
    piece = hold(piece, own_early)
    pieces = in_order(far, piece, hold(swap(piece, "tp", 2), got_early))
    first_part = width_of(hidden // 3, hidden)
    own_first = border_and_hidden(place, own, picks, w_heads, w_mlp_in, first_part, [own_early, piece])
    got_first = swap(own_first, "sx", 1)
    pieces = hold(jnp.concatenate(pieces, axis=1), got_early, own_first)
    near = swap(pieces, "tp", 1)
    even, odd = in_order(core, pieces, near)
    other = jnp.concatenate([even[:, :quarter], odd[:, :quarter], even[:, quarter:], odd[:, quarter:]], axis=1)
    terms = [got_early[:, 3 * edge + i : 3 * edge + i + 1].astype(F32) for i in range(6)]
    other = modulate(other, [terms[i] + terms[i + 1] + terms[i + 2] for i in (0, 3)])
    late_first = (1 - side) * edge
    other_late = [
        dot(other, lax.dynamic_slice(w_heads, (g, 0, late_first), (1, half_width, edge + head_dim))[0]).astype(BF16)
        for g in range(3)
    ]
    other_late = jnp.concatenate(other_late, axis=1)
    got_late = swap(other_late, "sx", 1)
    cut = tok_rows // 2
    own_heads, other_heads, other_border, own_rest, other_a, other_b = rest_of_first(
        place, own, other, picks, w_heads, w_mlp_in, first_part, cut, [other_late, got_first]
    )
    got_rest = swap(own_rest, "sx", 1)
    queries, keys_values, lower, upper = norm_units(
        place, (own_heads, got_late), (other_heads, got_early), (other_border, got_first), q_gain, k_gain, [other_a]
    )
    above = shift(lower, "sy", 1)
    below = shift(upper, "sy", -1)

    sent_mlp, kept_mlp, sent_attn, kept_attn = (
        lax.dynamic_slice_in_dim(w, start * block, block, 1)
        for w in (w_mlp_out, w_attn_out)
        for start in (1 - core, core)
    )

    def activate(mine, got, *earlier):
        got = hold(got, *earlier) if earlier else got
        return hold(jax.nn.gelu(mine.astype(F32) + got.astype(F32), approximate=True).astype(BF16))

    attended = attend(place, queries, keys_values, above, below, *window_codes(TILE), heads)
    got_attended = swap(attended, "sx", 1)
    got_other_a = swap(other_a, "sx", 1)
    got_own = jnp.concatenate([got_first[:tok_rows], hold(got_rest, attended)], axis=1)
    own_hidden = jnp.concatenate([own_first[:tok_rows], own_rest], axis=1)
    other_active = activate(jnp.concatenate([other_a, other_b], axis=0), got_own)
    other_sent, other_kept = dot(other_active, sent_mlp), dot(other_active, kept_mlp)
    got_other_b = swap(hold(other_b, other_sent), "sx", 1)

    def own_part(begin, end, got, *earlier):
        active, heads_part = activate(own_hidden[begin:end], got, *earlier), own_attended[begin:end]
        return (
            (dot(active, sent_mlp) + dot(heads_part, sent_attn)).astype(BF16),
            dot(active, kept_mlp) + dot(heads_part, kept_attn),
        )

    got_attended = hold(got_attended, other_sent, other_kept, got_other_a)
    here = edge + head_dim

    def natural(mine, middle, theirs):
        return jnp.concatenate(
            [jnp.where(side == 0, mine, theirs), middle, jnp.where(side == 0, theirs, mine)], axis=1
        )

    own_attended = natural(attended[:, :edge], attended[:, edge:here], got_attended[:, here:])
    other_attended = natural(attended[:, here:], got_attended[:, edge:here], got_attended[:, :edge])
    other_sent = (other_sent + dot(other_attended, sent_attn)).astype(BF16)
    other_kept = other_kept + dot(other_attended, kept_attn)
    other_come = swap(other_sent, "tp", 1)
    own_sent_a, own_kept_a = own_part(0, cut, got_other_a, other_sent, other_kept)

    def rows_of(half):
        kept = jnp.where(half == 0, other_kept[:cut], other_kept[cut:])
        return kept + jnp.where(half == 0, other_come[:cut], other_come[cut:]).astype(F32)

    passed = rows_of(1 - far).astype(BF16)
    passed = hold(swap(passed, "tp", 2), own_sent_a, own_kept_a)
    crossing = (rows_of(far) + passed.astype(F32)).astype(BF16)
    got = swap(crossing, "sx", 1)
    own_sum_a = own_kept_a + swap(own_sent_a, "tp", 1).astype(F32)
    come_a = swap(own_sum_a.astype(BF16), "tp", 2)
    own_sent_b, own_kept_b = own_part(cut, tok_rows, got_other_b, crossing)
    own_sum_b = hold(own_kept_b, got, come_a, cost=EARLY) + swap(own_sent_b, "tp", 1).astype(F32)

    home = far == side
    come_b = swap(jnp.where(home, got, own_sum_b.astype(BF16)), "tp", 2)
    wide = got.astype(F32)
    known = jnp.concatenate(
        [
            jnp.where(home, own_sum_a + come_a.astype(F32), jnp.where(far == 0, wide, 0.0)),
            jnp.where(home, own_sum_b, jnp.where(far == 0, 0.0, wide)),
        ],
        axis=0,
    )
    first_col = hold(part[None], own_sent_a)[0] * block
    gate_part = lax.dynamic_slice_in_dim(mod_gate, first_col, block, 0)
    residual_part = lax.dynamic_slice_in_dim(tokens, first_col, block, 1).astype(F32)
    known = hold(residual_part + gate_part * known)
    late_first = jnp.where(home, 1, 1 - far) * cut
    token = lax.broadcasted_iota(jnp.int32, (tok_rows, 1), 0)
    late = (token >= late_first) & (token < late_first + cut)
    late_part = jnp.concatenate([come_b, come_b], axis=0).astype(F32)
    return (known + jnp.where(late, gate_part * late_part, 0.0)).astype(BF16)


def shards(*arrays):
    local_heads = arrays[6].shape[0]
    if lax.axis_size("sx") == 2 and lax.axis_size("tp") == 4 and local_heads % 2 and local_heads > 1 and arrays[6].shape[1] == LANES:
        return paired_plan(*arrays)
    return gathered_plan(*arrays)


def solution(mesh):
    placed = (
        P(("sy", "sx"), None),
        P(),
        P(),
        P(),
        P("sx", None, "tp"),
        P("sx", "tp"),
        P("tp", None),
        P("tp", None),
        P("tp", "sx"),
        P("tp", "sx"),
    )
    return jax.shard_map(
        shards, mesh=mesh, in_specs=placed, out_specs=P(("sy", "sx"), "tp"), check_vma=False
    )
```

```python
import jax
import jax.numpy as jnp
import numpy as np
from jax import lax
from jax.experimental import pallas as pl
from jax.experimental.pallas import tpu as pltpu
from jax.sharding import PartitionSpec as P

TILE = 20


def with_halo(cells, sides, width):
    for axis, dim in sides:
        count = lax.axis_size(axis)
        ends = count - 1
        head = lax.slice_in_dim(cells, 0, width, axis=dim)
        tail = lax.slice_in_dim(cells, cells.shape[dim] - width, cells.shape[dim], axis=dim)
        cells = jnp.concatenate(
            [
                lax.ppermute(tail, axis, [(i, (i + 1) % count) for i in range(ends)]),
                cells,
                lax.ppermute(head, axis, [((i + 1) % count, i) for i in range(ends)]),
            ],
            axis=dim,
        )
    return cells


def layer_norm(vector):
    centered = vector - jnp.mean(vector, axis=-1, keepdims=True)
    variance = jnp.mean(centered * centered, axis=-1, keepdims=True)
    return centered * lax.rsqrt(variance + 1e-06)


def rms_gain(vector, scaling):
    mean_square = jnp.mean(vector * vector, axis=-1, keepdims=True)
    return vector * lax.rsqrt(mean_square + 1e-06) * scaling


def gathered_plan(
    tokens, mod_shift, mod_scale, mod_gate, w_qkv, w_mlp_in, q_gain, k_gain, w_attn_out, w_mlp_out
):
    tok_rows, model_width = tokens.shape
    tile_side = TILE
    half_side = TILE // 2
    inputs = tokens.astype(jnp.float32)
    modded = (layer_norm(inputs) * (1.0 + mod_scale) + mod_shift).astype(jnp.bfloat16)
    local_heads, head_dim = q_gain.shape
    local_width = local_heads * head_dim
    pieces = (
        lax.all_gather(w_qkv, "sx", axis=0, tiled=True),
        lax.all_gather(w_mlp_in, "sx", axis=0, tiled=True),
    )
    piece_rows = pieces[0].shape[0]
    qkv_sum = jnp.dot(
        modded, pieces[0].reshape(piece_rows, 3 * local_width), preferred_element_type=jnp.float32
    )
    mlp_sum = jnp.dot(modded, pieces[1], preferred_element_type=jnp.float32)
    qkv_parts = qkv_sum.reshape(tok_rows, 3, local_heads, head_dim)
    queries = rms_gain(qkv_parts[:, 0], q_gain).astype(jnp.bfloat16)
    key_rows = rms_gain(qkv_parts[:, 1], k_gain).astype(jnp.bfloat16)
    value_rows = qkv_parts[:, 2].astype(jnp.bfloat16)
    key_value = jnp.concatenate(
        [key_rows.reshape(tok_rows, local_width), value_rows.reshape(tok_rows, local_width)], axis=1
    )
    key_value = key_value.reshape(tile_side, tile_side, 2 * local_width)
    extended = with_halo(key_value, (("sy", 0), ("sx", 1)), half_side)
    window = extended.reshape(4 * tok_rows, 2 * local_width)
    window_keys = window[:, :local_width].reshape(4 * tok_rows, local_heads, head_dim)
    window_values = window[:, local_width:].reshape(4 * tok_rows, local_heads, head_dim)
    offsets = jnp.arange(2 * tile_side, dtype=jnp.int32)
    row_pos = lax.axis_index("sy") * tile_side - half_side + offsets
    col_pos = lax.axis_index("sx") * tile_side - half_side + offsets
    row_ok = (row_pos >= 0) & (row_pos < tile_side * lax.axis_size("sy"))
    col_ok = (col_pos >= 0) & (col_pos < tile_side * lax.axis_size("sx"))
    in_grid = (row_ok[:, None] & col_ok[None, :]).reshape(4 * tok_rows)
    scores = jnp.einsum(
        "qhd,khd->hqk", queries, window_keys, preferred_element_type=jnp.float32
    ) * head_dim ** (-0.5)
    scores = jnp.where(in_grid[None, None, :], scores, -jnp.inf)
    row_max = jnp.max(scores, axis=-1, keepdims=True)
    numerators = jnp.exp(scores - row_max)
    weights = (numerators / jnp.sum(numerators, axis=-1, keepdims=True)).astype(jnp.bfloat16)
    attended = jnp.einsum(
        "hqk,khd->qhd", weights, window_values, preferred_element_type=jnp.float32
    )
    attended = attended.astype(jnp.bfloat16).reshape(tok_rows, local_width)
    activated = jax.nn.gelu(mlp_sum, approximate=True).astype(jnp.bfloat16)
    pieces = (
        lax.all_gather(w_attn_out, "sx", axis=1, tiled=True),
        lax.all_gather(w_mlp_out, "sx", axis=1, tiled=True),
    )
    product_term = jnp.dot(attended, pieces[0], preferred_element_type=jnp.float32)
    product_term = product_term + jnp.dot(activated, pieces[1], preferred_element_type=jnp.float32)
    reduced = lax.psum_scatter(
        product_term.astype(jnp.bfloat16), "tp", scatter_dimension=1, tiled=True
    ).astype(jnp.float32)
    block_width = model_width // lax.axis_size("tp")
    first_col = lax.axis_index("tp") * block_width
    residual_part = lax.dynamic_slice_in_dim(inputs, first_col, block_width, 1)
    gate_part = lax.dynamic_slice_in_dim(mod_gate, first_col, block_width, 0)
    return (residual_part + gate_part * reduced).astype(jnp.bfloat16)


def swap(cells, axis, bit):
    count = lax.axis_size(axis)
    return lax.ppermute(cells, axis, [(i, i ^ bit) for i in range(count)])


def shift(cells, axis, step):
    count = lax.axis_size(axis)
    return lax.ppermute(
        cells, axis, [(i, i + step) for i in range(count) if 0 <= i + step < count]
    )


def dot(left, right):
    return jnp.dot(left, right, preferred_element_type=jnp.float32)


BF16, F32 = jnp.bfloat16, jnp.float32
LANES = 128
EARLY = 20_000_000
VMEM = 56
REST_VMEM = 40
POST_VMEM = 40
ROWS = 80


def width_of(total, most):
    return max(w for w in range(LANES, most + 1, LANES) if total % w == 0)


def call(body, grid, ins, outs, scratch=(), after=(), vmem=16, cost=(1000, 1000)):
    n_in, n_after = len(ins), len(after)

    def kernel(*refs):
        body(*refs[:n_in], *refs[n_in + n_after :])

    def spec(block, index):
        if block is None:
            return pl.BlockSpec(memory_space=index)
        return pl.BlockSpec(block, index)

    return pl.pallas_call(
        kernel,
        grid=(grid,),
        in_specs=[spec(b, i) for _, b, i in ins] + [pl.BlockSpec(memory_space=pl.ANY)] * n_after,
        out_specs=[spec(b, i) for _, _, b, i in outs],
        out_shape=[jax.ShapeDtypeStruct(s, d) for s, d, _, _ in outs],
        scratch_shapes=list(scratch),
        compiler_params=pltpu.CompilerParams(vmem_limit_bytes=vmem * 2**20),
        cost_estimate=pl.CostEstimate(flops=cost[0], bytes_accessed=cost[1], transcendentals=0),
    )(*[a for a, _, _ in ins], *after)


def in_order(bit, mine, other):
    return jnp.where(bit == 0, mine, other), jnp.where(bit == 0, other, mine)


def hold(cells, *earlier, cost=0):
    return pl.pallas_call(
        lambda *refs: None,
        in_specs=[pl.BlockSpec(memory_space=pl.ANY)] * (1 + len(earlier)),
        out_specs=pl.BlockSpec(memory_space=pl.ANY),
        out_shape=jax.ShapeDtypeStruct(cells.shape, cells.dtype),
        input_output_aliases={0: 0},
        compiler_params=pltpu.CompilerParams(vmem_limit_bytes=2**20),
        cost_estimate=pl.CostEstimate(flops=0, bytes_accessed=cost, transcendentals=0),
    )(cells, *earlier)


def at(*place):
    return lambda *_: place


def border_rows(tile_side):
    half = tile_side // 2
    return (half * half + 15) // 16 * 16


def border_picks(tile_side):
    half, rows = tile_side // 2, border_rows(tile_side)
    picks = np.zeros((2, 2 * rows, tile_side * tile_side), np.float32)
    for side in range(2):
        for low in range(2):
            for i in range(half):
                for j in range(half):
                    token = (low * half + i) * tile_side + j + (half if side == 0 else 0)
                    picks[side, low * rows + i * half + j, token] = 1
    return jnp.asarray(picks, BF16)


def modulate_and_heads(place, tokens, scale_row, shift_row, w_heads, after=()):
    rows, model_width = tokens.shape
    depth, width = w_heads.shape[1:]
    edge = (width - LANES) // 2
    block = max(b for b in range(16, rows + 1, 16) if rows % b == 0 and b <= ROWS)

    def body(place_ref, tokens_ref, scale_ref, shift_ref, w_heads_ref, own_ref, out_ref):
        side = place_ref[0]
        cells = tokens_ref[...].astype(F32)
        mean = jnp.mean(cells, axis=-1, keepdims=True)
        centered = cells - mean
        scaling = lax.rsqrt(jnp.mean(centered * centered, axis=-1, keepdims=True) + 1e-06)
        some = pl.ds(pl.multiple_of(side * depth, LANES), depth)
        normed = (tokens_ref[:, some].astype(F32) - mean) * scaling
        own = (normed * (1.0 + scale_ref[:, some]) + shift_ref[:, some]).astype(BF16)
        own_ref[...] = own
        theirs = pl.ds(pl.multiple_of((1 - side) * (width - edge), LANES), edge)
        for g in range(3):
            out_ref[:, g * edge : (g + 1) * edge] = dot(own, w_heads_ref[g, :, theirs]).astype(BF16)
        lane = lax.broadcasted_iota(jnp.int32, (block, LANES), 1)
        moments = jnp.zeros((block, LANES), F32)
        for first, moment in ((0, mean), (3, scaling)):
            for i in range(3):
                term = moment.astype(BF16).astype(F32)
                moments = jnp.where(lane == first + i, term, moments)
                moment = moment - term
        out_ref[:, 3 * edge :] = moments.astype(BF16)

    row = lambda i: (i, 0)
    return call(
        body, rows // block,
        [
            (place, None, pltpu.SMEM),
            (tokens, (block, model_width), row),
            (scale_row, scale_row.shape, at(0, 0)),
            (shift_row, shift_row.shape, at(0, 0)),
            (w_heads, w_heads.shape, at(0, 0, 0)),
        ],
        [
            ((rows, depth), BF16, (block, depth), row),
            ((rows, 3 * edge + LANES), BF16, (block, 3 * edge + LANES), row),
        ],
        after=after, vmem=VMEM,
    )


def border_and_hidden(place, own, picks, w_heads, hidden_weights, cut, after=()):
    rows, depth = own.shape
    half_border, width = picks.shape[1] // 2, w_heads.shape[2]

    def body(place_ref, own_ref, picks_ref, keys_ref, values_ref, w_ref, out_ref):
        taken = dot(picks_ref[place_ref[0]], own_ref[...]).astype(BF16)
        out_ref[:rows] = dot(own_ref[...], w_ref[...]).astype(BF16)
        for g, ref in enumerate((keys_ref, values_ref)):
            part = dot(taken, ref[0]).astype(BF16)
            out_ref[rows:, g * LANES : (g + 1) * LANES] = part[:half_border]
            out_ref[rows:, (2 + g) * LANES : (3 + g) * LANES] = part[half_border:]

    whole = at(0, 0)
    middle = (width - LANES) // 2 // LANES
    return call(
        body, 1,
        [(place, None, pltpu.SMEM), (own, own.shape, whole), (picks, picks.shape, at(0, 0, 0))]
        + [(w_heads, (1, depth, LANES), at(g, 0, middle)) for g in (1, 2)]
        + [(hidden_weights, (depth, cut), whole)],
        [((rows + half_border, cut), BF16, (rows + half_border, cut), whole)],
        after=after, vmem=VMEM,
    )[0]


def rest_of_first(place, own, other, picks, w_heads, hidden_weights, begin, cut, after=()):
    rows, depth = other.shape
    width, hidden = w_heads.shape[2], hidden_weights.shape[1]
    edge = (width - LANES) // 2
    border = picks.shape[1]
    block = width_of(begin, 512)
    parts = begin // block

    def body(
        place_ref, own_ref, other_ref, picks_ref, w_heads_ref, w_ref,
        qkv_ref, mine_ref, border_ref, rest_ref, a_ref, b_ref,
    ):
        side = place_ref[0]

        @pl.when(pl.program_id(0) == 0)
        def _():
            both = pl.ds(pl.multiple_of(side * edge, LANES), edge + LANES)
            mine = pl.ds(pl.multiple_of(side * (width - edge), LANES), edge)
            for g in range(3):
                qkv_ref[:, g * (edge + LANES) : (g + 1) * (edge + LANES)] = dot(own_ref[...], w_heads_ref[g, :, both])
                mine_ref[:, g * edge : (g + 1) * edge] = dot(other_ref[...], w_heads_ref[g, :, mine])
            taken = dot(picks_ref[1 - side], other_ref[...]).astype(BF16)
            for g in range(2):
                border_ref[:, g * LANES : (g + 1) * LANES] = dot(taken, w_heads_ref[1 + g, :, edge : edge + LANES])

        sums = dot(other_ref[...], w_ref[...])
        a_ref[...] = sums[:cut].astype(BF16)
        b_ref[...] = sums[cut:].astype(BF16)

        @pl.when(pl.program_id(0) >= parts)
        def _():
            rest_ref[...] = dot(own_ref[...], w_ref[...]).astype(BF16)

    whole = at(0, 0)
    column = lambda j: (0, j)
    out = lambda count, wide: ((count, wide), F32, (count, wide), whole)
    return call(
        body, hidden // block,
        [(place, None, pltpu.SMEM), (own, own.shape, whole), (other, other.shape, whole)]
        + [(a, a.shape, at(0, 0, 0)) for a in (picks, w_heads)]
        + [(hidden_weights, (depth, block), column)],
        [
            out(rows, 3 * (edge + LANES)),
            out(rows, 3 * edge),
            out(border, 2 * LANES),
            ((rows, hidden - begin), BF16, (rows, block), lambda j: (0, jnp.maximum(j - parts, 0))),
            ((cut, hidden), BF16, (cut, block), column),
            ((rows - cut, hidden), BF16, (rows - cut, block), column),
        ],
        after=after, vmem=REST_VMEM,
        cost=(
            2 * depth * (rows * 4 * width + border * 2 * LANES + rows * hidden),
            2 * depth * (2 * rows + 3 * width + hidden) + 12 * rows * width + 2 * rows * hidden,
        ),
    )


def norm_units(place, own, other, border, q_gain, k_gain, after=()):
    rows, heads, head_dim = own[0].shape[0], q_gain.shape[0], q_gain.shape[2]
    pair = heads // 2
    units = 2 * pair + 1
    half_border = border[0].shape[0] // 2
    sent_rows = (rows // 2 + 15) // 16 * 16
    sent = units * sent_rows + half_border

    def body(place_ref, *refs):
        own_refs, other_refs, border_refs = refs[:2], refs[2:4], refs[4:6]
        q_gain_ref, k_gain_ref, queries_ref, kv_ref, lower_ref, upper_ref = refs[6:]
        side = place_ref[0]
        first = side * (heads - pair)

        def head(two, index):
            some = pl.ds(pl.multiple_of(index * head_dim, LANES), head_dim)
            return sum(ref[:, some].astype(F32) for ref in two)

        def put(unit, two, p, count, index):
            q, k, v = (head(two, g * count + p) for g in range(3))
            kv = jnp.concatenate([rms_gain(k, k_gain_ref[index]), v], axis=1).astype(BF16)
            queries_ref[unit * rows : (unit + 1) * rows] = rms_gain(q, q_gain_ref[index]).astype(BF16)
            kv_ref[unit * rows : (unit + 1) * rows] = kv
            lower_ref[unit * sent_rows : (unit + 1) * sent_rows] = kv[rows - sent_rows :]
            upper_ref[unit * sent_rows : (unit + 1) * sent_rows] = kv[:sent_rows]

        for p in range(pair):
            put(2 * p, own_refs, side + p, pair + 1, first + p)
            put(2 * p + 1, other_refs, p, pair, first + p)
        put(2 * pair, own_refs, (1 - side) * pair, pair + 1, pair)
        got = border_refs[1][rows:].astype(F32)
        got = jnp.concatenate([got[:, : 2 * head_dim], got[:, 2 * head_dim : 4 * head_dim]], axis=0)
        both = border_refs[0][...] + got
        kv = [rms_gain(both[:, :head_dim], k_gain_ref[pair]), both[:, head_dim:]]
        kv = jnp.concatenate(kv, axis=1).astype(BF16)
        kv_ref[units * rows :] = kv
        upper_ref[units * sent_rows :] = kv[:half_border]
        lower_ref[units * sent_rows :] = kv[half_border:]

    whole = at(0, 0)
    out = lambda count, width: ((count, width), BF16, (count, width), whole)
    ins = [*own, *other, *border]
    return call(
        body, 1,
        [(place, None, pltpu.SMEM)]
        + [(a, a.shape, whole) for a in ins]
        + [(g, g.shape, at(0, 0, 0)) for g in (q_gain, k_gain)],
        [
            out(units * rows, head_dim),
            out(units * rows + 2 * half_border, 2 * head_dim),
            out(sent, 2 * head_dim),
            out(sent, 2 * head_dim),
        ],
        after=after, vmem=POST_VMEM,
    )


def window_codes(tile_side):
    rows, half = tile_side * tile_side, tile_side // 2
    sent_rows = (rows // 2 + 15) // 16 * 16
    extra = sent_rows - rows // 2
    column = np.arange(rows) % tile_side

    def lines(first, second):
        above = lambda on: np.concatenate([np.zeros(extra, np.int32), 2 * on[rows - rows // 2 :]])
        below = lambda on: np.concatenate([3 * on[: rows // 2], np.zeros(extra, np.int32)])
        return np.concatenate([first, second, above(first), above(second), below(first), below(second)])

    def padded(line):
        return np.pad(line, (0, -len(line) % LANES)).astype(np.float32)

    every = np.ones(rows, np.int32)
    right, left = (column >= half).astype(np.int32), (column < half).astype(np.int32)
    by_side = np.stack([
        np.stack([padded(lines(every, left)), padded(lines(right, every))]),
        np.stack([padded(lines(every, right)), padded(lines(left, every))]),
    ])
    pad = border_rows(tile_side)
    part = np.pad(np.ones(half * half, np.int32), (0, pad - half * half))
    above = np.concatenate([np.zeros(extra, np.int32), 2 * np.ones(rows // 2, np.int32), 2 * part])
    below = np.concatenate([3 * np.ones(rows // 2, np.int32), np.zeros(extra, np.int32), 3 * part])
    middle = padded(np.concatenate([every, part, part, above, below]))[None]
    return jnp.asarray(by_side), jnp.asarray(middle)


def attend(place, queries, keys_values, above, below, codes, middle_codes, heads, after=()):
    pair = heads // 2
    units = 2 * pair + 1
    head_dim = queries.shape[1]
    rows = queries.shape[0] // units
    border = keys_values.shape[0] - units * rows
    sent_rows = (above.shape[0] - border // 2) // units

    def body(place_ref, queries_ref, kv_ref, above_ref, below_ref, codes_ref, middle_ref, out_ref):
        side = place_ref[0]

        def unit_rows(ref, unit, count, size):
            return ref[unit * size : (unit + count) * size]

        def rest_rows(ref, size):
            return ref[units * size :]

        def one(unit, blocks, line, column):
            there = (line == 1) | ((line == 2) & (place_ref[2] == 1)) | ((line == 3) & (place_ref[3] == 1))
            line = jnp.where(there, 0.0, -jnp.inf)
            spare = line.shape[1] - sum(b.shape[0] for b in blocks)
            if spare:
                blocks = blocks + [jnp.zeros((spare, 2 * head_dim), BF16)]
            both = jnp.concatenate(blocks, axis=0)
            keys, values = both[:, :head_dim], both[:, head_dim:]
            mine = unit_rows(queries_ref, unit, 1, rows)
            scores = lax.dot_general(mine, keys, (((1,), (1,)), ((), ())), preferred_element_type=F32)
            scores = scores * head_dim ** (-0.5) + line
            numerators = jnp.exp(scores - jnp.max(scores, axis=-1, keepdims=True))
            total = jnp.sum(numerators, axis=-1, keepdims=True)
            got = (dot(numerators.astype(BF16), values) / total).astype(BF16)
            out_ref[:, column * head_dim : (column + 1) * head_dim] = got

        for p in range(pair):
            blocks = [
                unit_rows(kv_ref, 2 * p, 2, rows),
                unit_rows(above_ref, 2 * p, 2, sent_rows),
                unit_rows(below_ref, 2 * p, 2, sent_rows),
            ]
            one(2 * p, blocks, codes_ref[side][0:1], p)
            one(2 * p + 1, blocks, codes_ref[side][1:2], pair + 1 + p)
        blocks = [
            kv_ref[2 * pair * rows :],
            above_ref[2 * pair * sent_rows :],
            below_ref[2 * pair * sent_rows :],
        ]
        one(2 * pair, blocks, middle_ref[...], pair)

    ins = [queries, keys_values, above, below, middle_codes]
    whole = [(a, a.shape, at(0, 0)) for a in ins]
    return call(
        body, 1,
        [(place, None, pltpu.SMEM)] + whole[:4] + [(codes, codes.shape, at(0, 0, 0))] + whole[4:],
        [((rows, units * head_dim), BF16, (rows, units * head_dim), at(0, 0))],
        after=after, vmem=POST_VMEM,
    )[0]


def paired_plan(
    tokens, mod_shift, mod_scale, mod_gate, w_qkv, w_mlp_in, q_gain, k_gain, w_attn_out, w_mlp_out
):
    tok_rows, model_width = tokens.shape
    half_width, hidden = w_mlp_in.shape
    heads, head_dim = q_gain.shape
    width = heads * head_dim
    side = lax.axis_index("sx")
    part = lax.axis_index("tp")
    core, far = part % 2, part // 2
    mid = hidden // 2
    block = half_width // 2
    row = lax.axis_index("sy")
    place = jnp.stack([side, core, row > 0, row < lax.axis_size("sy") - 1]).astype(jnp.int32)
    picks = border_picks(TILE)
    q_gain, k_gain = q_gain[:, None, :], k_gain[:, None, :]

    quarter = half_width // 4
    other_first = (1 - side) * half_width + part * quarter
    sent = lax.dynamic_slice_in_dim(lax.optimization_barrier(tokens), other_first, quarter, 1)
    piece = swap(sent, "sx", 1)
    first = side * half_width
    gain_part = 1.0 + lax.dynamic_slice_in_dim(mod_scale, first, half_width, 0)
    shift_part = lax.dynamic_slice_in_dim(mod_shift, first, half_width, 0)

    def modulate(cells, pair):
        cells = (cells.astype(F32) - pair[0]) * pair[1]
        return (cells * gain_part + shift_part).astype(BF16)

    pair = heads // 2
    edge = pair * head_dim
    w_heads = jnp.transpose(w_qkv, (1, 0, 2))

    own, own_early = modulate_and_heads(place, tokens, mod_scale[None], mod_shift[None], w_heads, [sent])
    got_early = swap(own_early, "sx", 1)
    piece = hold(piece, own_early)
    near = swap(piece, "tp", 1)
    piece_far = hold(swap(piece, "tp", 2), got_early)
    first_part = width_of(hidden // 3, hidden)
    own_first = border_and_hidden(place, own, picks, w_heads, w_mlp_in, first_part, [own_early, piece])
    got_first = swap(own_first, "sx", 1)
    piece_far = hold(piece_far, own_first)
    near_far = swap(piece_far, "tp", 1)
    lower, upper = in_order(far, piece, piece_far), in_order(far, near, near_far)
    quarters = [part for pair_of in zip(lower, upper) for part in in_order(core, *pair_of)]
    other = jnp.concatenate(quarters, axis=1)
    terms = [got_early[:, 3 * edge + i : 3 * edge + i + 1].astype(F32) for i in range(6)]
    other = modulate(other, [terms[i] + terms[i + 1] + terms[i + 2] for i in (0, 3)])
    late_first = (1 - side) * edge
    other_late = [
        dot(other, lax.dynamic_slice(w_heads, (g, 0, late_first), (1, half_width, edge + head_dim))[0]).astype(BF16)
        for g in range(3)
    ]
    other_late = jnp.concatenate(other_late, axis=1)
    got_late = swap(other_late, "sx", 1)
    cut = tok_rows // 2
    own_heads, other_heads, other_border, own_rest, other_a, other_b = rest_of_first(
        place, own, other, picks, w_heads, w_mlp_in, first_part, cut, [other_late, got_first]
    )
    got_rest = swap(own_rest, "sx", 1)
    queries, keys_values, lower, upper = norm_units(
        place, (own_heads, got_late), (other_heads, got_early), (other_border, got_first), q_gain, k_gain, [other_a]
    )
    above = shift(lower, "sy", 1)
    below = shift(upper, "sy", -1)

    sent_mlp, kept_mlp, sent_attn, kept_attn = (
        lax.dynamic_slice_in_dim(w, start * block, block, 1)
        for w in (w_mlp_out, w_attn_out)
        for start in (1 - core, core)
    )

    def activate(mine, got, *earlier):
        got = hold(got, *earlier) if earlier else got
        return hold(jax.nn.gelu(mine.astype(F32) + got.astype(F32), approximate=True).astype(BF16))

    attended = attend(place, queries, keys_values, above, below, *window_codes(TILE), heads)
    got_attended = swap(attended, "sx", 1)
    got_other_a = swap(other_a, "sx", 1)
    got_own = jnp.concatenate([got_first[:tok_rows], hold(got_rest, attended)], axis=1)
    own_hidden = jnp.concatenate([own_first[:tok_rows], own_rest], axis=1)
    other_active = activate(jnp.concatenate([other_a, other_b], axis=0), got_own)
    other_sent, other_kept = dot(other_active, sent_mlp), dot(other_active, kept_mlp)
    got_other_b = swap(hold(other_b, other_sent), "sx", 1)

    def own_part(begin, end, got, *earlier):
        active, heads_part = activate(own_hidden[begin:end], got, *earlier), own_attended[begin:end]
        return (
            (dot(active, sent_mlp) + dot(heads_part, sent_attn)).astype(BF16),
            dot(active, kept_mlp) + dot(heads_part, kept_attn),
        )

    got_attended = hold(got_attended, other_sent, other_kept, got_other_a)
    here = edge + head_dim

    def natural(mine, middle, theirs):
        return jnp.concatenate(
            [jnp.where(side == 0, mine, theirs), middle, jnp.where(side == 0, theirs, mine)], axis=1
        )

    own_attended = natural(attended[:, :edge], attended[:, edge:here], got_attended[:, here:])
    other_attended = natural(attended[:, here:], got_attended[:, edge:here], got_attended[:, :edge])
    other_sent = (other_sent + dot(other_attended, sent_attn)).astype(BF16)
    other_kept = other_kept + dot(other_attended, kept_attn)
    other_come = swap(other_sent, "tp", 1)
    own_sent_a, own_kept_a = own_part(0, cut, got_other_a, other_sent, other_kept)

    def rows_of(half):
        kept = jnp.where(half == 0, other_kept[:cut], other_kept[cut:])
        return kept + jnp.where(half == 0, other_come[:cut], other_come[cut:]).astype(F32)

    passed = rows_of(1 - far).astype(BF16)
    passed = hold(swap(passed, "tp", 2), own_sent_a, own_kept_a)
    crossing = (rows_of(far) + passed.astype(F32)).astype(BF16)
    got = swap(crossing, "sx", 1)
    own_sum_a = own_kept_a + swap(own_sent_a, "tp", 1).astype(F32)
    come_a = swap(own_sum_a.astype(BF16), "tp", 2)
    own_sent_b, own_kept_b = own_part(cut, tok_rows, got_other_b, crossing)
    own_sum_b = hold(own_kept_b, got, come_a, cost=EARLY) + swap(own_sent_b, "tp", 1).astype(F32)

    home = far == side
    come_b = swap(jnp.where(home, got, own_sum_b.astype(BF16)), "tp", 2)
    wide = got.astype(F32)
    known = jnp.concatenate(
        [
            jnp.where(home, own_sum_a + come_a.astype(F32), jnp.where(far == 0, wide, 0.0)),
            jnp.where(home, own_sum_b, jnp.where(far == 0, 0.0, wide)),
        ],
        axis=0,
    )
    first_col = part * block
    gate_part = lax.dynamic_slice_in_dim(mod_gate, first_col, block, 0)
    residual_part = lax.dynamic_slice_in_dim(tokens, first_col, block, 1).astype(F32)
    known = hold(residual_part + gate_part * known)
    late_first = jnp.where(home, 1, 1 - far) * cut
    token = lax.broadcasted_iota(jnp.int32, (tok_rows, 1), 0)
    late = (token >= late_first) & (token < late_first + cut)
    late_part = jnp.concatenate([come_b, come_b], axis=0).astype(F32)
    return (known + jnp.where(late, gate_part * late_part, 0.0)).astype(BF16)


def shards(*arrays):
    local_heads = arrays[6].shape[0]
    if lax.axis_size("sx") == 2 and lax.axis_size("tp") == 4 and local_heads % 2 and local_heads > 1 and arrays[6].shape[1] == LANES:
        return paired_plan(*arrays)
    return gathered_plan(*arrays)


def solution(mesh):
    placed = (
        P(("sy", "sx"), None),
        P(),
        P(),
        P(),
        P("sx", None, "tp"),
        P("sx", "tp"),
        P("tp", None),
        P("tp", None),
        P("tp", "sx"),
        P("tp", "sx"),
    )
    return jax.shard_map(
        shards, mesh=mesh, in_specs=placed, out_specs=P(("sy", "sx"), "tp"), check_vma=False
    )
```

```python
import jax
import jax.numpy as jnp
import numpy as np
from jax import lax
from jax.experimental import pallas as pl
from jax.experimental.pallas import tpu as pltpu
from jax.sharding import PartitionSpec as P

TILE = 20


def with_halo(cells, sides, width):
    for axis, dim in sides:
        count = lax.axis_size(axis)
        ends = count - 1
        head = lax.slice_in_dim(cells, 0, width, axis=dim)
        tail = lax.slice_in_dim(cells, cells.shape[dim] - width, cells.shape[dim], axis=dim)
        cells = jnp.concatenate(
            [
                lax.ppermute(tail, axis, [(i, (i + 1) % count) for i in range(ends)]),
                cells,
                lax.ppermute(head, axis, [((i + 1) % count, i) for i in range(ends)]),
            ],
            axis=dim,
        )
    return cells


def layer_norm(vector):
    centered = vector - jnp.mean(vector, axis=-1, keepdims=True)
    variance = jnp.mean(centered * centered, axis=-1, keepdims=True)
    return centered * lax.rsqrt(variance + 1e-06)


def rms_gain(vector, scaling):
    mean_square = jnp.mean(vector * vector, axis=-1, keepdims=True)
    return vector * lax.rsqrt(mean_square + 1e-06) * scaling


def gathered_plan(
    tokens, mod_shift, mod_scale, mod_gate, w_qkv, w_mlp_in, q_gain, k_gain, w_attn_out, w_mlp_out
):
    tok_rows, model_width = tokens.shape
    tile_side = TILE
    half_side = TILE // 2
    inputs = tokens.astype(jnp.float32)
    modded = (layer_norm(inputs) * (1.0 + mod_scale) + mod_shift).astype(jnp.bfloat16)
    local_heads, head_dim = q_gain.shape
    local_width = local_heads * head_dim
    pieces = (
        lax.all_gather(w_qkv, "sx", axis=0, tiled=True),
        lax.all_gather(w_mlp_in, "sx", axis=0, tiled=True),
    )
    piece_rows = pieces[0].shape[0]
    qkv_sum = jnp.dot(
        modded, pieces[0].reshape(piece_rows, 3 * local_width), preferred_element_type=jnp.float32
    )
    mlp_sum = jnp.dot(modded, pieces[1], preferred_element_type=jnp.float32)
    qkv_parts = qkv_sum.reshape(tok_rows, 3, local_heads, head_dim)
    queries = rms_gain(qkv_parts[:, 0], q_gain).astype(jnp.bfloat16)
    key_rows = rms_gain(qkv_parts[:, 1], k_gain).astype(jnp.bfloat16)
    value_rows = qkv_parts[:, 2].astype(jnp.bfloat16)
    key_value = jnp.concatenate(
        [key_rows.reshape(tok_rows, local_width), value_rows.reshape(tok_rows, local_width)], axis=1
    )
    key_value = key_value.reshape(tile_side, tile_side, 2 * local_width)
    extended = with_halo(key_value, (("sy", 0), ("sx", 1)), half_side)
    window = extended.reshape(4 * tok_rows, 2 * local_width)
    window_keys = window[:, :local_width].reshape(4 * tok_rows, local_heads, head_dim)
    window_values = window[:, local_width:].reshape(4 * tok_rows, local_heads, head_dim)
    offsets = jnp.arange(2 * tile_side, dtype=jnp.int32)
    row_pos = lax.axis_index("sy") * tile_side - half_side + offsets
    col_pos = lax.axis_index("sx") * tile_side - half_side + offsets
    row_ok = (row_pos >= 0) & (row_pos < tile_side * lax.axis_size("sy"))
    col_ok = (col_pos >= 0) & (col_pos < tile_side * lax.axis_size("sx"))
    in_grid = (row_ok[:, None] & col_ok[None, :]).reshape(4 * tok_rows)
    scores = jnp.einsum(
        "qhd,khd->hqk", queries, window_keys, preferred_element_type=jnp.float32
    ) * head_dim ** (-0.5)
    scores = jnp.where(in_grid[None, None, :], scores, -jnp.inf)
    row_max = jnp.max(scores, axis=-1, keepdims=True)
    numerators = jnp.exp(scores - row_max)
    weights = (numerators / jnp.sum(numerators, axis=-1, keepdims=True)).astype(jnp.bfloat16)
    attended = jnp.einsum(
        "hqk,khd->qhd", weights, window_values, preferred_element_type=jnp.float32
    )
    attended = attended.astype(jnp.bfloat16).reshape(tok_rows, local_width)
    activated = jax.nn.gelu(mlp_sum, approximate=True).astype(jnp.bfloat16)
    pieces = (
        lax.all_gather(w_attn_out, "sx", axis=1, tiled=True),
        lax.all_gather(w_mlp_out, "sx", axis=1, tiled=True),
    )
    product_term = jnp.dot(attended, pieces[0], preferred_element_type=jnp.float32)
    product_term = product_term + jnp.dot(activated, pieces[1], preferred_element_type=jnp.float32)
    reduced = lax.psum_scatter(
        product_term.astype(jnp.bfloat16), "tp", scatter_dimension=1, tiled=True
    ).astype(jnp.float32)
    block_width = model_width // lax.axis_size("tp")
    first_col = lax.axis_index("tp") * block_width
    residual_part = lax.dynamic_slice_in_dim(inputs, first_col, block_width, 1)
    gate_part = lax.dynamic_slice_in_dim(mod_gate, first_col, block_width, 0)
    return (residual_part + gate_part * reduced).astype(jnp.bfloat16)


def swap(cells, axis, bit):
    count = lax.axis_size(axis)
    return lax.ppermute(cells, axis, [(i, i ^ bit) for i in range(count)])


def shift(cells, axis, step):
    count = lax.axis_size(axis)
    return lax.ppermute(
        cells, axis, [(i, i + step) for i in range(count) if 0 <= i + step < count]
    )


def dot(left, right):
    return jnp.dot(left, right, preferred_element_type=jnp.float32)


BF16, F32 = jnp.bfloat16, jnp.float32
LANES = 128
EARLY = 20_000_000
VMEM = 56
REST_VMEM = 40
POST_VMEM = 40


def width_of(total, most):
    return max(w for w in range(LANES, most + 1, LANES) if total % w == 0)


def call(body, grid, ins, outs, scratch=(), after=(), vmem=16, cost=(1000, 1000)):
    n_in, n_after = len(ins), len(after)

    def kernel(*refs):
        body(*refs[:n_in], *refs[n_in + n_after :])

    def spec(block, index):
        if block is None:
            return pl.BlockSpec(memory_space=index)
        return pl.BlockSpec(block, index)

    return pl.pallas_call(
        kernel,
        grid=(grid,),
        in_specs=[spec(b, i) for _, b, i in ins] + [pl.BlockSpec(memory_space=pl.ANY)] * n_after,
        out_specs=[spec(b, i) for _, _, b, i in outs],
        out_shape=[jax.ShapeDtypeStruct(s, d) for s, d, _, _ in outs],
        scratch_shapes=list(scratch),
        compiler_params=pltpu.CompilerParams(vmem_limit_bytes=vmem * 2**20),
        cost_estimate=pl.CostEstimate(flops=cost[0], bytes_accessed=cost[1], transcendentals=0),
    )(*[a for a, _, _ in ins], *after)


def in_order(bit, mine, other):
    return jnp.where(bit == 0, mine, other), jnp.where(bit == 0, other, mine)


def hold(cells, *earlier, cost=0):
    return pl.pallas_call(
        lambda *refs: None,
        in_specs=[pl.BlockSpec(memory_space=pl.ANY)] * (1 + len(earlier)),
        out_specs=pl.BlockSpec(memory_space=pl.ANY),
        out_shape=jax.ShapeDtypeStruct(cells.shape, cells.dtype),
        input_output_aliases={0: 0},
        compiler_params=pltpu.CompilerParams(vmem_limit_bytes=2**20),
        cost_estimate=pl.CostEstimate(flops=0, bytes_accessed=cost, transcendentals=0),
    )(cells, *earlier)


def at(*place):
    return lambda *_: place


def border_rows(tile_side):
    half = tile_side // 2
    return (half * half + 15) // 16 * 16


def border_picks(tile_side):
    half, rows = tile_side // 2, border_rows(tile_side)
    picks = np.zeros((2, 2 * rows, tile_side * tile_side), np.float32)
    for side in range(2):
        for low in range(2):
            for i in range(half):
                for j in range(half):
                    token = (low * half + i) * tile_side + j + (half if side == 0 else 0)
                    picks[side, low * rows + i * half + j, token] = 1
    return jnp.asarray(picks, BF16)


def token_block(rows):
    return max(b for b in range(16, LANES + 1, 16) if rows % b == 0)


def modulate_and_heads(place, tokens, scale_row, shift_row, w_heads, after=()):
    rows, model_width = tokens.shape
    depth, width = w_heads.shape[1:]
    edge = (width - LANES) // 2
    block = token_block(rows)

    def body(place_ref, tokens_ref, scale_ref, shift_ref, w_heads_ref, own_ref, out_ref, moments_ref):
        side = place_ref[0]
        cells = tokens_ref[...].astype(F32)
        mean = jnp.mean(cells, axis=-1, keepdims=True)
        centered = cells - mean
        scaling = lax.rsqrt(jnp.mean(centered * centered, axis=-1, keepdims=True) + 1e-06)
        some = pl.ds(pl.multiple_of(side * depth, LANES), depth)
        normed = (tokens_ref[:, some].astype(F32) - mean) * scaling
        own = (normed * (1.0 + scale_ref[:, some]) + shift_ref[:, some]).astype(BF16)
        own_ref[...] = own
        theirs = pl.ds(pl.multiple_of((1 - side) * (width - edge), LANES), edge)
        for g in range(3):
            out_ref[:, g * edge : (g + 1) * edge] = dot(own, w_heads_ref[g, :, theirs]).astype(BF16)
        lane = lax.broadcasted_iota(jnp.int32, (LANES, LANES), 1)
        mean, scaling = (jnp.pad(m, ((0, LANES - block), (0, 0))) for m in (mean, scaling))
        moments = jnp.where(lane == 0, mean, jnp.where(lane == 1, scaling, 0.0))
        moments_ref[0] = moments.T[:8]

    row = lambda i: (i, 0)
    return call(
        body, rows // block,
        [
            (place, None, pltpu.SMEM),
            (tokens, (block, model_width), row),
            (scale_row, scale_row.shape, at(0, 0)),
            (shift_row, shift_row.shape, at(0, 0)),
            (w_heads, w_heads.shape, at(0, 0, 0)),
        ],
        [
            ((rows, depth), BF16, (block, depth), row),
            ((rows, 3 * edge), BF16, (block, 3 * edge), row),
            ((rows // block, 8, LANES), F32, (1, 8, LANES), lambda i: (i, 0, 0)),
        ],
        after=after, vmem=VMEM,
    )


def border_and_hidden(place, own, picks, w_heads, hidden_weights, cut, after=()):
    rows, depth = own.shape
    half_border, width = picks.shape[1] // 2, w_heads.shape[2]

    def body(place_ref, own_ref, picks_ref, keys_ref, values_ref, w_ref, out_ref):
        taken = dot(picks_ref[place_ref[0]], own_ref[...]).astype(BF16)
        out_ref[:rows] = dot(own_ref[...], w_ref[...]).astype(BF16)
        for g, ref in enumerate((keys_ref, values_ref)):
            part = dot(taken, ref[0]).astype(BF16)
            out_ref[rows:, g * LANES : (g + 1) * LANES] = part[:half_border]
            out_ref[rows:, (2 + g) * LANES : (3 + g) * LANES] = part[half_border:]

    whole = at(0, 0)
    middle = (width - LANES) // 2 // LANES
    return call(
        body, 1,
        [(place, None, pltpu.SMEM), (own, own.shape, whole), (picks, picks.shape, at(0, 0, 0))]
        + [(w_heads, (1, depth, LANES), at(g, 0, middle)) for g in (1, 2)]
        + [(hidden_weights, (depth, cut), whole)],
        [((rows + half_border, cut), BF16, (rows + half_border, cut), whole)],
        after=after, vmem=VMEM,
    )[0]


def rest_of_first(place, own, other, picks, w_heads, hidden_weights, begin, cut, after=()):
    rows, depth = other.shape
    width, hidden = w_heads.shape[2], hidden_weights.shape[1]
    edge = (width - LANES) // 2
    border = picks.shape[1]
    block = width_of(begin, 512)
    parts = begin // block

    def body(
        place_ref, own_ref, other_ref, picks_ref, w_heads_ref, w_ref,
        qkv_ref, mine_ref, border_ref, rest_ref, a_ref, b_ref,
    ):
        side = place_ref[0]

        @pl.when(pl.program_id(0) == 0)
        def _():
            both = pl.ds(pl.multiple_of(side * edge, LANES), edge + LANES)
            mine = pl.ds(pl.multiple_of(side * (width - edge), LANES), edge)
            for g in range(3):
                qkv_ref[:, g * (edge + LANES) : (g + 1) * (edge + LANES)] = dot(own_ref[...], w_heads_ref[g, :, both])
                mine_ref[:, g * edge : (g + 1) * edge] = dot(other_ref[...], w_heads_ref[g, :, mine])
            taken = dot(picks_ref[1 - side], other_ref[...]).astype(BF16)
            for g in range(2):
                border_ref[:, g * LANES : (g + 1) * LANES] = dot(taken, w_heads_ref[1 + g, :, edge : edge + LANES])

        sums = dot(other_ref[...], w_ref[...])
        a_ref[...] = sums[:cut].astype(BF16)
        b_ref[...] = sums[cut:].astype(BF16)

        @pl.when(pl.program_id(0) >= parts)
        def _():
            rest_ref[...] = dot(own_ref[...], w_ref[...]).astype(BF16)

    whole = at(0, 0)
    column = lambda j: (0, j)
    out = lambda count, wide: ((count, wide), F32, (count, wide), whole)
    return call(
        body, hidden // block,
        [(place, None, pltpu.SMEM), (own, own.shape, whole), (other, other.shape, whole)]
        + [(a, a.shape, at(0, 0, 0)) for a in (picks, w_heads)]
        + [(hidden_weights, (depth, block), column)],
        [
            out(rows, 3 * (edge + LANES)),
            out(rows, 3 * edge),
            out(border, 2 * LANES),
            ((rows, hidden - begin), BF16, (rows, block), lambda j: (0, jnp.maximum(j - parts, 0))),
            ((cut, hidden), BF16, (cut, block), column),
            ((rows - cut, hidden), BF16, (rows - cut, block), column),
        ],
        after=after, vmem=REST_VMEM,
        cost=(
            2 * depth * (rows * 4 * width + border * 2 * LANES + rows * hidden),
            2 * depth * (2 * rows + 3 * width + hidden) + 12 * rows * width + 2 * rows * hidden,
        ),
    )


def norm_units(place, own, other, border, q_gain, k_gain, after=()):
    rows, heads, head_dim = own[0].shape[0], q_gain.shape[0], q_gain.shape[2]
    pair = heads // 2
    units = 2 * pair + 1
    half_border = border[0].shape[0] // 2
    sent_rows = (rows // 2 + 15) // 16 * 16
    sent = units * sent_rows + half_border

    def body(place_ref, *refs):
        own_refs, other_refs, border_refs = refs[:2], refs[2:4], refs[4:6]
        q_gain_ref, k_gain_ref, queries_ref, kv_ref, lower_ref, upper_ref = refs[6:]
        side = place_ref[0]
        first = side * (heads - pair)

        def head(two, index):
            some = pl.ds(pl.multiple_of(index * head_dim, LANES), head_dim)
            return sum(ref[:, some].astype(F32) for ref in two)

        def put(unit, two, p, count, index):
            q, k, v = (head(two, g * count + p) for g in range(3))
            kv = jnp.concatenate([rms_gain(k, k_gain_ref[index]), v], axis=1).astype(BF16)
            queries_ref[unit * rows : (unit + 1) * rows] = rms_gain(q, q_gain_ref[index]).astype(BF16)
            kv_ref[unit * rows : (unit + 1) * rows] = kv
            lower_ref[unit * sent_rows : (unit + 1) * sent_rows] = kv[rows - sent_rows :]
            upper_ref[unit * sent_rows : (unit + 1) * sent_rows] = kv[:sent_rows]

        for p in range(pair):
            put(2 * p, own_refs, side + p, pair + 1, first + p)
            put(2 * p + 1, other_refs, p, pair, first + p)
        put(2 * pair, own_refs, (1 - side) * pair, pair + 1, pair)
        got = border_refs[1][rows:].astype(F32)
        got = jnp.concatenate([got[:, : 2 * head_dim], got[:, 2 * head_dim : 4 * head_dim]], axis=0)
        both = border_refs[0][...] + got
        kv = [rms_gain(both[:, :head_dim], k_gain_ref[pair]), both[:, head_dim:]]
        kv = jnp.concatenate(kv, axis=1).astype(BF16)
        kv_ref[units * rows :] = kv
        upper_ref[units * sent_rows :] = kv[:half_border]
        lower_ref[units * sent_rows :] = kv[half_border:]

    whole = at(0, 0)
    out = lambda count, width: ((count, width), BF16, (count, width), whole)
    ins = [*own, *other, *border]
    return call(
        body, 1,
        [(place, None, pltpu.SMEM)]
        + [(a, a.shape, whole) for a in ins]
        + [(g, g.shape, at(0, 0, 0)) for g in (q_gain, k_gain)],
        [
            out(units * rows, head_dim),
            out(units * rows + 2 * half_border, 2 * head_dim),
            out(sent, 2 * head_dim),
            out(sent, 2 * head_dim),
        ],
        after=after, vmem=POST_VMEM,
    )


def window_codes(tile_side):
    rows, half = tile_side * tile_side, tile_side // 2
    sent_rows = (rows // 2 + 15) // 16 * 16
    extra = sent_rows - rows // 2
    column = np.arange(rows) % tile_side

    def lines(first, second):
        above = lambda on: np.concatenate([np.zeros(extra, np.int32), 2 * on[rows - rows // 2 :]])
        below = lambda on: np.concatenate([3 * on[: rows // 2], np.zeros(extra, np.int32)])
        return np.concatenate([first, second, above(first), above(second), below(first), below(second)])

    def padded(line):
        return np.pad(line, (0, -len(line) % LANES)).astype(np.float32)

    every = np.ones(rows, np.int32)
    right, left = (column >= half).astype(np.int32), (column < half).astype(np.int32)
    by_side = np.stack([
        np.stack([padded(lines(every, left)), padded(lines(right, every))]),
        np.stack([padded(lines(every, right)), padded(lines(left, every))]),
    ])
    pad = border_rows(tile_side)
    part = np.pad(np.ones(half * half, np.int32), (0, pad - half * half))
    above = np.concatenate([np.zeros(extra, np.int32), 2 * np.ones(rows // 2, np.int32), 2 * part])
    below = np.concatenate([3 * np.ones(rows // 2, np.int32), np.zeros(extra, np.int32), 3 * part])
    middle = padded(np.concatenate([every, part, part, above, below]))[None]
    return jnp.asarray(by_side), jnp.asarray(middle)


def attend(place, queries, keys_values, above, below, codes, middle_codes, heads, after=()):
    pair = heads // 2
    units = 2 * pair + 1
    head_dim = queries.shape[1]
    rows = queries.shape[0] // units
    border = keys_values.shape[0] - units * rows
    sent_rows = (above.shape[0] - border // 2) // units

    def body(place_ref, queries_ref, kv_ref, above_ref, below_ref, codes_ref, middle_ref, out_ref):
        side = place_ref[0]

        def unit_rows(ref, unit, count, size):
            return ref[unit * size : (unit + count) * size]

        def rest_rows(ref, size):
            return ref[units * size :]

        def one(unit, blocks, line, column):
            there = (line == 1) | ((line == 2) & (place_ref[2] == 1)) | ((line == 3) & (place_ref[3] == 1))
            line = jnp.where(there, 0.0, -jnp.inf)
            spare = line.shape[1] - sum(b.shape[0] for b in blocks)
            if spare:
                blocks = blocks + [jnp.zeros((spare, 2 * head_dim), BF16)]
            both = jnp.concatenate(blocks, axis=0)
            keys, values = both[:, :head_dim], both[:, head_dim:]
            mine = unit_rows(queries_ref, unit, 1, rows)
            scores = lax.dot_general(mine, keys, (((1,), (1,)), ((), ())), preferred_element_type=F32)
            scores = scores * head_dim ** (-0.5) + line
            numerators = jnp.exp(scores - jnp.max(scores, axis=-1, keepdims=True))
            total = jnp.sum(numerators, axis=-1, keepdims=True)
            got = (dot(numerators.astype(BF16), values) / total).astype(BF16)
            out_ref[:, column * head_dim : (column + 1) * head_dim] = got

        for p in range(pair):
            blocks = [
                unit_rows(kv_ref, 2 * p, 2, rows),
                unit_rows(above_ref, 2 * p, 2, sent_rows),
                unit_rows(below_ref, 2 * p, 2, sent_rows),
            ]
            one(2 * p, blocks, codes_ref[side][0:1], p)
            one(2 * p + 1, blocks, codes_ref[side][1:2], pair + 1 + p)
        blocks = [
            kv_ref[2 * pair * rows :],
            above_ref[2 * pair * sent_rows :],
            below_ref[2 * pair * sent_rows :],
        ]
        one(2 * pair, blocks, middle_ref[...], pair)

    ins = [queries, keys_values, above, below, middle_codes]
    whole = [(a, a.shape, at(0, 0)) for a in ins]
    return call(
        body, 1,
        [(place, None, pltpu.SMEM)] + whole[:4] + [(codes, codes.shape, at(0, 0, 0))] + whole[4:],
        [((rows, units * head_dim), BF16, (rows, units * head_dim), at(0, 0))],
        after=after, vmem=POST_VMEM,
    )[0]


def paired_plan(
    tokens, mod_shift, mod_scale, mod_gate, w_qkv, w_mlp_in, q_gain, k_gain, w_attn_out, w_mlp_out
):
    tok_rows, model_width = tokens.shape
    half_width, hidden = w_mlp_in.shape
    heads, head_dim = q_gain.shape
    width = heads * head_dim
    side = lax.axis_index("sx")
    part = lax.axis_index("tp")
    core, far = part % 2, part // 2
    mid = hidden // 2
    block = half_width // 2
    row = lax.axis_index("sy")
    place = jnp.stack([side, core, row > 0, row < lax.axis_size("sy") - 1]).astype(jnp.int32)
    picks = border_picks(TILE)
    q_gain, k_gain = q_gain[:, None, :], k_gain[:, None, :]

    quarter = half_width // 4
    other_first = (1 - side) * half_width + part * quarter
    sent = lax.dynamic_slice_in_dim(lax.optimization_barrier(tokens), other_first, quarter, 1)
    piece = swap(sent, "sx", 1)
    first = side * half_width
    gain_part = 1.0 + lax.dynamic_slice_in_dim(mod_scale, first, half_width, 0)
    shift_part = lax.dynamic_slice_in_dim(mod_shift, first, half_width, 0)

    def modulate(cells, pair):
        cells = (cells.astype(F32) - pair[0]) * pair[1]
        return (cells * gain_part + shift_part).astype(BF16)

    pair = heads // 2
    edge = pair * head_dim
    w_heads = jnp.transpose(w_qkv, (1, 0, 2))

    own, own_early, moments = modulate_and_heads(place, tokens, mod_scale[None], mod_shift[None], w_heads, [sent])
    got_early, got_moments = swap(own_early, "sx", 1), swap(moments, "sx", 1)
    piece = hold(piece, own_early)
    near = swap(piece, "tp", 1)
    piece_far = hold(swap(piece, "tp", 2), got_early, got_moments)
    first_part = width_of(hidden // 3, hidden)
    own_first = border_and_hidden(place, own, picks, w_heads, w_mlp_in, first_part, [own_early, piece])
    got_first = swap(own_first, "sx", 1)
    piece_far = hold(piece_far, own_first)
    near_far = swap(piece_far, "tp", 1)
    lower, upper = in_order(far, piece, piece_far), in_order(far, near, near_far)
    quarters = [part for pair_of in zip(lower, upper) for part in in_order(core, *pair_of)]
    other = jnp.concatenate(quarters, axis=1)
    other = modulate(other, [got_moments[:, i, : token_block(tok_rows)].reshape(tok_rows, 1) for i in range(2)])
    late_first = (1 - side) * edge
    other_late = [
        dot(other, lax.dynamic_slice(w_heads, (g, 0, late_first), (1, half_width, edge + head_dim))[0]).astype(BF16)
        for g in range(3)
    ]
    other_late = jnp.concatenate(other_late, axis=1)
    got_late = swap(other_late, "sx", 1)
    cut = tok_rows // 2
    own_heads, other_heads, other_border, own_rest, other_a, other_b = rest_of_first(
        place, own, other, picks, w_heads, w_mlp_in, first_part, cut, [other_late, got_first]
    )
    got_rest = swap(own_rest, "sx", 1)
    queries, keys_values, lower, upper = norm_units(
        place, (own_heads, got_late), (other_heads, got_early), (other_border, got_first), q_gain, k_gain, [other_a]
    )
    above = shift(lower, "sy", 1)
    below = shift(upper, "sy", -1)

    sent_mlp, kept_mlp, sent_attn, kept_attn = (
        lax.dynamic_slice_in_dim(w, start * block, block, 1)
        for w in (w_mlp_out, w_attn_out)
        for start in (1 - core, core)
    )

    def activate(mine, got, *earlier):
        got = hold(got, *earlier) if earlier else got
        return hold(jax.nn.gelu(mine.astype(F32) + got.astype(F32), approximate=True).astype(BF16))

    attended = attend(place, queries, keys_values, above, below, *window_codes(TILE), heads)
    got_attended = swap(attended, "sx", 1)
    got_other_a = swap(other_a, "sx", 1)
    got_own = jnp.concatenate([got_first[:tok_rows], hold(got_rest, attended)], axis=1)
    own_hidden = jnp.concatenate([own_first[:tok_rows], own_rest], axis=1)
    other_active = activate(jnp.concatenate([other_a, other_b], axis=0), got_own)
    other_sent, other_kept = dot(other_active, sent_mlp), dot(other_active, kept_mlp)
    got_other_b = swap(hold(other_b, other_sent), "sx", 1)

    def own_part(begin, end, got, *earlier):
        active, heads_part = activate(own_hidden[begin:end], got, *earlier), own_attended[begin:end]
        return (
            (dot(active, sent_mlp) + dot(heads_part, sent_attn)).astype(BF16),
            dot(active, kept_mlp) + dot(heads_part, kept_attn),
        )

    got_attended = hold(got_attended, other_sent, other_kept, got_other_a)
    here = edge + head_dim

    def natural(mine, middle, theirs):
        return jnp.concatenate(
            [jnp.where(side == 0, mine, theirs), middle, jnp.where(side == 0, theirs, mine)], axis=1
        )

    own_attended = natural(attended[:, :edge], attended[:, edge:here], got_attended[:, here:])
    other_attended = natural(attended[:, here:], got_attended[:, edge:here], got_attended[:, :edge])
    other_sent = (other_sent + dot(other_attended, sent_attn)).astype(BF16)
    other_kept = other_kept + dot(other_attended, kept_attn)
    other_come = swap(other_sent, "tp", 1)
    own_sent_a, own_kept_a = own_part(0, cut, got_other_a, other_sent, other_kept)

    def rows_of(half):
        kept = jnp.where(half == 0, other_kept[:cut], other_kept[cut:])
        return kept + jnp.where(half == 0, other_come[:cut], other_come[cut:]).astype(F32)

    passed = rows_of(1 - far).astype(BF16)
    passed = hold(swap(passed, "tp", 2), own_sent_a, own_kept_a)
    crossing = (rows_of(far) + passed.astype(F32)).astype(BF16)
    got = swap(crossing, "sx", 1)
    own_sum_a = own_kept_a + swap(own_sent_a, "tp", 1).astype(F32)
    come_a = swap(own_sum_a.astype(BF16), "tp", 2)
    own_sent_b, own_kept_b = own_part(cut, tok_rows, got_other_b, crossing)
    own_sum_b = hold(own_kept_b, got, come_a, cost=EARLY) + swap(own_sent_b, "tp", 1).astype(F32)

    home = far == side
    come_b = swap(jnp.where(home, got, own_sum_b.astype(BF16)), "tp", 2)
    wide = got.astype(F32)
    known = jnp.concatenate(
        [
            jnp.where(home, own_sum_a + come_a.astype(F32), jnp.where(far == 0, wide, 0.0)),
            jnp.where(home, own_sum_b, jnp.where(far == 0, 0.0, wide)),
        ],
        axis=0,
    )
    first_col = part * block
    gate_part = lax.dynamic_slice_in_dim(mod_gate, first_col, block, 0)
    residual_part = lax.dynamic_slice_in_dim(tokens, first_col, block, 1).astype(F32)
    known = hold(residual_part + gate_part * known)
    late_first = jnp.where(home, 1, 1 - far) * cut
    token = lax.broadcasted_iota(jnp.int32, (tok_rows, 1), 0)
    late = (token >= late_first) & (token < late_first + cut)
    late_part = jnp.concatenate([come_b, come_b], axis=0).astype(F32)
    return (known + jnp.where(late, gate_part * late_part, 0.0)).astype(BF16)


def shards(*arrays):
    local_heads = arrays[6].shape[0]
    if lax.axis_size("sx") == 2 and lax.axis_size("tp") == 4 and local_heads % 2 and local_heads > 1 and arrays[6].shape[1] == LANES:
        return paired_plan(*arrays)
    return gathered_plan(*arrays)


def solution(mesh):
    placed = (
        P(("sy", "sx"), None),
        P(),
        P(),
        P(),
        P("sx", None, "tp"),
        P("sx", "tp"),
        P("tp", None),
        P("tp", None),
        P("tp", "sx"),
        P("tp", "sx"),
    )
    return jax.shard_map(
        shards, mesh=mesh, in_specs=placed, out_specs=P(("sy", "sx"), "tp"), check_vma=False
    )
```

```python
import jax
import jax.numpy as jnp
import numpy as np
from jax import lax
from jax.experimental import pallas as pl
from jax.experimental.pallas import tpu as pltpu
from jax.sharding import PartitionSpec as P

TILE = 20


def with_halo(cells, sides, width):
    for axis, dim in sides:
        count = lax.axis_size(axis)
        ends = count - 1
        head = lax.slice_in_dim(cells, 0, width, axis=dim)
        tail = lax.slice_in_dim(cells, cells.shape[dim] - width, cells.shape[dim], axis=dim)
        cells = jnp.concatenate(
            [
                lax.ppermute(tail, axis, [(i, (i + 1) % count) for i in range(ends)]),
                cells,
                lax.ppermute(head, axis, [((i + 1) % count, i) for i in range(ends)]),
            ],
            axis=dim,
        )
    return cells


def layer_norm(vector):
    centered = vector - jnp.mean(vector, axis=-1, keepdims=True)
    variance = jnp.mean(centered * centered, axis=-1, keepdims=True)
    return centered * lax.rsqrt(variance + 1e-06)


def rms_gain(vector, scaling):
    mean_square = jnp.mean(vector * vector, axis=-1, keepdims=True)
    return vector * lax.rsqrt(mean_square + 1e-06) * scaling


def gathered_plan(
    tokens, mod_shift, mod_scale, mod_gate, w_qkv, w_mlp_in, q_gain, k_gain, w_attn_out, w_mlp_out
):
    tok_rows, model_width = tokens.shape
    tile_side = TILE
    half_side = TILE // 2
    inputs = tokens.astype(jnp.float32)
    modded = (layer_norm(inputs) * (1.0 + mod_scale) + mod_shift).astype(jnp.bfloat16)
    local_heads, head_dim = q_gain.shape
    local_width = local_heads * head_dim
    pieces = (
        lax.all_gather(w_qkv, "sx", axis=0, tiled=True),
        lax.all_gather(w_mlp_in, "sx", axis=0, tiled=True),
    )
    piece_rows = pieces[0].shape[0]
    qkv_sum = jnp.dot(
        modded, pieces[0].reshape(piece_rows, 3 * local_width), preferred_element_type=jnp.float32
    )
    mlp_sum = jnp.dot(modded, pieces[1], preferred_element_type=jnp.float32)
    qkv_parts = qkv_sum.reshape(tok_rows, 3, local_heads, head_dim)
    queries = rms_gain(qkv_parts[:, 0], q_gain).astype(jnp.bfloat16)
    key_rows = rms_gain(qkv_parts[:, 1], k_gain).astype(jnp.bfloat16)
    value_rows = qkv_parts[:, 2].astype(jnp.bfloat16)
    key_value = jnp.concatenate(
        [key_rows.reshape(tok_rows, local_width), value_rows.reshape(tok_rows, local_width)], axis=1
    )
    key_value = key_value.reshape(tile_side, tile_side, 2 * local_width)
    extended = with_halo(key_value, (("sy", 0), ("sx", 1)), half_side)
    window = extended.reshape(4 * tok_rows, 2 * local_width)
    window_keys = window[:, :local_width].reshape(4 * tok_rows, local_heads, head_dim)
    window_values = window[:, local_width:].reshape(4 * tok_rows, local_heads, head_dim)
    offsets = jnp.arange(2 * tile_side, dtype=jnp.int32)
    row_pos = lax.axis_index("sy") * tile_side - half_side + offsets
    col_pos = lax.axis_index("sx") * tile_side - half_side + offsets
    row_ok = (row_pos >= 0) & (row_pos < tile_side * lax.axis_size("sy"))
    col_ok = (col_pos >= 0) & (col_pos < tile_side * lax.axis_size("sx"))
    in_grid = (row_ok[:, None] & col_ok[None, :]).reshape(4 * tok_rows)
    scores = jnp.einsum(
        "qhd,khd->hqk", queries, window_keys, preferred_element_type=jnp.float32
    ) * head_dim ** (-0.5)
    scores = jnp.where(in_grid[None, None, :], scores, -jnp.inf)
    row_max = jnp.max(scores, axis=-1, keepdims=True)
    numerators = jnp.exp(scores - row_max)
    weights = (numerators / jnp.sum(numerators, axis=-1, keepdims=True)).astype(jnp.bfloat16)
    attended = jnp.einsum(
        "hqk,khd->qhd", weights, window_values, preferred_element_type=jnp.float32
    )
    attended = attended.astype(jnp.bfloat16).reshape(tok_rows, local_width)
    activated = jax.nn.gelu(mlp_sum, approximate=True).astype(jnp.bfloat16)
    pieces = (
        lax.all_gather(w_attn_out, "sx", axis=1, tiled=True),
        lax.all_gather(w_mlp_out, "sx", axis=1, tiled=True),
    )
    product_term = jnp.dot(attended, pieces[0], preferred_element_type=jnp.float32)
    product_term = product_term + jnp.dot(activated, pieces[1], preferred_element_type=jnp.float32)
    reduced = lax.psum_scatter(
        product_term.astype(jnp.bfloat16), "tp", scatter_dimension=1, tiled=True
    ).astype(jnp.float32)
    block_width = model_width // lax.axis_size("tp")
    first_col = lax.axis_index("tp") * block_width
    residual_part = lax.dynamic_slice_in_dim(inputs, first_col, block_width, 1)
    gate_part = lax.dynamic_slice_in_dim(mod_gate, first_col, block_width, 0)
    return (residual_part + gate_part * reduced).astype(jnp.bfloat16)


def swap(cells, axis, bit):
    count = lax.axis_size(axis)
    return lax.ppermute(cells, axis, [(i, i ^ bit) for i in range(count)])


def shift(cells, axis, step):
    count = lax.axis_size(axis)
    return lax.ppermute(
        cells, axis, [(i, i + step) for i in range(count) if 0 <= i + step < count]
    )


def dot(left, right):
    return jnp.dot(left, right, preferred_element_type=jnp.float32)


BF16, F32 = jnp.bfloat16, jnp.float32
LANES = 128
EARLY = 20_000_000
VMEM = 56
REST_VMEM = 40
POST_VMEM = 40


def width_of(total, most):
    return max(w for w in range(LANES, most + 1, LANES) if total % w == 0)


def call(body, grid, ins, outs, scratch=(), after=(), vmem=16, cost=(1000, 1000)):
    n_in, n_after = len(ins), len(after)

    def kernel(*refs):
        body(*refs[:n_in], *refs[n_in + n_after :])

    def spec(block, index):
        if block is None:
            return pl.BlockSpec(memory_space=index)
        return pl.BlockSpec(block, index)

    return pl.pallas_call(
        kernel,
        grid=(grid,),
        in_specs=[spec(b, i) for _, b, i in ins] + [pl.BlockSpec(memory_space=pl.ANY)] * n_after,
        out_specs=[spec(b, i) for _, _, b, i in outs],
        out_shape=[jax.ShapeDtypeStruct(s, d) for s, d, _, _ in outs],
        scratch_shapes=list(scratch),
        compiler_params=pltpu.CompilerParams(vmem_limit_bytes=vmem * 2**20),
        cost_estimate=pl.CostEstimate(flops=cost[0], bytes_accessed=cost[1], transcendentals=0),
    )(*[a for a, _, _ in ins], *after)


def in_order(bit, mine, other):
    return jnp.where(bit == 0, mine, other), jnp.where(bit == 0, other, mine)


def hold(cells, *earlier, cost=0):
    return pl.pallas_call(
        lambda *refs: None,
        in_specs=[pl.BlockSpec(memory_space=pl.ANY)] * (1 + len(earlier)),
        out_specs=pl.BlockSpec(memory_space=pl.ANY),
        out_shape=jax.ShapeDtypeStruct(cells.shape, cells.dtype),
        input_output_aliases={0: 0},
        compiler_params=pltpu.CompilerParams(vmem_limit_bytes=2**20),
        cost_estimate=pl.CostEstimate(flops=0, bytes_accessed=cost, transcendentals=0),
    )(cells, *earlier)


def at(*place):
    return lambda *_: place


def border_rows(tile_side):
    half = tile_side // 2
    return (half * half + 15) // 16 * 16


def border_picks(tile_side):
    half, rows = tile_side // 2, border_rows(tile_side)
    picks = np.zeros((2, 2 * rows, tile_side * tile_side), np.float32)
    for side in range(2):
        for low in range(2):
            for i in range(half):
                for j in range(half):
                    token = (low * half + i) * tile_side + j + (half if side == 0 else 0)
                    picks[side, low * rows + i * half + j, token] = 1
    return jnp.asarray(picks, BF16)


def token_block(rows):
    return max(b for b in range(16, LANES + 1, 16) if rows % b == 0)


def modulate_and_heads(tokens, scale_row, shift_row, w_heads, after=()):
    rows, model_width = tokens.shape
    depth, width = w_heads.shape[1:]
    edge = (width - LANES) // 2
    block = token_block(rows)

    def body(tokens_ref, scale_ref, shift_ref, w_heads_ref, own_ref, out_ref, moments_ref):
        side = lax.axis_index("sx")
        cells = tokens_ref[...].astype(F32)
        mean = jnp.mean(cells, axis=-1, keepdims=True)
        centered = cells - mean
        scaling = lax.rsqrt(jnp.mean(centered * centered, axis=-1, keepdims=True) + 1e-06)
        some = pl.ds(pl.multiple_of(side * depth, LANES), depth)
        normed = (tokens_ref[:, some].astype(F32) - mean) * scaling
        own = (normed * (1.0 + scale_ref[:, some]) + shift_ref[:, some]).astype(BF16)
        own_ref[...] = own
        theirs = pl.ds(pl.multiple_of((1 - side) * (width - edge), LANES), edge)
        for g in range(3):
            out_ref[:, g * edge : (g + 1) * edge] = dot(own, w_heads_ref[g, :, theirs]).astype(BF16)
        lane = lax.broadcasted_iota(jnp.int32, (LANES, LANES), 1)
        mean, scaling = (jnp.pad(m, ((0, LANES - block), (0, 0))) for m in (mean, scaling))
        moments = jnp.where(lane == 0, mean, jnp.where(lane == 1, scaling, 0.0))
        moments_ref[0] = moments.T[:8]

    row = lambda i: (i, 0)
    return call(
        body, rows // block,
        [
            (tokens, (block, model_width), row),
            (scale_row, scale_row.shape, at(0, 0)),
            (shift_row, shift_row.shape, at(0, 0)),
            (w_heads, w_heads.shape, at(0, 0, 0)),
        ],
        [
            ((rows, depth), BF16, (block, depth), row),
            ((rows, 3 * edge), BF16, (block, 3 * edge), row),
            ((rows // block, 8, LANES), F32, (1, 8, LANES), lambda i: (i, 0, 0)),
        ],
        after=after, vmem=VMEM,
    )


def border_and_hidden(own, picks, w_heads, hidden_weights, cut, after=()):
    rows, depth = own.shape
    half_border, width = picks.shape[1] // 2, w_heads.shape[2]

    def body(own_ref, picks_ref, keys_ref, values_ref, w_ref, out_ref):
        taken = dot(picks_ref[lax.axis_index("sx")], own_ref[...]).astype(BF16)
        out_ref[:rows] = dot(own_ref[...], w_ref[...]).astype(BF16)
        for g, ref in enumerate((keys_ref, values_ref)):
            part = dot(taken, ref[0]).astype(BF16)
            out_ref[rows:, g * LANES : (g + 1) * LANES] = part[:half_border]
            out_ref[rows:, (2 + g) * LANES : (3 + g) * LANES] = part[half_border:]

    whole = at(0, 0)
    middle = (width - LANES) // 2 // LANES
    return call(
        body, 1,
        [(own, own.shape, whole), (picks, picks.shape, at(0, 0, 0))]
        + [(w_heads, (1, depth, LANES), at(g, 0, middle)) for g in (1, 2)]
        + [(hidden_weights, (depth, cut), whole)],
        [((rows + half_border, cut), BF16, (rows + half_border, cut), whole)],
        after=after, vmem=VMEM,
    )[0]


def rest_of_first(place, own, other, picks, w_heads, hidden_weights, begin, cut, after=()):
    rows, depth = other.shape
    width, hidden = w_heads.shape[2], hidden_weights.shape[1]
    edge = (width - LANES) // 2
    border = picks.shape[1]
    block = width_of(begin, 512)
    parts = begin // block

    def body(
        place_ref, own_ref, other_ref, picks_ref, w_heads_ref, w_ref,
        qkv_ref, mine_ref, border_ref, rest_ref, a_ref, b_ref,
    ):
        side = place_ref[0]

        @pl.when(pl.program_id(0) == 0)
        def _():
            both = pl.ds(pl.multiple_of(side * edge, LANES), edge + LANES)
            mine = pl.ds(pl.multiple_of(side * (width - edge), LANES), edge)
            for g in range(3):
                qkv_ref[:, g * (edge + LANES) : (g + 1) * (edge + LANES)] = dot(own_ref[...], w_heads_ref[g, :, both])
                mine_ref[:, g * edge : (g + 1) * edge] = dot(other_ref[...], w_heads_ref[g, :, mine])
            taken = dot(picks_ref[1 - side], other_ref[...]).astype(BF16)
            for g in range(2):
                border_ref[:, g * LANES : (g + 1) * LANES] = dot(taken, w_heads_ref[1 + g, :, edge : edge + LANES])

        sums = dot(other_ref[...], w_ref[...])
        a_ref[...] = sums[:cut].astype(BF16)
        b_ref[...] = sums[cut:].astype(BF16)

        @pl.when(pl.program_id(0) >= parts)
        def _():
            rest_ref[...] = dot(own_ref[...], w_ref[...]).astype(BF16)

    whole = at(0, 0)
    column = lambda j: (0, j)
    out = lambda count, wide: ((count, wide), F32, (count, wide), whole)
    return call(
        body, hidden // block,
        [(place, None, pltpu.SMEM), (own, own.shape, whole), (other, other.shape, whole)]
        + [(a, a.shape, at(0, 0, 0)) for a in (picks, w_heads)]
        + [(hidden_weights, (depth, block), column)],
        [
            out(rows, 3 * (edge + LANES)),
            out(rows, 3 * edge),
            out(border, 2 * LANES),
            ((rows, hidden - begin), BF16, (rows, block), lambda j: (0, jnp.maximum(j - parts, 0))),
            ((cut, hidden), BF16, (cut, block), column),
            ((rows - cut, hidden), BF16, (rows - cut, block), column),
        ],
        after=after, vmem=REST_VMEM,
        cost=(
            2 * depth * (rows * 4 * width + border * 2 * LANES + rows * hidden),
            2 * depth * (2 * rows + 3 * width + hidden) + 12 * rows * width + 2 * rows * hidden,
        ),
    )


def norm_units(place, own, other, border, q_gain, k_gain, after=()):
    rows, heads, head_dim = own[0].shape[0], q_gain.shape[0], q_gain.shape[2]
    pair = heads // 2
    units = 2 * pair + 1
    half_border = border[0].shape[0] // 2
    sent_rows = (rows // 2 + 15) // 16 * 16
    sent = units * sent_rows + half_border

    def body(place_ref, *refs):
        own_refs, other_refs, border_refs = refs[:2], refs[2:4], refs[4:6]
        q_gain_ref, k_gain_ref, queries_ref, kv_ref, lower_ref, upper_ref = refs[6:]
        side = place_ref[0]
        first = side * (heads - pair)

        def head(two, index):
            some = pl.ds(pl.multiple_of(index * head_dim, LANES), head_dim)
            return sum(ref[:, some].astype(F32) for ref in two)

        def put(unit, two, p, count, index):
            q, k, v = (head(two, g * count + p) for g in range(3))
            kv = jnp.concatenate([rms_gain(k, k_gain_ref[index]), v], axis=1).astype(BF16)
            queries_ref[unit * rows : (unit + 1) * rows] = rms_gain(q, q_gain_ref[index]).astype(BF16)
            kv_ref[unit * rows : (unit + 1) * rows] = kv
            lower_ref[unit * sent_rows : (unit + 1) * sent_rows] = kv[rows - sent_rows :]
            upper_ref[unit * sent_rows : (unit + 1) * sent_rows] = kv[:sent_rows]

        for p in range(pair):
            put(2 * p, own_refs, side + p, pair + 1, first + p)
            put(2 * p + 1, other_refs, p, pair, first + p)
        put(2 * pair, own_refs, (1 - side) * pair, pair + 1, pair)
        got = border_refs[1][rows:].astype(F32)
        got = jnp.concatenate([got[:, : 2 * head_dim], got[:, 2 * head_dim : 4 * head_dim]], axis=0)
        both = border_refs[0][...] + got
        kv = [rms_gain(both[:, :head_dim], k_gain_ref[pair]), both[:, head_dim:]]
        kv = jnp.concatenate(kv, axis=1).astype(BF16)
        kv_ref[units * rows :] = kv
        upper_ref[units * sent_rows :] = kv[:half_border]
        lower_ref[units * sent_rows :] = kv[half_border:]

    whole = at(0, 0)
    out = lambda count, width: ((count, width), BF16, (count, width), whole)
    ins = [*own, *other, *border]
    return call(
        body, 1,
        [(place, None, pltpu.SMEM)]
        + [(a, a.shape, whole) for a in ins]
        + [(g, g.shape, at(0, 0, 0)) for g in (q_gain, k_gain)],
        [
            out(units * rows, head_dim),
            out(units * rows + 2 * half_border, 2 * head_dim),
            out(sent, 2 * head_dim),
            out(sent, 2 * head_dim),
        ],
        after=after, vmem=POST_VMEM,
    )


def window_codes(tile_side):
    rows, half = tile_side * tile_side, tile_side // 2
    sent_rows = (rows // 2 + 15) // 16 * 16
    extra = sent_rows - rows // 2
    column = np.arange(rows) % tile_side

    def lines(first, second):
        above = lambda on: np.concatenate([np.zeros(extra, np.int32), 2 * on[rows - rows // 2 :]])
        below = lambda on: np.concatenate([3 * on[: rows // 2], np.zeros(extra, np.int32)])
        return np.concatenate([first, second, above(first), above(second), below(first), below(second)])

    def padded(line):
        return np.pad(line, (0, -len(line) % LANES)).astype(np.float32)

    every = np.ones(rows, np.int32)
    right, left = (column >= half).astype(np.int32), (column < half).astype(np.int32)
    by_side = np.stack([
        np.stack([padded(lines(every, left)), padded(lines(right, every))]),
        np.stack([padded(lines(every, right)), padded(lines(left, every))]),
    ])
    pad = border_rows(tile_side)
    part = np.pad(np.ones(half * half, np.int32), (0, pad - half * half))
    above = np.concatenate([np.zeros(extra, np.int32), 2 * np.ones(rows // 2, np.int32), 2 * part])
    below = np.concatenate([3 * np.ones(rows // 2, np.int32), np.zeros(extra, np.int32), 3 * part])
    middle = padded(np.concatenate([every, part, part, above, below]))[None]
    return jnp.asarray(by_side), jnp.asarray(middle)


def attend(place, queries, keys_values, above, below, codes, middle_codes, heads, after=()):
    pair = heads // 2
    units = 2 * pair + 1
    head_dim = queries.shape[1]
    rows = queries.shape[0] // units
    border = keys_values.shape[0] - units * rows
    sent_rows = (above.shape[0] - border // 2) // units

    def body(place_ref, queries_ref, kv_ref, above_ref, below_ref, codes_ref, middle_ref, out_ref):
        side = place_ref[0]

        def unit_rows(ref, unit, count, size):
            return ref[unit * size : (unit + count) * size]

        def rest_rows(ref, size):
            return ref[units * size :]

        def one(unit, blocks, line, column):
            there = (line == 1) | ((line == 2) & (place_ref[2] == 1)) | ((line == 3) & (place_ref[3] == 1))
            line = jnp.where(there, 0.0, -jnp.inf)
            spare = line.shape[1] - sum(b.shape[0] for b in blocks)
            if spare:
                blocks = blocks + [jnp.zeros((spare, 2 * head_dim), BF16)]
            both = jnp.concatenate(blocks, axis=0)
            keys, values = both[:, :head_dim], both[:, head_dim:]
            mine = unit_rows(queries_ref, unit, 1, rows)
            scores = lax.dot_general(mine, keys, (((1,), (1,)), ((), ())), preferred_element_type=F32)
            scores = scores * head_dim ** (-0.5) + line
            numerators = jnp.exp(scores - jnp.max(scores, axis=-1, keepdims=True))
            total = jnp.sum(numerators, axis=-1, keepdims=True)
            got = (dot(numerators.astype(BF16), values) / total).astype(BF16)
            out_ref[:, column * head_dim : (column + 1) * head_dim] = got

        for p in range(pair):
            blocks = [
                unit_rows(kv_ref, 2 * p, 2, rows),
                unit_rows(above_ref, 2 * p, 2, sent_rows),
                unit_rows(below_ref, 2 * p, 2, sent_rows),
            ]
            one(2 * p, blocks, codes_ref[side][0:1], p)
            one(2 * p + 1, blocks, codes_ref[side][1:2], pair + 1 + p)
        blocks = [
            kv_ref[2 * pair * rows :],
            above_ref[2 * pair * sent_rows :],
            below_ref[2 * pair * sent_rows :],
        ]
        one(2 * pair, blocks, middle_ref[...], pair)

    ins = [queries, keys_values, above, below, middle_codes]
    whole = [(a, a.shape, at(0, 0)) for a in ins]
    return call(
        body, 1,
        [(place, None, pltpu.SMEM)] + whole[:4] + [(codes, codes.shape, at(0, 0, 0))] + whole[4:],
        [((rows, units * head_dim), BF16, (rows, units * head_dim), at(0, 0))],
        after=after, vmem=POST_VMEM,
    )[0]


def paired_plan(
    tokens, mod_shift, mod_scale, mod_gate, w_qkv, w_mlp_in, q_gain, k_gain, w_attn_out, w_mlp_out
):
    tok_rows, model_width = tokens.shape
    half_width, hidden = w_mlp_in.shape
    heads, head_dim = q_gain.shape
    width = heads * head_dim
    side = lax.axis_index("sx")
    part = lax.axis_index("tp")
    core, far = part % 2, part // 2
    mid = hidden // 2
    block = half_width // 2
    row = lax.axis_index("sy")
    place = jnp.stack([side, core, row > 0, row < lax.axis_size("sy") - 1]).astype(jnp.int32)
    picks = border_picks(TILE)
    q_gain, k_gain = q_gain[:, None, :], k_gain[:, None, :]

    quarter = half_width // 4
    other_first = (1 - side) * half_width + part * quarter
    sent = lax.dynamic_slice_in_dim(lax.optimization_barrier(tokens), other_first, quarter, 1)
    piece = swap(sent, "sx", 1)
    first = side * half_width
    gain_part = 1.0 + lax.dynamic_slice_in_dim(mod_scale, first, half_width, 0)
    shift_part = lax.dynamic_slice_in_dim(mod_shift, first, half_width, 0)

    def modulate(cells, pair):
        cells = (cells.astype(F32) - pair[0]) * pair[1]
        return (cells * gain_part + shift_part).astype(BF16)

    pair = heads // 2
    edge = pair * head_dim
    w_heads = jnp.transpose(w_qkv, (1, 0, 2))

    own, own_early, moments = modulate_and_heads(tokens, mod_scale[None], mod_shift[None], w_heads, [sent])
    got_early, got_moments = swap(own_early, "sx", 1), swap(moments, "sx", 1)
    near = swap(piece, "tp", 1)
    piece_far = hold(swap(piece, "tp", 2), got_early, got_moments)
    first_part = width_of(hidden // 3, hidden)
    own_first = border_and_hidden(own, picks, w_heads, w_mlp_in, first_part, [moments, piece])
    got_first = swap(own_first, "sx", 1)
    piece_far = hold(piece_far, own_first)
    near_far = swap(piece_far, "tp", 1)
    lower, upper = in_order(far, piece, piece_far), in_order(far, near, near_far)
    quarters = [part for pair_of in zip(lower, upper) for part in in_order(core, *pair_of)]
    other = jnp.concatenate(quarters, axis=1)
    other = modulate(other, [got_moments[:, i, : token_block(tok_rows)].reshape(tok_rows, 1) for i in range(2)])
    late_first = (1 - side) * edge
    other_late = [
        dot(other, lax.dynamic_slice(w_heads, (g, 0, late_first), (1, half_width, edge + head_dim))[0]).astype(BF16)
        for g in range(3)
    ]
    other_late = jnp.concatenate(other_late, axis=1)
    got_late = swap(other_late, "sx", 1)
    cut = tok_rows // 2
    own_heads, other_heads, other_border, own_rest, other_a, other_b = rest_of_first(
        place, own, other, picks, w_heads, w_mlp_in, first_part, cut, [other_late, got_first]
    )
    got_rest = swap(own_rest, "sx", 1)
    queries, keys_values, lower, upper = norm_units(
        place, (own_heads, got_late), (other_heads, got_early), (other_border, got_first), q_gain, k_gain, [other_a]
    )
    above = shift(lower, "sy", 1)
    below = shift(upper, "sy", -1)

    sent_mlp, kept_mlp, sent_attn, kept_attn = (
        lax.dynamic_slice_in_dim(w, start * block, block, 1)
        for w in (w_mlp_out, w_attn_out)
        for start in (1 - core, core)
    )

    def activate(mine, got, *earlier):
        got = hold(got, *earlier) if earlier else got
        return hold(jax.nn.gelu(mine.astype(F32) + got.astype(F32), approximate=True).astype(BF16))

    attended = attend(place, queries, keys_values, above, below, *window_codes(TILE), heads)
    got_attended = swap(attended, "sx", 1)
    got_other_a = swap(other_a, "sx", 1)
    got_own = jnp.concatenate([got_first[:tok_rows], hold(got_rest, attended)], axis=1)
    own_hidden = jnp.concatenate([own_first[:tok_rows], own_rest], axis=1)
    other_active = activate(jnp.concatenate([other_a, other_b], axis=0), got_own)
    other_sent, other_kept = dot(other_active, sent_mlp), dot(other_active, kept_mlp)
    got_other_b = swap(hold(other_b, other_sent), "sx", 1)

    def own_part(begin, end, got, *earlier):
        active, heads_part = activate(own_hidden[begin:end], got, *earlier), own_attended[begin:end]
        return (
            (dot(active, sent_mlp) + dot(heads_part, sent_attn)).astype(BF16),
            dot(active, kept_mlp) + dot(heads_part, kept_attn),
        )

    got_attended = hold(got_attended, other_sent, other_kept, got_other_a)
    here = edge + head_dim

    def natural(mine, middle, theirs):
        return jnp.concatenate(
            [jnp.where(side == 0, mine, theirs), middle, jnp.where(side == 0, theirs, mine)], axis=1
        )

    own_attended = natural(attended[:, :edge], attended[:, edge:here], got_attended[:, here:])
    other_attended = natural(attended[:, here:], got_attended[:, edge:here], got_attended[:, :edge])
    other_sent = (other_sent + dot(other_attended, sent_attn)).astype(BF16)
    other_kept = other_kept + dot(hold(other_attended, other_sent), kept_attn)
    other_come = swap(other_sent, "tp", 1)
    own_sent_a, own_kept_a = own_part(0, cut, got_other_a, other_sent, other_kept)

    def rows_of(half):
        kept = jnp.where(half == 0, other_kept[:cut], other_kept[cut:])
        return kept + jnp.where(half == 0, other_come[:cut], other_come[cut:]).astype(F32)

    passed = rows_of(1 - far).astype(BF16)
    passed = hold(swap(passed, "tp", 2), own_sent_a, own_kept_a)
    crossing = (rows_of(far) + passed.astype(F32)).astype(BF16)
    got = swap(crossing, "sx", 1)
    own_sum_a = own_kept_a + swap(own_sent_a, "tp", 1).astype(F32)
    come_a = swap(own_sum_a.astype(BF16), "tp", 2)
    own_sent_b, own_kept_b = own_part(cut, tok_rows, got_other_b, crossing)
    own_sum_b = hold(own_kept_b, got, come_a, cost=EARLY) + swap(own_sent_b, "tp", 1).astype(F32)

    home = far == side
    come_b = swap(jnp.where(home, got, own_sum_b.astype(BF16)), "tp", 2)
    wide = got.astype(F32)
    known = jnp.concatenate(
        [
            jnp.where(home, own_sum_a + come_a.astype(F32), jnp.where(far == 0, wide, 0.0)),
            jnp.where(home, own_sum_b, jnp.where(far == 0, 0.0, wide)),
        ],
        axis=0,
    )
    first_col = part * block
    gate_part = lax.dynamic_slice_in_dim(mod_gate, first_col, block, 0)
    residual_part = lax.dynamic_slice_in_dim(tokens, first_col, block, 1).astype(F32)
    known = hold(residual_part + gate_part * known)
    late_first = jnp.where(home, 1, 1 - far) * cut
    token = lax.broadcasted_iota(jnp.int32, (tok_rows, 1), 0)
    late = (token >= late_first) & (token < late_first + cut)
    late_part = jnp.concatenate([come_b, come_b], axis=0).astype(F32)
    return (known + jnp.where(late, gate_part * late_part, 0.0)).astype(BF16)


def shards(*arrays):
    local_heads = arrays[6].shape[0]
    if lax.axis_size("sx") == 2 and lax.axis_size("tp") == 4 and local_heads % 2 and local_heads > 1 and arrays[6].shape[1] == LANES:
        return paired_plan(*arrays)
    return gathered_plan(*arrays)


def solution(mesh):
    placed = (
        P(("sy", "sx"), None),
        P(),
        P(),
        P(),
        P("sx", None, "tp"),
        P("sx", "tp"),
        P("tp", None),
        P("tp", None),
        P("tp", "sx"),
        P("tp", "sx"),
    )
    return jax.shard_map(
        shards, mesh=mesh, in_specs=placed, out_specs=P(("sy", "sx"), "tp"), check_vma=False
    )
```

```python
import jax
import jax.numpy as jnp
import numpy as np
from jax import lax
from jax.experimental import pallas as pl
from jax.experimental.pallas import tpu as pltpu
from jax.sharding import PartitionSpec as P

TILE = 20


def with_halo(cells, sides, width):
    for axis, dim in sides:
        count = lax.axis_size(axis)
        ends = count - 1
        head = lax.slice_in_dim(cells, 0, width, axis=dim)
        tail = lax.slice_in_dim(cells, cells.shape[dim] - width, cells.shape[dim], axis=dim)
        cells = jnp.concatenate(
            [
                lax.ppermute(tail, axis, [(i, (i + 1) % count) for i in range(ends)]),
                cells,
                lax.ppermute(head, axis, [((i + 1) % count, i) for i in range(ends)]),
            ],
            axis=dim,
        )
    return cells


def layer_norm(vector):
    centered = vector - jnp.mean(vector, axis=-1, keepdims=True)
    variance = jnp.mean(centered * centered, axis=-1, keepdims=True)
    return centered * lax.rsqrt(variance + 1e-06)


def rms_gain(vector, scaling):
    mean_square = jnp.mean(vector * vector, axis=-1, keepdims=True)
    return vector * lax.rsqrt(mean_square + 1e-06) * scaling


def gathered_plan(
    tokens, mod_shift, mod_scale, mod_gate, w_qkv, w_mlp_in, q_gain, k_gain, w_attn_out, w_mlp_out
):
    tok_rows, model_width = tokens.shape
    tile_side = TILE
    half_side = TILE // 2
    inputs = tokens.astype(jnp.float32)
    modded = (layer_norm(inputs) * (1.0 + mod_scale) + mod_shift).astype(jnp.bfloat16)
    local_heads, head_dim = q_gain.shape
    local_width = local_heads * head_dim
    pieces = (
        lax.all_gather(w_qkv, "sx", axis=0, tiled=True),
        lax.all_gather(w_mlp_in, "sx", axis=0, tiled=True),
    )
    piece_rows = pieces[0].shape[0]
    qkv_sum = jnp.dot(
        modded, pieces[0].reshape(piece_rows, 3 * local_width), preferred_element_type=jnp.float32
    )
    mlp_sum = jnp.dot(modded, pieces[1], preferred_element_type=jnp.float32)
    qkv_parts = qkv_sum.reshape(tok_rows, 3, local_heads, head_dim)
    queries = rms_gain(qkv_parts[:, 0], q_gain).astype(jnp.bfloat16)
    key_rows = rms_gain(qkv_parts[:, 1], k_gain).astype(jnp.bfloat16)
    value_rows = qkv_parts[:, 2].astype(jnp.bfloat16)
    key_value = jnp.concatenate(
        [key_rows.reshape(tok_rows, local_width), value_rows.reshape(tok_rows, local_width)], axis=1
    )
    key_value = key_value.reshape(tile_side, tile_side, 2 * local_width)
    extended = with_halo(key_value, (("sy", 0), ("sx", 1)), half_side)
    window = extended.reshape(4 * tok_rows, 2 * local_width)
    window_keys = window[:, :local_width].reshape(4 * tok_rows, local_heads, head_dim)
    window_values = window[:, local_width:].reshape(4 * tok_rows, local_heads, head_dim)
    offsets = jnp.arange(2 * tile_side, dtype=jnp.int32)
    row_pos = lax.axis_index("sy") * tile_side - half_side + offsets
    col_pos = lax.axis_index("sx") * tile_side - half_side + offsets
    row_ok = (row_pos >= 0) & (row_pos < tile_side * lax.axis_size("sy"))
    col_ok = (col_pos >= 0) & (col_pos < tile_side * lax.axis_size("sx"))
    in_grid = (row_ok[:, None] & col_ok[None, :]).reshape(4 * tok_rows)
    scores = jnp.einsum(
        "qhd,khd->hqk", queries, window_keys, preferred_element_type=jnp.float32
    ) * head_dim ** (-0.5)
    scores = jnp.where(in_grid[None, None, :], scores, -jnp.inf)
    row_max = jnp.max(scores, axis=-1, keepdims=True)
    numerators = jnp.exp(scores - row_max)
    weights = (numerators / jnp.sum(numerators, axis=-1, keepdims=True)).astype(jnp.bfloat16)
    attended = jnp.einsum(
        "hqk,khd->qhd", weights, window_values, preferred_element_type=jnp.float32
    )
    attended = attended.astype(jnp.bfloat16).reshape(tok_rows, local_width)
    activated = jax.nn.gelu(mlp_sum, approximate=True).astype(jnp.bfloat16)
    pieces = (
        lax.all_gather(w_attn_out, "sx", axis=1, tiled=True),
        lax.all_gather(w_mlp_out, "sx", axis=1, tiled=True),
    )
    product_term = jnp.dot(attended, pieces[0], preferred_element_type=jnp.float32)
    product_term = product_term + jnp.dot(activated, pieces[1], preferred_element_type=jnp.float32)
    reduced = lax.psum_scatter(
        product_term.astype(jnp.bfloat16), "tp", scatter_dimension=1, tiled=True
    ).astype(jnp.float32)
    block_width = model_width // lax.axis_size("tp")
    first_col = lax.axis_index("tp") * block_width
    residual_part = lax.dynamic_slice_in_dim(inputs, first_col, block_width, 1)
    gate_part = lax.dynamic_slice_in_dim(mod_gate, first_col, block_width, 0)
    return (residual_part + gate_part * reduced).astype(jnp.bfloat16)


def swap(cells, axis, bit):
    count = lax.axis_size(axis)
    return lax.ppermute(cells, axis, [(i, i ^ bit) for i in range(count)])


def shift(cells, axis, step):
    count = lax.axis_size(axis)
    return lax.ppermute(
        cells, axis, [(i, i + step) for i in range(count) if 0 <= i + step < count]
    )


def dot(left, right):
    return jnp.dot(left, right, preferred_element_type=jnp.float32)


BF16, F32 = jnp.bfloat16, jnp.float32
LANES = 128
EARLY = 20_000_000
VMEM = 56
REST_VMEM = 28
POST_VMEM = 40


def width_of(total, most):
    return max(w for w in range(LANES, most + 1, LANES) if total % w == 0)


def call(body, grid, ins, outs, scratch=(), after=(), vmem=16, cost=(1000, 1000)):
    n_in, n_after = len(ins), len(after)

    def kernel(*refs):
        body(*refs[:n_in], *refs[n_in + n_after :])

    def spec(block, index):
        if block is None:
            return pl.BlockSpec(memory_space=index)
        return pl.BlockSpec(block, index)

    return pl.pallas_call(
        kernel,
        grid=(grid,),
        in_specs=[spec(b, i) for _, b, i in ins] + [pl.BlockSpec(memory_space=pl.ANY)] * n_after,
        out_specs=[spec(b, i) for _, _, b, i in outs],
        out_shape=[jax.ShapeDtypeStruct(s, d) for s, d, _, _ in outs],
        scratch_shapes=list(scratch),
        compiler_params=pltpu.CompilerParams(vmem_limit_bytes=vmem * 2**20),
        cost_estimate=pl.CostEstimate(flops=cost[0], bytes_accessed=cost[1], transcendentals=0),
    )(*[a for a, _, _ in ins], *after)


def in_order(bit, mine, other):
    return jnp.where(bit == 0, mine, other), jnp.where(bit == 0, other, mine)


def hold(cells, *earlier, cost=0):
    return pl.pallas_call(
        lambda *refs: None,
        in_specs=[pl.BlockSpec(memory_space=pl.ANY)] * (1 + len(earlier)),
        out_specs=pl.BlockSpec(memory_space=pl.ANY),
        out_shape=jax.ShapeDtypeStruct(cells.shape, cells.dtype),
        input_output_aliases={0: 0},
        compiler_params=pltpu.CompilerParams(vmem_limit_bytes=2**20),
        cost_estimate=pl.CostEstimate(flops=0, bytes_accessed=cost, transcendentals=0),
    )(cells, *earlier)


def at(*place):
    return lambda *_: place


def border_rows(tile_side):
    half = tile_side // 2
    return (half * half + 15) // 16 * 16


def border_picks(tile_side):
    half, rows = tile_side // 2, border_rows(tile_side)
    picks = np.zeros((2, 2 * rows, tile_side * tile_side), np.float32)
    for side in range(2):
        for low in range(2):
            for i in range(half):
                for j in range(half):
                    token = (low * half + i) * tile_side + j + (half if side == 0 else 0)
                    picks[side, low * rows + i * half + j, token] = 1
    return jnp.asarray(picks, BF16)


def token_block(rows):
    return max(b for b in range(16, LANES + 1, 16) if rows % b == 0)


def modulate_and_heads(tokens, scale_row, shift_row, w_heads, after=()):
    rows, model_width = tokens.shape
    depth, width = w_heads.shape[1:]
    edge = (width - LANES) // 2
    block = token_block(rows)

    def body(tokens_ref, scale_ref, shift_ref, w_heads_ref, own_ref, out_ref, moments_ref):
        side = lax.axis_index("sx")
        cells = tokens_ref[...].astype(F32)
        mean = jnp.mean(cells, axis=-1, keepdims=True)
        centered = cells - mean
        scaling = lax.rsqrt(jnp.mean(centered * centered, axis=-1, keepdims=True) + 1e-06)
        some = pl.ds(pl.multiple_of(side * depth, LANES), depth)
        normed = (tokens_ref[:, some].astype(F32) - mean) * scaling
        own = (normed * (1.0 + scale_ref[:, some]) + shift_ref[:, some]).astype(BF16)
        own_ref[...] = own
        theirs = pl.ds(pl.multiple_of((1 - side) * (width - edge), LANES), edge)
        for g in range(3):
            out_ref[:, g * edge : (g + 1) * edge] = dot(own, w_heads_ref[g, :, theirs]).astype(BF16)
        lane = lax.broadcasted_iota(jnp.int32, (LANES, LANES), 1)
        mean, scaling = (jnp.pad(m, ((0, LANES - block), (0, 0))) for m in (mean, scaling))
        moments = jnp.where(lane == 0, mean, jnp.where(lane == 1, scaling, 0.0))
        moments_ref[0] = moments.T[:8]

    row = lambda i: (i, 0)
    return call(
        body, rows // block,
        [
            (tokens, (block, model_width), row),
            (scale_row, scale_row.shape, at(0, 0)),
            (shift_row, shift_row.shape, at(0, 0)),
            (w_heads, w_heads.shape, at(0, 0, 0)),
        ],
        [
            ((rows, depth), BF16, (block, depth), row),
            ((rows, 3 * edge), BF16, (block, 3 * edge), row),
            ((rows // block, 8, LANES), F32, (1, 8, LANES), lambda i: (i, 0, 0)),
        ],
        after=after, vmem=VMEM,
    )


def border_and_hidden(own, picks, w_heads, hidden_weights, cut, after=()):
    rows, depth = own.shape
    half_border, width = picks.shape[1] // 2, w_heads.shape[2]

    def body(own_ref, picks_ref, keys_ref, values_ref, w_ref, out_ref):
        taken = dot(picks_ref[lax.axis_index("sx")], own_ref[...]).astype(BF16)
        out_ref[:rows] = dot(own_ref[...], w_ref[...]).astype(BF16)
        for g, ref in enumerate((keys_ref, values_ref)):
            part = dot(taken, ref[0]).astype(BF16)
            out_ref[rows:, g * LANES : (g + 1) * LANES] = part[:half_border]
            out_ref[rows:, (2 + g) * LANES : (3 + g) * LANES] = part[half_border:]

    whole = at(0, 0)
    middle = (width - LANES) // 2 // LANES
    return call(
        body, 1,
        [(own, own.shape, whole), (picks, picks.shape, at(0, 0, 0))]
        + [(w_heads, (1, depth, LANES), at(g, 0, middle)) for g in (1, 2)]
        + [(hidden_weights, (depth, cut), whole)],
        [((rows + half_border, cut), BF16, (rows + half_border, cut), whole)],
        after=after, vmem=VMEM,
    )[0]


def rest_of_first(place, own, other, picks, w_heads, hidden_weights, begin, cut, after=()):
    rows, depth = other.shape
    width, hidden = w_heads.shape[2], hidden_weights.shape[1]
    edge = (width - LANES) // 2
    border = picks.shape[1]
    block = width_of(begin, 512)
    parts = begin // block

    def body(
        place_ref, own_ref, other_ref, picks_ref, w_heads_ref, w_ref,
        qkv_ref, mine_ref, border_ref, rest_ref, a_ref, b_ref,
    ):
        side = place_ref[0]

        @pl.when(pl.program_id(0) == 0)
        def _():
            both = pl.ds(pl.multiple_of(side * edge, LANES), edge + LANES)
            mine = pl.ds(pl.multiple_of(side * (width - edge), LANES), edge)
            for g in range(3):
                qkv_ref[:, g * (edge + LANES) : (g + 1) * (edge + LANES)] = dot(own_ref[...], w_heads_ref[g, :, both])
                mine_ref[:, g * edge : (g + 1) * edge] = dot(other_ref[...], w_heads_ref[g, :, mine])
            taken = dot(picks_ref[1 - side], other_ref[...]).astype(BF16)
            for g in range(2):
                border_ref[:, g * LANES : (g + 1) * LANES] = dot(taken, w_heads_ref[1 + g, :, edge : edge + LANES])

        sums = dot(other_ref[...], w_ref[...])
        a_ref[...] = sums[:cut].astype(BF16)
        b_ref[...] = sums[cut:].astype(BF16)

        @pl.when(pl.program_id(0) >= parts)
        def _():
            rest_ref[...] = dot(own_ref[...], w_ref[...]).astype(BF16)

    whole = at(0, 0)
    column = lambda j: (0, j)
    out = lambda count, wide: ((count, wide), F32, (count, wide), whole)
    return call(
        body, hidden // block,
        [(place, None, pltpu.SMEM), (own, own.shape, whole), (other, other.shape, whole)]
        + [(a, a.shape, at(0, 0, 0)) for a in (picks, w_heads)]
        + [(hidden_weights, (depth, block), column)],
        [
            out(rows, 3 * (edge + LANES)),
            out(rows, 3 * edge),
            out(border, 2 * LANES),
            ((rows, hidden - begin), BF16, (rows, block), lambda j: (0, jnp.maximum(j - parts, 0))),
            ((cut, hidden), BF16, (cut, block), column),
            ((rows - cut, hidden), BF16, (rows - cut, block), column),
        ],
        after=after, vmem=REST_VMEM,
        cost=(
            2 * depth * (rows * 4 * width + border * 2 * LANES + rows * hidden),
            2 * depth * (2 * rows + 3 * width + hidden) + 12 * rows * width + 2 * rows * hidden,
        ),
    )


def norm_units(place, own, other, border, q_gain, k_gain, after=()):
    rows, heads, head_dim = own[0].shape[0], q_gain.shape[0], q_gain.shape[2]
    pair = heads // 2
    units = 2 * pair + 1
    half_border = border[0].shape[0] // 2
    sent_rows = (rows // 2 + 15) // 16 * 16
    sent = units * sent_rows + half_border

    def body(place_ref, *refs):
        own_refs, other_refs, border_refs = refs[:2], refs[2:4], refs[4:6]
        q_gain_ref, k_gain_ref, queries_ref, kv_ref, lower_ref, upper_ref = refs[6:]
        side = place_ref[0]
        first = side * (heads - pair)

        def head(two, index):
            some = pl.ds(pl.multiple_of(index * head_dim, LANES), head_dim)
            return sum(ref[:, some].astype(F32) for ref in two)

        def put(unit, two, p, count, index):
            q, k, v = (head(two, g * count + p) for g in range(3))
            kv = jnp.concatenate([rms_gain(k, k_gain_ref[index]), v], axis=1).astype(BF16)
            queries_ref[unit * rows : (unit + 1) * rows] = rms_gain(q, q_gain_ref[index]).astype(BF16)
            kv_ref[unit * rows : (unit + 1) * rows] = kv
            lower_ref[unit * sent_rows : (unit + 1) * sent_rows] = kv[rows - sent_rows :]
            upper_ref[unit * sent_rows : (unit + 1) * sent_rows] = kv[:sent_rows]

        for p in range(pair):
            put(2 * p, own_refs, side + p, pair + 1, first + p)
            put(2 * p + 1, other_refs, p, pair, first + p)
        put(2 * pair, own_refs, (1 - side) * pair, pair + 1, pair)
        got = border_refs[1][rows:].astype(F32)
        got = jnp.concatenate([got[:, : 2 * head_dim], got[:, 2 * head_dim : 4 * head_dim]], axis=0)
        both = border_refs[0][...] + got
        kv = [rms_gain(both[:, :head_dim], k_gain_ref[pair]), both[:, head_dim:]]
        kv = jnp.concatenate(kv, axis=1).astype(BF16)
        kv_ref[units * rows :] = kv
        upper_ref[units * sent_rows :] = kv[:half_border]
        lower_ref[units * sent_rows :] = kv[half_border:]

    whole = at(0, 0)
    out = lambda count, width: ((count, width), BF16, (count, width), whole)
    ins = [*own, *other, *border]
    return call(
        body, 1,
        [(place, None, pltpu.SMEM)]
        + [(a, a.shape, whole) for a in ins]
        + [(g, g.shape, at(0, 0, 0)) for g in (q_gain, k_gain)],
        [
            out(units * rows, head_dim),
            out(units * rows + 2 * half_border, 2 * head_dim),
            out(sent, 2 * head_dim),
            out(sent, 2 * head_dim),
        ],
        after=after, vmem=POST_VMEM,
    )


def window_codes(tile_side):
    rows, half = tile_side * tile_side, tile_side // 2
    sent_rows = (rows // 2 + 15) // 16 * 16
    extra = sent_rows - rows // 2
    column = np.arange(rows) % tile_side

    def lines(first, second):
        above = lambda on: np.concatenate([np.zeros(extra, np.int32), 2 * on[rows - rows // 2 :]])
        below = lambda on: np.concatenate([3 * on[: rows // 2], np.zeros(extra, np.int32)])
        return np.concatenate([first, second, above(first), above(second), below(first), below(second)])

    def padded(line):
        return np.pad(line, (0, -len(line) % LANES)).astype(np.float32)

    every = np.ones(rows, np.int32)
    right, left = (column >= half).astype(np.int32), (column < half).astype(np.int32)
    by_side = np.stack([
        np.stack([padded(lines(every, left)), padded(lines(right, every))]),
        np.stack([padded(lines(every, right)), padded(lines(left, every))]),
    ])
    pad = border_rows(tile_side)
    part = np.pad(np.ones(half * half, np.int32), (0, pad - half * half))
    above = np.concatenate([np.zeros(extra, np.int32), 2 * np.ones(rows // 2, np.int32), 2 * part])
    below = np.concatenate([3 * np.ones(rows // 2, np.int32), np.zeros(extra, np.int32), 3 * part])
    middle = padded(np.concatenate([every, part, part, above, below]))[None]
    return jnp.asarray(by_side), jnp.asarray(middle)


def attend(place, queries, keys_values, above, below, codes, middle_codes, heads, after=()):
    pair = heads // 2
    units = 2 * pair + 1
    head_dim = queries.shape[1]
    rows = queries.shape[0] // units
    border = keys_values.shape[0] - units * rows
    sent_rows = (above.shape[0] - border // 2) // units

    def body(place_ref, queries_ref, kv_ref, above_ref, below_ref, codes_ref, middle_ref, out_ref):
        side = place_ref[0]

        def unit_rows(ref, unit, count, size):
            return ref[unit * size : (unit + count) * size]

        def rest_rows(ref, size):
            return ref[units * size :]

        def one(unit, blocks, line, column):
            there = (line == 1) | ((line == 2) & (place_ref[2] == 1)) | ((line == 3) & (place_ref[3] == 1))
            line = jnp.where(there, 0.0, -jnp.inf)
            spare = line.shape[1] - sum(b.shape[0] for b in blocks)
            if spare:
                blocks = blocks + [jnp.zeros((spare, 2 * head_dim), BF16)]
            both = jnp.concatenate(blocks, axis=0)
            keys, values = both[:, :head_dim], both[:, head_dim:]
            mine = unit_rows(queries_ref, unit, 1, rows)
            scores = lax.dot_general(mine, keys, (((1,), (1,)), ((), ())), preferred_element_type=F32)
            scores = scores * head_dim ** (-0.5) + line
            numerators = jnp.exp(scores - jnp.max(scores, axis=-1, keepdims=True))
            total = jnp.sum(numerators, axis=-1, keepdims=True)
            got = (dot(numerators.astype(BF16), values) / total).astype(BF16)
            out_ref[:, column * head_dim : (column + 1) * head_dim] = got

        for p in range(pair):
            blocks = [
                unit_rows(kv_ref, 2 * p, 2, rows),
                unit_rows(above_ref, 2 * p, 2, sent_rows),
                unit_rows(below_ref, 2 * p, 2, sent_rows),
            ]
            one(2 * p, blocks, codes_ref[side][0:1], p)
            one(2 * p + 1, blocks, codes_ref[side][1:2], pair + 1 + p)
        blocks = [
            kv_ref[2 * pair * rows :],
            above_ref[2 * pair * sent_rows :],
            below_ref[2 * pair * sent_rows :],
        ]
        one(2 * pair, blocks, middle_ref[...], pair)

    ins = [queries, keys_values, above, below, middle_codes]
    whole = [(a, a.shape, at(0, 0)) for a in ins]
    return call(
        body, 1,
        [(place, None, pltpu.SMEM)] + whole[:4] + [(codes, codes.shape, at(0, 0, 0))] + whole[4:],
        [((rows, units * head_dim), BF16, (rows, units * head_dim), at(0, 0))],
        after=after, vmem=POST_VMEM,
    )[0]


def paired_plan(
    tokens, mod_shift, mod_scale, mod_gate, w_qkv, w_mlp_in, q_gain, k_gain, w_attn_out, w_mlp_out
):
    tok_rows, model_width = tokens.shape
    half_width, hidden = w_mlp_in.shape
    heads, head_dim = q_gain.shape
    width = heads * head_dim
    side = lax.axis_index("sx")
    part = lax.axis_index("tp")
    core, far = part % 2, part // 2
    mid = hidden // 2
    block = half_width // 2
    row = lax.axis_index("sy")
    place = jnp.stack([side, core, row > 0, row < lax.axis_size("sy") - 1]).astype(jnp.int32)
    picks = border_picks(TILE)
    q_gain, k_gain = q_gain[:, None, :], k_gain[:, None, :]

    quarter = half_width // 4
    other_first = (1 - side) * half_width + part * quarter
    sent = lax.dynamic_slice_in_dim(lax.optimization_barrier(tokens), other_first, quarter, 1)
    piece = swap(sent, "sx", 1)
    first = side * half_width
    gain_part = 1.0 + lax.dynamic_slice_in_dim(mod_scale, first, half_width, 0)
    shift_part = lax.dynamic_slice_in_dim(mod_shift, first, half_width, 0)

    def modulate(cells, pair):
        cells = (cells.astype(F32) - pair[0]) * pair[1]
        return (cells * gain_part + shift_part).astype(BF16)

    pair = heads // 2
    edge = pair * head_dim
    w_heads = jnp.transpose(w_qkv, (1, 0, 2))

    own, own_early, moments = modulate_and_heads(tokens, mod_scale[None], mod_shift[None], w_heads, [sent])
    got_early, got_moments = swap(own_early, "sx", 1), swap(moments, "sx", 1)
    near = swap(piece, "tp", 1)
    piece_far = hold(swap(piece, "tp", 2), got_early)
    first_part = width_of(hidden // 3, hidden)
    own_first = border_and_hidden(own, picks, w_heads, w_mlp_in, first_part, [moments, piece])
    got_first = swap(own_first, "sx", 1)
    piece_far = hold(piece_far, own_first)
    near_far = swap(piece_far, "tp", 1)
    lower, upper = in_order(far, piece, piece_far), in_order(far, near, near_far)
    quarters = [part for pair_of in zip(lower, upper) for part in in_order(core, *pair_of)]
    other = jnp.concatenate(quarters, axis=1)
    other = modulate(other, [got_moments[:, i, : token_block(tok_rows)].reshape(tok_rows, 1) for i in range(2)])
    late_first = (1 - side) * edge
    other_late = [
        dot(other, lax.dynamic_slice(w_heads, (g, 0, late_first), (1, half_width, edge + head_dim))[0]).astype(BF16)
        for g in range(3)
    ]
    other_late = jnp.concatenate(other_late, axis=1)
    got_late = swap(other_late, "sx", 1)
    cut = tok_rows // 2
    own_heads, other_heads, other_border, own_rest, other_a, other_b = rest_of_first(
        place, own, other, picks, w_heads, w_mlp_in, first_part, cut, [other_late, got_first]
    )
    got_rest = swap(own_rest, "sx", 1)
    queries, keys_values, lower, upper = norm_units(
        place, (own_heads, got_late), (other_heads, got_early), (other_border, got_first), q_gain, k_gain, [other_a]
    )
    above = shift(lower, "sy", 1)
    below = shift(upper, "sy", -1)

    sent_mlp, kept_mlp, sent_attn, kept_attn = (
        lax.dynamic_slice_in_dim(w, start * block, block, 1)
        for w in (w_mlp_out, w_attn_out)
        for start in (1 - core, core)
    )

    def activate(mine, got, *earlier):
        got = hold(got, *earlier) if earlier else got
        return hold(jax.nn.gelu(mine.astype(F32) + got.astype(F32), approximate=True).astype(BF16))

    attended = attend(place, queries, keys_values, above, below, *window_codes(TILE), heads)
    got_attended = swap(attended, "sx", 1)
    got_other_a = swap(other_a, "sx", 1)
    got_own = jnp.concatenate([got_first[:tok_rows], hold(got_rest, attended)], axis=1)
    own_hidden = jnp.concatenate([own_first[:tok_rows], own_rest], axis=1)
    other_active = activate(jnp.concatenate([other_a, other_b], axis=0), got_own)
    other_sent, other_kept = dot(other_active, sent_mlp), dot(other_active, kept_mlp)
    got_other_b = swap(hold(other_b, other_sent), "sx", 1)

    def own_part(begin, end, got, *earlier):
        active, heads_part = activate(own_hidden[begin:end], got, *earlier), own_attended[begin:end]
        return (
            (dot(active, sent_mlp) + dot(heads_part, sent_attn)).astype(BF16),
            dot(active, kept_mlp) + dot(heads_part, kept_attn),
        )

    got_attended = hold(got_attended, other_sent, other_kept, got_other_a)
    here = edge + head_dim

    def natural(mine, middle, theirs):
        return jnp.concatenate(
            [jnp.where(side == 0, mine, theirs), middle, jnp.where(side == 0, theirs, mine)], axis=1
        )

    own_attended = natural(attended[:, :edge], attended[:, edge:here], got_attended[:, here:])
    other_attended = natural(attended[:, here:], got_attended[:, edge:here], got_attended[:, :edge])
    other_sent = (other_sent + dot(other_attended, sent_attn)).astype(BF16)
    other_kept = other_kept + dot(hold(other_attended, other_sent), kept_attn)
    other_come = swap(other_sent, "tp", 1)
    own_sent_a, own_kept_a = own_part(0, cut, got_other_a, other_sent, other_kept)

    def rows_of(half):
        kept = jnp.where(half == 0, other_kept[:cut], other_kept[cut:])
        return kept + jnp.where(half == 0, other_come[:cut], other_come[cut:]).astype(F32)

    passed = rows_of(1 - far).astype(BF16)
    passed = hold(swap(passed, "tp", 2), own_sent_a, own_kept_a)
    crossing = (rows_of(far) + passed.astype(F32)).astype(BF16)
    got = swap(crossing, "sx", 1)
    own_sum_a = own_kept_a + swap(own_sent_a, "tp", 1).astype(F32)
    come_a = swap(own_sum_a.astype(BF16), "tp", 2)
    own_sent_b, own_kept_b = own_part(cut, tok_rows, got_other_b, crossing)
    own_sum_b = hold(own_kept_b, got, come_a, cost=EARLY) + swap(own_sent_b, "tp", 1).astype(F32)

    home = far == side
    come_b = swap(jnp.where(home, got, own_sum_b.astype(BF16)), "tp", 2)
    wide = got.astype(F32)
    known = jnp.concatenate(
        [
            jnp.where(home, own_sum_a + come_a.astype(F32), jnp.where(far == 0, wide, 0.0)),
            jnp.where(home, own_sum_b, jnp.where(far == 0, 0.0, wide)),
        ],
        axis=0,
    )
    first_col = part * block
    gate_part = lax.dynamic_slice_in_dim(mod_gate, first_col, block, 0)
    residual_part = lax.dynamic_slice_in_dim(tokens, first_col, block, 1).astype(F32)
    known = hold(residual_part + gate_part * known)
    late_first = jnp.where(home, 1, 1 - far) * cut
    token = lax.broadcasted_iota(jnp.int32, (tok_rows, 1), 0)
    late = (token >= late_first) & (token < late_first + cut)
    late_part = jnp.concatenate([come_b, come_b], axis=0).astype(F32)
    return (known + jnp.where(late, gate_part * late_part, 0.0)).astype(BF16)


def shards(*arrays):
    local_heads = arrays[6].shape[0]
    if lax.axis_size("sx") == 2 and lax.axis_size("tp") == 4 and local_heads % 2 and local_heads > 1 and arrays[6].shape[1] == LANES:
        return paired_plan(*arrays)
    return gathered_plan(*arrays)


def solution(mesh):
    placed = (
        P(("sy", "sx"), None),
        P(),
        P(),
        P(),
        P("sx", None, "tp"),
        P("sx", "tp"),
        P("tp", None),
        P("tp", None),
        P("tp", "sx"),
        P("tp", "sx"),
    )
    return jax.shard_map(
        shards, mesh=mesh, in_specs=placed, out_specs=P(("sy", "sx"), "tp"), check_vma=False
    )
```

```python
import jax
import jax.numpy as jnp
import numpy as np
from jax import lax
from jax.experimental import pallas as pl
from jax.experimental.pallas import tpu as pltpu
from jax.sharding import PartitionSpec as P

TILE = 20


def with_halo(cells, sides, width):
    for axis, dim in sides:
        count = lax.axis_size(axis)
        ends = count - 1
        head = lax.slice_in_dim(cells, 0, width, axis=dim)
        tail = lax.slice_in_dim(cells, cells.shape[dim] - width, cells.shape[dim], axis=dim)
        cells = jnp.concatenate(
            [
                lax.ppermute(tail, axis, [(i, (i + 1) % count) for i in range(ends)]),
                cells,
                lax.ppermute(head, axis, [((i + 1) % count, i) for i in range(ends)]),
            ],
            axis=dim,
        )
    return cells


def layer_norm(vector):
    centered = vector - jnp.mean(vector, axis=-1, keepdims=True)
    variance = jnp.mean(centered * centered, axis=-1, keepdims=True)
    return centered * lax.rsqrt(variance + 1e-06)


def rms_gain(vector, scaling):
    mean_square = jnp.mean(vector * vector, axis=-1, keepdims=True)
    return vector * lax.rsqrt(mean_square + 1e-06) * scaling


def gathered_plan(
    tokens, mod_shift, mod_scale, mod_gate, w_qkv, w_mlp_in, q_gain, k_gain, w_attn_out, w_mlp_out
):
    tok_rows, model_width = tokens.shape
    tile_side = TILE
    half_side = TILE // 2
    inputs = tokens.astype(jnp.float32)
    modded = (layer_norm(inputs) * (1.0 + mod_scale) + mod_shift).astype(jnp.bfloat16)
    local_heads, head_dim = q_gain.shape
    local_width = local_heads * head_dim
    pieces = (
        lax.all_gather(w_qkv, "sx", axis=0, tiled=True),
        lax.all_gather(w_mlp_in, "sx", axis=0, tiled=True),
    )
    piece_rows = pieces[0].shape[0]
    qkv_sum = jnp.dot(
        modded, pieces[0].reshape(piece_rows, 3 * local_width), preferred_element_type=jnp.float32
    )
    mlp_sum = jnp.dot(modded, pieces[1], preferred_element_type=jnp.float32)
    qkv_parts = qkv_sum.reshape(tok_rows, 3, local_heads, head_dim)
    queries = rms_gain(qkv_parts[:, 0], q_gain).astype(jnp.bfloat16)
    key_rows = rms_gain(qkv_parts[:, 1], k_gain).astype(jnp.bfloat16)
    value_rows = qkv_parts[:, 2].astype(jnp.bfloat16)
    key_value = jnp.concatenate(
        [key_rows.reshape(tok_rows, local_width), value_rows.reshape(tok_rows, local_width)], axis=1
    )
    key_value = key_value.reshape(tile_side, tile_side, 2 * local_width)
    extended = with_halo(key_value, (("sy", 0), ("sx", 1)), half_side)
    window = extended.reshape(4 * tok_rows, 2 * local_width)
    window_keys = window[:, :local_width].reshape(4 * tok_rows, local_heads, head_dim)
    window_values = window[:, local_width:].reshape(4 * tok_rows, local_heads, head_dim)
    offsets = jnp.arange(2 * tile_side, dtype=jnp.int32)
    row_pos = lax.axis_index("sy") * tile_side - half_side + offsets
    col_pos = lax.axis_index("sx") * tile_side - half_side + offsets
    row_ok = (row_pos >= 0) & (row_pos < tile_side * lax.axis_size("sy"))
    col_ok = (col_pos >= 0) & (col_pos < tile_side * lax.axis_size("sx"))
    in_grid = (row_ok[:, None] & col_ok[None, :]).reshape(4 * tok_rows)
    scores = jnp.einsum(
        "qhd,khd->hqk", queries, window_keys, preferred_element_type=jnp.float32
    ) * head_dim ** (-0.5)
    scores = jnp.where(in_grid[None, None, :], scores, -jnp.inf)
    row_max = jnp.max(scores, axis=-1, keepdims=True)
    numerators = jnp.exp(scores - row_max)
    weights = (numerators / jnp.sum(numerators, axis=-1, keepdims=True)).astype(jnp.bfloat16)
    attended = jnp.einsum(
        "hqk,khd->qhd", weights, window_values, preferred_element_type=jnp.float32
    )
    attended = attended.astype(jnp.bfloat16).reshape(tok_rows, local_width)
    activated = jax.nn.gelu(mlp_sum, approximate=True).astype(jnp.bfloat16)
    pieces = (
        lax.all_gather(w_attn_out, "sx", axis=1, tiled=True),
        lax.all_gather(w_mlp_out, "sx", axis=1, tiled=True),
    )
    product_term = jnp.dot(attended, pieces[0], preferred_element_type=jnp.float32)
    product_term = product_term + jnp.dot(activated, pieces[1], preferred_element_type=jnp.float32)
    reduced = lax.psum_scatter(
        product_term.astype(jnp.bfloat16), "tp", scatter_dimension=1, tiled=True
    ).astype(jnp.float32)
    block_width = model_width // lax.axis_size("tp")
    first_col = lax.axis_index("tp") * block_width
    residual_part = lax.dynamic_slice_in_dim(inputs, first_col, block_width, 1)
    gate_part = lax.dynamic_slice_in_dim(mod_gate, first_col, block_width, 0)
    return (residual_part + gate_part * reduced).astype(jnp.bfloat16)


def swap(cells, axis, bit):
    count = lax.axis_size(axis)
    return lax.ppermute(cells, axis, [(i, i ^ bit) for i in range(count)])


def shift(cells, axis, step):
    count = lax.axis_size(axis)
    return lax.ppermute(
        cells, axis, [(i, i + step) for i in range(count) if 0 <= i + step < count]
    )


def dot(left, right):
    return jnp.dot(left, right, preferred_element_type=jnp.float32)


BF16, F32 = jnp.bfloat16, jnp.float32
LANES = 128
EARLY = 20_000_000
VMEM = 56
REST_VMEM = 40
POST_VMEM = 40


def width_of(total, most):
    return max(w for w in range(LANES, most + 1, LANES) if total % w == 0)


def call(body, grid, ins, outs, scratch=(), after=(), vmem=16, cost=(1000, 1000)):
    n_in, n_after = len(ins), len(after)

    def kernel(*refs):
        body(*refs[:n_in], *refs[n_in + n_after :])

    def spec(block, index):
        if block is None:
            return pl.BlockSpec(memory_space=index)
        return pl.BlockSpec(block, index)

    return pl.pallas_call(
        kernel,
        grid=(grid,),
        in_specs=[spec(b, i) for _, b, i in ins] + [pl.BlockSpec(memory_space=pl.ANY)] * n_after,
        out_specs=[spec(b, i) for _, _, b, i in outs],
        out_shape=[jax.ShapeDtypeStruct(s, d) for s, d, _, _ in outs],
        scratch_shapes=list(scratch),
        compiler_params=pltpu.CompilerParams(vmem_limit_bytes=vmem * 2**20),
        cost_estimate=pl.CostEstimate(flops=cost[0], bytes_accessed=cost[1], transcendentals=0),
    )(*[a for a, _, _ in ins], *after)


def in_order(bit, mine, other):
    return jnp.where(bit == 0, mine, other), jnp.where(bit == 0, other, mine)


def hold(cells, *earlier, cost=0):
    return pl.pallas_call(
        lambda *refs: None,
        in_specs=[pl.BlockSpec(memory_space=pl.ANY)] * (1 + len(earlier)),
        out_specs=pl.BlockSpec(memory_space=pl.ANY),
        out_shape=jax.ShapeDtypeStruct(cells.shape, cells.dtype),
        input_output_aliases={0: 0},
        compiler_params=pltpu.CompilerParams(vmem_limit_bytes=2**20),
        cost_estimate=pl.CostEstimate(flops=0, bytes_accessed=cost, transcendentals=0),
    )(cells, *earlier)


def at(*place):
    return lambda *_: place


def border_rows(tile_side):
    half = tile_side // 2
    return (half * half + 15) // 16 * 16


def border_picks(tile_side):
    half, rows = tile_side // 2, border_rows(tile_side)
    picks = np.zeros((2, 2 * rows, tile_side * tile_side), np.float32)
    for side in range(2):
        for low in range(2):
            for i in range(half):
                for j in range(half):
                    token = (low * half + i) * tile_side + j + (half if side == 0 else 0)
                    picks[side, low * rows + i * half + j, token] = 1
    return jnp.asarray(picks, BF16)


def token_block(rows):
    return max(b for b in range(16, LANES + 1, 16) if rows % b == 0)


def modulate_and_heads(tokens, scale_row, shift_row, w_heads, after=()):
    rows, model_width = tokens.shape
    depth, width = w_heads.shape[1:]
    edge = (width - LANES) // 2
    block = token_block(rows)

    def body(tokens_ref, scale_ref, shift_ref, w_heads_ref, own_ref, out_ref, moments_ref):
        side = lax.axis_index("sx")
        cells = tokens_ref[...].astype(F32)
        mean = jnp.mean(cells, axis=-1, keepdims=True)
        centered = cells - mean
        scaling = lax.rsqrt(jnp.mean(centered * centered, axis=-1, keepdims=True) + 1e-06)
        some = pl.ds(pl.multiple_of(side * depth, LANES), depth)
        normed = (tokens_ref[:, some].astype(F32) - mean) * scaling
        own = (normed * (1.0 + scale_ref[:, some]) + shift_ref[:, some]).astype(BF16)
        own_ref[...] = own
        theirs = pl.ds(pl.multiple_of((1 - side) * (width - edge), LANES), edge)
        for g in range(3):
            out_ref[:, g * edge : (g + 1) * edge] = dot(own, w_heads_ref[g, :, theirs]).astype(BF16)
        lane = lax.broadcasted_iota(jnp.int32, (LANES, LANES), 1)
        mean, scaling = (jnp.pad(m, ((0, LANES - block), (0, 0))) for m in (mean, scaling))
        moments = jnp.where(lane == 0, mean, jnp.where(lane == 1, scaling, 0.0))
        moments_ref[0] = moments.T[:8]

    row = lambda i: (i, 0)
    return call(
        body, rows // block,
        [
            (tokens, (block, model_width), row),
            (scale_row, scale_row.shape, at(0, 0)),
            (shift_row, shift_row.shape, at(0, 0)),
            (w_heads, w_heads.shape, at(0, 0, 0)),
        ],
        [
            ((rows, depth), BF16, (block, depth), row),
            ((rows, 3 * edge), BF16, (block, 3 * edge), row),
            ((rows // block, 8, LANES), F32, (1, 8, LANES), lambda i: (i, 0, 0)),
        ],
        after=after, vmem=VMEM,
    )


def border_and_hidden(own, picks, w_heads, hidden_weights, cut, after=()):
    rows, depth = own.shape
    half_border, width = picks.shape[1] // 2, w_heads.shape[2]

    def body(own_ref, picks_ref, keys_ref, values_ref, w_ref, out_ref):
        taken = dot(picks_ref[lax.axis_index("sx")], own_ref[...]).astype(BF16)
        out_ref[:rows] = dot(own_ref[...], w_ref[...]).astype(BF16)
        for g, ref in enumerate((keys_ref, values_ref)):
            part = dot(taken, ref[0]).astype(BF16)
            out_ref[rows:, g * LANES : (g + 1) * LANES] = part[:half_border]
            out_ref[rows:, (2 + g) * LANES : (3 + g) * LANES] = part[half_border:]

    whole = at(0, 0)
    middle = (width - LANES) // 2 // LANES
    return call(
        body, 1,
        [(own, own.shape, whole), (picks, picks.shape, at(0, 0, 0))]
        + [(w_heads, (1, depth, LANES), at(g, 0, middle)) for g in (1, 2)]
        + [(hidden_weights, (depth, cut), whole)],
        [((rows + half_border, cut), BF16, (rows + half_border, cut), whole)],
        after=after, vmem=VMEM,
    )[0]


def rest_of_first(place, own, other, picks, w_heads, hidden_weights, begin, cut, after=()):
    rows, depth = other.shape
    width, hidden = w_heads.shape[2], hidden_weights.shape[1]
    edge = (width - LANES) // 2
    border = picks.shape[1]
    block = width_of(begin, 512)
    parts = begin // block

    def body(
        place_ref, own_ref, other_ref, picks_ref, w_heads_ref, w_ref,
        qkv_ref, mine_ref, border_ref, rest_ref, a_ref, b_ref,
    ):
        side = place_ref[0]

        @pl.when(pl.program_id(0) == 0)
        def _():
            both = pl.ds(pl.multiple_of(side * edge, LANES), edge + LANES)
            mine = pl.ds(pl.multiple_of(side * (width - edge), LANES), edge)
            for g in range(3):
                qkv_ref[:, g * (edge + LANES) : (g + 1) * (edge + LANES)] = dot(own_ref[...], w_heads_ref[g, :, both])
                mine_ref[:, g * edge : (g + 1) * edge] = dot(other_ref[...], w_heads_ref[g, :, mine])
            taken = dot(picks_ref[1 - side], other_ref[...]).astype(BF16)
            for g in range(2):
                border_ref[:, g * LANES : (g + 1) * LANES] = dot(taken, w_heads_ref[1 + g, :, edge : edge + LANES])

        sums = dot(other_ref[...], w_ref[...])
        a_ref[...] = sums[:cut].astype(BF16)
        b_ref[...] = sums[cut:].astype(BF16)

        @pl.when(pl.program_id(0) >= parts)
        def _():
            rest_ref[...] = dot(own_ref[...], w_ref[...]).astype(BF16)

    whole = at(0, 0)
    column = lambda j: (0, j)
    out = lambda count, wide: ((count, wide), F32, (count, wide), whole)
    return call(
        body, hidden // block,
        [(place, None, pltpu.SMEM), (own, own.shape, whole), (other, other.shape, whole)]
        + [(a, a.shape, at(0, 0, 0)) for a in (picks, w_heads)]
        + [(hidden_weights, (depth, block), column)],
        [
            out(rows, 3 * (edge + LANES)),
            out(rows, 3 * edge),
            out(border, 2 * LANES),
            ((rows, hidden - begin), BF16, (rows, block), lambda j: (0, jnp.maximum(j - parts, 0))),
            ((cut, hidden), BF16, (cut, block), column),
            ((rows - cut, hidden), BF16, (rows - cut, block), column),
        ],
        after=after, vmem=REST_VMEM,
        cost=(
            2 * depth * (rows * 4 * width + border * 2 * LANES + rows * hidden),
            2 * depth * (2 * rows + 3 * width + hidden) + 12 * rows * width + 2 * rows * hidden,
        ),
    )


def norm_units(place, own, other, border, q_gain, k_gain, after=()):
    rows, heads, head_dim = own[0].shape[0], q_gain.shape[0], q_gain.shape[2]
    pair = heads // 2
    units = 2 * pair + 1
    half_border = border[0].shape[0] // 2
    sent_rows = (rows // 2 + 15) // 16 * 16
    sent = units * sent_rows + half_border

    def body(place_ref, *refs):
        own_refs, other_refs, border_refs = refs[:2], refs[2:4], refs[4:6]
        q_gain_ref, k_gain_ref, queries_ref, kv_ref, lower_ref, upper_ref = refs[6:]
        side = place_ref[0]
        first = side * (heads - pair)

        def head(two, index):
            some = pl.ds(pl.multiple_of(index * head_dim, LANES), head_dim)
            return sum(ref[:, some].astype(F32) for ref in two)

        def put(unit, two, p, count, index):
            q, k, v = (head(two, g * count + p) for g in range(3))
            kv = jnp.concatenate([rms_gain(k, k_gain_ref[index]), v], axis=1).astype(BF16)
            queries_ref[unit * rows : (unit + 1) * rows] = rms_gain(q, q_gain_ref[index]).astype(BF16)
            kv_ref[unit * rows : (unit + 1) * rows] = kv
            lower_ref[unit * sent_rows : (unit + 1) * sent_rows] = kv[rows - sent_rows :]
            upper_ref[unit * sent_rows : (unit + 1) * sent_rows] = kv[:sent_rows]

        for p in range(pair):
            put(2 * p, own_refs, side + p, pair + 1, first + p)
            put(2 * p + 1, other_refs, p, pair, first + p)
        put(2 * pair, own_refs, (1 - side) * pair, pair + 1, pair)
        got = border_refs[1][rows:].astype(F32)
        got = jnp.concatenate([got[:, : 2 * head_dim], got[:, 2 * head_dim : 4 * head_dim]], axis=0)
        both = border_refs[0][...] + got
        kv = [rms_gain(both[:, :head_dim], k_gain_ref[pair]), both[:, head_dim:]]
        kv = jnp.concatenate(kv, axis=1).astype(BF16)
        kv_ref[units * rows :] = kv
        upper_ref[units * sent_rows :] = kv[:half_border]
        lower_ref[units * sent_rows :] = kv[half_border:]

    whole = at(0, 0)
    out = lambda count, width: ((count, width), BF16, (count, width), whole)
    ins = [*own, *other, *border]
    return call(
        body, 1,
        [(place, None, pltpu.SMEM)]
        + [(a, a.shape, whole) for a in ins]
        + [(g, g.shape, at(0, 0, 0)) for g in (q_gain, k_gain)],
        [
            out(units * rows, head_dim),
            out(units * rows + 2 * half_border, 2 * head_dim),
            out(sent, 2 * head_dim),
            out(sent, 2 * head_dim),
        ],
        after=after, vmem=POST_VMEM,
    )


def window_codes(tile_side):
    rows, half = tile_side * tile_side, tile_side // 2
    sent_rows = (rows // 2 + 15) // 16 * 16
    extra = sent_rows - rows // 2
    column = np.arange(rows) % tile_side

    def lines(first, second):
        above = lambda on: np.concatenate([np.zeros(extra, np.int32), 2 * on[rows - rows // 2 :]])
        below = lambda on: np.concatenate([3 * on[: rows // 2], np.zeros(extra, np.int32)])
        return np.concatenate([first, second, above(first), above(second), below(first), below(second)])

    def padded(line):
        return np.pad(line, (0, -len(line) % LANES)).astype(np.float32)

    every = np.ones(rows, np.int32)
    right, left = (column >= half).astype(np.int32), (column < half).astype(np.int32)
    by_side = np.stack([
        np.stack([padded(lines(every, left)), padded(lines(right, every))]),
        np.stack([padded(lines(every, right)), padded(lines(left, every))]),
    ])
    pad = border_rows(tile_side)
    part = np.pad(np.ones(half * half, np.int32), (0, pad - half * half))
    above = np.concatenate([np.zeros(extra, np.int32), 2 * np.ones(rows // 2, np.int32), 2 * part])
    below = np.concatenate([3 * np.ones(rows // 2, np.int32), np.zeros(extra, np.int32), 3 * part])
    middle = padded(np.concatenate([every, part, part, above, below]))[None]
    return jnp.asarray(by_side), jnp.asarray(middle)


def attend(place, queries, keys_values, above, below, codes, middle_codes, heads, after=()):
    pair = heads // 2
    units = 2 * pair + 1
    head_dim = queries.shape[1]
    rows = queries.shape[0] // units
    border = keys_values.shape[0] - units * rows
    sent_rows = (above.shape[0] - border // 2) // units

    def body(place_ref, queries_ref, kv_ref, above_ref, below_ref, codes_ref, middle_ref, out_ref):
        side = place_ref[0]

        def unit_rows(ref, unit, count, size):
            return ref[unit * size : (unit + count) * size]

        def rest_rows(ref, size):
            return ref[units * size :]

        def one(unit, blocks, line, column):
            there = (line == 1) | ((line == 2) & (place_ref[2] == 1)) | ((line == 3) & (place_ref[3] == 1))
            line = jnp.where(there, 0.0, -jnp.inf)
            spare = line.shape[1] - sum(b.shape[0] for b in blocks)
            if spare:
                blocks = blocks + [jnp.zeros((spare, 2 * head_dim), BF16)]
            both = jnp.concatenate(blocks, axis=0)
            keys, values = both[:, :head_dim], both[:, head_dim:]
            mine = unit_rows(queries_ref, unit, 1, rows)
            scores = lax.dot_general(mine, keys, (((1,), (1,)), ((), ())), preferred_element_type=F32)
            scores = scores * head_dim ** (-0.5) + line
            numerators = jnp.exp(scores - jnp.max(scores, axis=-1, keepdims=True))
            total = jnp.sum(numerators, axis=-1, keepdims=True)
            got = (dot(numerators.astype(BF16), values) / total).astype(BF16)
            out_ref[:, column * head_dim : (column + 1) * head_dim] = got

        for p in range(pair):
            blocks = [
                unit_rows(kv_ref, 2 * p, 2, rows),
                unit_rows(above_ref, 2 * p, 2, sent_rows),
                unit_rows(below_ref, 2 * p, 2, sent_rows),
            ]
            one(2 * p, blocks, codes_ref[side][0:1], p)
            one(2 * p + 1, blocks, codes_ref[side][1:2], pair + 1 + p)
        blocks = [
            kv_ref[2 * pair * rows :],
            above_ref[2 * pair * sent_rows :],
            below_ref[2 * pair * sent_rows :],
        ]
        one(2 * pair, blocks, middle_ref[...], pair)

    ins = [queries, keys_values, above, below, middle_codes]
    whole = [(a, a.shape, at(0, 0)) for a in ins]
    return call(
        body, 1,
        [(place, None, pltpu.SMEM)] + whole[:4] + [(codes, codes.shape, at(0, 0, 0))] + whole[4:],
        [((rows, units * head_dim), BF16, (rows, units * head_dim), at(0, 0))],
        after=after, vmem=POST_VMEM,
    )[0]


def paired_plan(
    tokens, mod_shift, mod_scale, mod_gate, w_qkv, w_mlp_in, q_gain, k_gain, w_attn_out, w_mlp_out
):
    tok_rows, model_width = tokens.shape
    half_width, hidden = w_mlp_in.shape
    heads, head_dim = q_gain.shape
    width = heads * head_dim
    side = lax.axis_index("sx")
    part = lax.axis_index("tp")
    core, far = part % 2, part // 2
    mid = hidden // 2
    block = half_width // 2
    row = lax.axis_index("sy")
    place = jnp.stack([side, core, row > 0, row < lax.axis_size("sy") - 1]).astype(jnp.int32)
    picks = border_picks(TILE)
    q_gain, k_gain = q_gain[:, None, :], k_gain[:, None, :]

    quarter = half_width // 4
    other_first = (1 - side) * half_width + part * quarter
    sent = lax.dynamic_slice_in_dim(lax.optimization_barrier(tokens), other_first, quarter, 1)
    piece = swap(sent, "sx", 1)
    first = side * half_width
    gain_part = 1.0 + lax.dynamic_slice_in_dim(mod_scale, first, half_width, 0)
    shift_part = lax.dynamic_slice_in_dim(mod_shift, first, half_width, 0)

    def modulate(cells, pair):
        cells = (cells.astype(F32) - pair[0]) * pair[1]
        return (cells * gain_part + shift_part).astype(BF16)

    pair = heads // 2
    edge = pair * head_dim
    w_heads = jnp.transpose(w_qkv, (1, 0, 2))

    own, own_early, moments = modulate_and_heads(tokens, mod_scale[None], mod_shift[None], w_heads, [sent])
    got_early, got_moments = swap(own_early, "sx", 1), swap(moments, "sx", 1)
    near = swap(piece, "tp", 1)
    piece_far = hold(swap(piece, "tp", 2), got_early)
    first_part = width_of(hidden // 3, hidden)
    own_first = border_and_hidden(own, picks, w_heads, w_mlp_in, first_part, [moments, piece])
    got_first = swap(own_first, "sx", 1)
    piece_far = hold(piece_far, own_first)
    near_far = swap(piece_far, "tp", 1)
    lower, upper = in_order(far, piece, piece_far), in_order(far, near, near_far)
    quarters = [part for pair_of in zip(lower, upper) for part in in_order(core, *pair_of)]
    other = jnp.concatenate(quarters, axis=1)
    other = modulate(other, [got_moments[:, i, : token_block(tok_rows)].reshape(tok_rows, 1) for i in range(2)])
    late_first = (1 - side) * edge
    other_late = [
        dot(other, lax.dynamic_slice(w_heads, (g, 0, late_first), (1, half_width, edge + head_dim))[0]).astype(BF16)
        for g in range(3)
    ]
    other_late = jnp.concatenate(other_late, axis=1)
    got_late = swap(other_late, "sx", 1)
    cut = tok_rows // 2
    own_heads, other_heads, other_border, own_rest, other_a, other_b = rest_of_first(
        place, own, other, picks, w_heads, w_mlp_in, first_part, cut, [other_late, got_first]
    )
    got_rest = swap(own_rest, "sx", 1)
    queries, keys_values, lower, upper = norm_units(
        place, (own_heads, got_late), (other_heads, got_early), (other_border, got_first), q_gain, k_gain, [other_a]
    )
    above = shift(lower, "sy", 1)
    below = shift(upper, "sy", -1)

    sent_mlp, kept_mlp, sent_attn, kept_attn = (
        lax.dynamic_slice_in_dim(w, start * block, block, 1)
        for w in (w_mlp_out, w_attn_out)
        for start in (1 - core, core)
    )

    def activate(mine, got, *earlier):
        got = hold(got, *earlier) if earlier else got
        return hold(jax.nn.gelu(mine.astype(F32) + got.astype(F32), approximate=True).astype(BF16))

    attended = attend(place, queries, keys_values, above, below, *window_codes(TILE), heads)
    got_attended = swap(attended, "sx", 1)
    got_other_a = swap(other_a, "sx", 1)
    got_own = jnp.concatenate([got_first[:tok_rows], hold(got_rest, attended)], axis=1)
    own_hidden = jnp.concatenate([own_first[:tok_rows], own_rest], axis=1)
    other_active = activate(jnp.concatenate([other_a, other_b], axis=0), got_own)
    other_sent, other_kept = dot(other_active, sent_mlp), dot(other_active, kept_mlp)
    got_other_b = swap(hold(other_b, other_sent), "sx", 1)

    def own_part(begin, end, got, *earlier):
        active, heads_part = activate(own_hidden[begin:end], got, *earlier), own_attended[begin:end]
        return (
            (dot(active, sent_mlp) + dot(heads_part, sent_attn)).astype(BF16),
            dot(active, kept_mlp) + dot(heads_part, kept_attn),
        )

    got_attended = hold(got_attended, other_sent, other_kept, got_other_a)
    here = edge + head_dim

    def natural(mine, middle, theirs):
        return jnp.concatenate(
            [jnp.where(side == 0, mine, theirs), middle, jnp.where(side == 0, theirs, mine)], axis=1
        )

    own_attended = natural(attended[:, :edge], attended[:, edge:here], got_attended[:, here:])
    other_attended = natural(attended[:, here:], got_attended[:, edge:here], got_attended[:, :edge])
    other_sent = (other_sent + dot(other_attended, sent_attn)).astype(BF16)
    other_kept = other_kept + dot(hold(other_attended, other_sent), kept_attn)
    other_come = swap(other_sent, "tp", 1)
    own_sent_a, own_kept_a = own_part(0, cut, got_other_a, other_sent)

    def rows_of(half):
        kept = jnp.where(half == 0, other_kept[:cut], other_kept[cut:])
        return kept + jnp.where(half == 0, other_come[:cut], other_come[cut:]).astype(F32)

    passed = rows_of(1 - far).astype(BF16)
    passed = hold(swap(passed, "tp", 2), own_sent_a, own_kept_a)
    crossing = (rows_of(far) + passed.astype(F32)).astype(BF16)
    got = swap(crossing, "sx", 1)
    own_sum_a = own_kept_a + swap(own_sent_a, "tp", 1).astype(F32)
    come_a = swap(own_sum_a.astype(BF16), "tp", 2)
    own_sent_b, own_kept_b = own_part(cut, tok_rows, got_other_b, crossing)
    own_sum_b = hold(own_kept_b, got, come_a, cost=EARLY) + swap(own_sent_b, "tp", 1).astype(F32)

    home = far == side
    come_b = swap(jnp.where(home, got, own_sum_b.astype(BF16)), "tp", 2)
    wide = got.astype(F32)
    known = jnp.concatenate(
        [
            jnp.where(home, own_sum_a + come_a.astype(F32), jnp.where(far == 0, wide, 0.0)),
            jnp.where(home, own_sum_b, jnp.where(far == 0, 0.0, wide)),
        ],
        axis=0,
    )
    first_col = part * block
    gate_part = lax.dynamic_slice_in_dim(mod_gate, first_col, block, 0)
    residual_part = lax.dynamic_slice_in_dim(tokens, first_col, block, 1).astype(F32)
    known = hold(residual_part + gate_part * known)
    late_first = jnp.where(home, 1, 1 - far) * cut
    token = lax.broadcasted_iota(jnp.int32, (tok_rows, 1), 0)
    late = (token >= late_first) & (token < late_first + cut)
    late_part = jnp.concatenate([come_b, come_b], axis=0).astype(F32)
    return (known + jnp.where(late, gate_part * late_part, 0.0)).astype(BF16)


def shards(*arrays):
    local_heads = arrays[6].shape[0]
    if lax.axis_size("sx") == 2 and lax.axis_size("tp") == 4 and local_heads % 2 and local_heads > 1 and arrays[6].shape[1] == LANES:
        return paired_plan(*arrays)
    return gathered_plan(*arrays)


def solution(mesh):
    placed = (
        P(("sy", "sx"), None),
        P(),
        P(),
        P(),
        P("sx", None, "tp"),
        P("sx", "tp"),
        P("tp", None),
        P("tp", None),
        P("tp", "sx"),
        P("tp", "sx"),
    )
    return jax.shard_map(
        shards, mesh=mesh, in_specs=placed, out_specs=P(("sy", "sx"), "tp"), check_vma=False
    )
```
